32 devices in a mesh: dp: 2 (over core), expert: 16 (over z, y, x).
Axes of the slice: x: 2, y: 2, z: 4, core: 2. Of those that a mesh axis runs over, the one named last changes fastest.
Arguments:
- tokens: bfloat16 [16384, 768], P(('dp', 'expert')), may hold values from -6 to 6
- cotangent: bfloat16 [16384, 768], P(('dp', 'expert')), may hold values from -6 to 6
- routes: int32 [16384, 1], P(('dp', 'expert')), may hold values from 0 to 15; in each aligned block of 512 rows (0 to 511, 512 to 1023, ...) at most 64 rows name the same one
- buckets: int32 [512, 512], replicated, may hold values from 0 to 31, as said below
- gain_attn: bfloat16 [768], P(('dp', 'expert')), may hold values from 0.099609375 to 1.8984375
- w_qkv: bfloat16 [768, 2304], P(('dp', 'expert')), may hold values from -0.21875 to 0.21875
- w_att: bfloat16 [768, 768], P(('dp', 'expert')), may hold values from -1.25 to 1.25
- rel_bias: float32 [32, 12], replicated, may hold values from -4 to 4
- gain_moe: bfloat16 [768], P(('dp', 'expert')), may hold values from 0.099609375 to 1.8984375
- w_router: bfloat16 [768, 16], P(('dp', 'expert')), may hold values from -0.15625 to 0.15625
- w_in: bfloat16 [16, 768, 3072], P('expert'), may hold values from -0.21875 to 0.21875
- w_out: bfloat16 [16, 768, 3072], P('expert'), may hold values from -1.75 to 1.75
Outputs:
- mixed: bfloat16 [16384, 768], P(('dp', 'expert'))
- grad_tokens: float32 [16384, 768], P(('dp', 'expert'))
- grad_gain_attn: float32 [768], P(('dp', 'expert'))
- grad_qkv: float32 [768, 2304], P(('dp', 'expert'))
- grad_att: float32 [768, 768], P(('dp', 'expert'))
- grad_bias: float32 [32, 12], replicated
- grad_gain_moe: float32 [768], P(('dp', 'expert'))
- grad_router: float32 [768, 16], P(('dp', 'expert'))
- grad_in: float32 [16, 768, 3072], P('expert', None, 'dp')
- grad_out: float32 [16, 768, 3072], P('expert', None, 'dp')
The draws below stay inside these ranges and needn't reach their ends.
Inputs may be any that keep to these rules, and one draw needn't show every extreme that they name: `routes`: among the tokens of one device no expert is named more than 64 times; some experts are named far more often than the mean. buckets[i, j] depends only on j - i, never falls as |j - i| grows on either side, is below 16 for j <= i and 16 or more for j > i, and is 0 for j = i.
All inputs are finite; a program needn't handle non-finite values.
Results may differ from the reference program's by a relative error of at most 0.019.
Values may be sent and summed in bfloat16 or wider, within the bound.
A program may use at most 256 MiB of HBM per device.

```python
import math
import jax
import jax.numpy as jnp
import numpy as np
from jax import lax

D = 768
H = 12
DH = 64
FF = 3072
NB = 32
SEQ = 512
EXPERTS = 16
TOK_DEV = 512
TOKENS = 16384
MOST = 64


def draw_buckets(key, part):
    key = jax.random.fold_in(key, 11)
    side_count = NB // 2
    bounds = jax.random.randint(key, (2, side_count - 1), 1, SEQ)
    places = jnp.arange(SEQ, dtype=jnp.int32)
    offsets = places[None, :] - places[:, None]
    later = (offsets > 0).astype(jnp.int32)
    reach = jnp.abs(offsets)
    chosen = jnp.where(later[:, :, None] > 0, bounds[1][None, None, :], bounds[0][None, None, :])
    passed = jnp.sum((reach[:, :, None] >= chosen).astype(jnp.int32), axis=2, dtype=jnp.int32)
    return (later * side_count + passed).astype(jnp.int32)


def steps_of(own_key, extent, split, smallest, top_value):
    factor_of = 1.0
    for position, blocks in split:
        heights = jax.random.uniform(jax.random.fold_in(jax.random.fold_in(own_key, 6), position), (blocks,), jnp.float32, smallest / len(split), top_value / len(split))
        factor_of = factor_of * jnp.repeat(jnp.exp(heights), extent[position] // blocks).reshape((-1,) + (1,) * (len(extent) - 1 - position))
    return factor_of


def assign_block(key, own, number, rows, number_of, top, bound, skew):
    sequence = jax.random.permutation(key, number_of)
    crowded, ordinary = portions_of(number_of, rows * top, bound, skew, True), portions_of(number_of, rows * top, bound, skew, False)
    places = jnp.arange(number_of)

    def named(tallies, rotation):
        used = int((tallies > 0).sum())
        fixed = max(1, used // 4)
        moved = fixed + (places - fixed + rotation * (used - fixed)) % max(1, number_of - fixed)
        return jnp.zeros((number_of,), jnp.int32).at[sequence[jnp.where(places < fixed, places, moved)]].set(jnp.asarray(tallies, jnp.int32))

    tallies = jnp.where(number % 4 == 0, named(crowded, number // 4), named(ordinary, number - number // 4 - 1))
    mixed = jax.random.permutation(jax.random.fold_in(own, 3), number_of)
    giver, sink = mixed[0:number_of // 2 * 2:2], mixed[1:number_of // 2 * 2:2]
    room = jnp.minimum(tallies[giver] - 1, bound - tallies[sink]) // 2
    room = jnp.where((giver == sequence[0]) | (sink == sequence[0]) | (tallies[sink] == 0), 0, jnp.maximum(room, 0))
    moved = jax.random.randint(jax.random.fold_in(own, 4), (number_of // 2,), 0, 1 << 20) % (room + 1)
    tallies = tallies.at[giver].add(-moved).at[sink].add(moved)
    members = jnp.searchsorted(jnp.cumsum(tallies), jnp.arange(rows * top), side="right").astype(jnp.int32)
    listing = members.reshape(top, rows).T
    listing = listing[jax.random.permutation(jax.random.fold_in(own, 1), rows)]
    rotation = jax.random.randint(jax.random.fold_in(own, 2), (rows, 1), 0, top)
    return jnp.take_along_axis(listing, (jnp.arange(top)[None, :] + rotation) % top, axis=1)


def portions_of(number_of, total, most, skew, full):
    weights = [(1 << 20) // math.isqrt(rank ** skew) + 1 for rank in range(1, number_of + 1)]
    largest = most if full else min(most, max(-(-total // number_of), total * weights[0] // sum(weights)))
    least = 1 if total - largest >= number_of - 1 else 0
    counts, spare = [largest] + [least] * (number_of - 1), total - largest - least * (number_of - 1)
    while spare > 0:
        movable = [i for i in range(1, number_of) if counts[i] < largest] or [i for i in range(1, number_of) if counts[i] < most]
        pool, budget = sum([weights[i] for i in movable]), spare
        for i in movable:
            addition = min(most - counts[i], max(1, budget * weights[i] // pool), spare)
            counts[i] = counts[i] + addition
            spare = spare - addition
    return np.array(counts)


def gaussian(own_key, shape, spread, most, shards=(), kind=jnp.bfloat16):
    array = spread * jax.random.normal(own_key, shape, jnp.float32)
    if shards:
        array = array * steps_of(own_key, shape, shards, -0.22, 0.18)
    return jnp.clip(array, -most, most).astype(kind)


def setup_inputs(seed: int = 0) -> dict:
    seeds = jax.random.split(jax.random.key(seed), 13)
    tokens = gaussian(seeds[0], (TOKENS, D), 1.0, 6.0, ((0, 32),))
    cotangent = gaussian(seeds[1], (TOKENS, D), 1.0, 6.0, ((0, 32),))
    routes_keys = jax.random.split(jax.random.fold_in(seeds[2], 1), TOKENS // TOK_DEV)
    routes_turns = jax.random.permutation(jax.random.fold_in(seeds[2], 3), TOKENS // TOK_DEV)
    routes = jax.vmap(lambda own, number: assign_block(jax.random.fold_in(seeds[2], 2), own, number, TOK_DEV, EXPERTS, 1, MOST, 2))(routes_keys, routes_turns).reshape((TOKENS, 1))
    buckets = draw_buckets(jax.random.fold_in(seeds[12], 71), 0)
    gain_attn = jnp.clip(1.0 + 0.18 * jax.random.normal(seeds[4], (D,), jnp.float32), 0.099609375, 1.8984375).astype(jnp.bfloat16)
    w_qkv = gaussian(seeds[5], (D, 3 * D), D ** -0.5, 0.21875, ((0, 32),))
    w_att = gaussian(seeds[6], (D, D), (D // 32) ** -0.5, 1.25, ((0, 32),))
    rel_bias = gaussian(seeds[7], (NB, H), 1.0, 4.0, (), jnp.float32)
    gain_moe = jnp.clip(1.0 + 0.18 * jax.random.normal(seeds[8], (D,), jnp.float32), 0.099609375, 1.8984375).astype(jnp.bfloat16)
    w_router = gaussian(seeds[9], (D, EXPERTS), (2 * D) ** -0.5, 0.15625, ((0, 32),))
    w_in = gaussian(seeds[10], (EXPERTS, D, FF), D ** -0.5, 0.21875, ((0, 16),))
    w_out = gaussian(seeds[11], (EXPERTS, D, FF), (EXPERTS / FF ** 0.5), 1.75, ((0, 16),))
    return {"tokens": tokens, "cotangent": cotangent, "routes": routes, "buckets": buckets, "gain_attn": gain_attn, "w_qkv": w_qkv, "w_att": w_att, "rel_bias": rel_bias, "gain_moe": gain_moe, "w_router": w_router, "w_in": w_in, "w_out": w_out}


@jax.custom_vjp
def low(v):
    return lax.optimization_barrier(v.astype(jnp.bfloat16)).astype(jnp.float32)

@jax.custom_vjp
def low_back(v):
    return v

def low_keep(v):
    return (low(v), None)

def low_pass(kept, grad):
    return (grad,)

def back_keep(v):
    return (v, None)

def back_low(kept, grad):
    return (low(grad),)
low.defvjp(low_keep, low_pass)
low_back.defvjp(back_keep, back_low)
EPSILON = 1e-06
PRECISE = lax.Precision.HIGHEST

def round_both(values):
    return low(low_back(values))

def rms_scale(values, gains):
    return values * lax.rsqrt(lax.optimization_barrier(jnp.mean(values * values, axis=-1, keepdims=True)) + EPSILON) * gains

def attend(normed_seq, qkv_weight, att_weight, bias_table):
    packed = round_both(jnp.dot(normed_seq, qkv_weight, precision=PRECISE))
    query_rows = packed[:, :D].reshape(SEQ, H, DH)
    key_rows = packed[:, D:2 * D].reshape(SEQ, H, DH)
    value_rows = packed[:, 2 * D:].reshape(SEQ, H, DH)
    scores = low_back(jnp.einsum('qhd,khd->hqk', query_rows, key_rows, precision=PRECISE) * DH ** (-0.5) + bias_table)
    log_total = jax.nn.logsumexp(scores, axis=-1, keepdims=True)
    weights = low(jnp.exp(scores - log_total))
    attended = round_both(jnp.einsum('hqk,khd->qhd', weights, value_rows, precision=PRECISE).reshape(SEQ, D))
    return low_back(jnp.dot(attended, att_weight, precision=PRECISE))

def slot_tables(routes):
    expert_of = routes[:, 0].astype(jnp.int32)
    blocks = TOKENS // TOK_DEV
    hits = (expert_of[:, None] == jnp.arange(EXPERTS, dtype=jnp.int32)[None, :]).astype(jnp.int32)
    hits = hits.reshape(blocks, TOK_DEV, EXPERTS)
    ranks = lax.optimization_barrier(jnp.sum((jnp.cumsum(hits, axis=1, dtype=jnp.int32) - 1) * hits, axis=2, dtype=jnp.int32)).reshape(TOKENS)
    block_of = jnp.arange(TOKENS, dtype=jnp.int32) // TOK_DEV
    slot_of = ((expert_of * blocks + block_of) * MOST + ranks).astype(jnp.int32)
    total_slots = EXPERTS * blocks * MOST
    slot_token = jnp.zeros((total_slots,), jnp.int32).at[slot_of].set(jnp.arange(TOKENS, dtype=jnp.int32))
    slot_live = jnp.zeros((total_slots,), jnp.float32).at[slot_of].set(1.0)
    return (expert_of, slot_of, slot_token.reshape(EXPERTS, blocks * MOST), slot_live.reshape(EXPERTS, blocks * MOST))

def reference(tokens, cotangent, routes, buckets, gain_attn, w_qkv, w_att, rel_bias, gain_moe, w_router, w_in, w_out):
    expert_of, slot_of, slot_token, slot_live = slot_tables(routes)

    def forward(inputs, gain_one, qkv_weight, att_weight, bias_weight, gain_two, router_weight, in_weight, out_weight):
        bias_table = jnp.transpose(jnp.take(bias_weight, buckets, axis=0), (2, 0, 1))
        normed = low(rms_scale(inputs, gain_one))
        per_seq = normed.reshape(TOKENS // SEQ, SEQ, D)
        attn_part = lax.map(jax.checkpoint(lambda one_seq: attend(one_seq, qkv_weight, att_weight, bias_table)), per_seq)
        middle = inputs + attn_part.reshape(TOKENS, D)
        moe_in = low(rms_scale(middle, gain_two))
        logits = low_back(jnp.dot(moe_in, router_weight, precision=PRECISE))
        router_prob = jax.nn.softmax(logits, axis=-1)
        gate_value = jnp.take_along_axis(router_prob, expert_of[:, None], axis=1)[:, 0]
        sent_rows = low_back(moe_in)

        def expert_apply(pieces):
            weight_one, weight_two, token_ids, live_rows = pieces
            rows_here = jnp.take(sent_rows, token_ids, axis=0) * live_rows[:, None]
            hidden = low_back(jnp.dot(rows_here, weight_one, precision=PRECISE))
            active = low(jax.nn.gelu(hidden))
            return round_both(jnp.dot(active, weight_two.T, precision=PRECISE))
        produced = lax.map(jax.checkpoint(expert_apply), (in_weight, out_weight, slot_token, slot_live))
        expert_back = jnp.take(produced.reshape(-1, D), slot_of, axis=0)
        return middle + gate_value[:, None] * expert_back
    float_args = tuple((value.astype(jnp.float32) for value in (tokens, gain_attn, w_qkv, w_att, rel_bias, gain_moe, w_router, w_in, w_out)))
    result, pullback = jax.vjp(forward, *float_args)
    grads = pullback(cotangent.astype(jnp.float32))
    return (result.astype(jnp.bfloat16), grads[0], grads[1], grads[2], grads[3], grads[4], grads[5], grads[6], grads[7], grads[8])
```

```python
import functools
import jax
import jax.numpy as jnp
from jax import lax
from jax.experimental import pallas as pl
from jax.experimental.pallas import tpu as pltpu
from jax.sharding import PartitionSpec as P

MESH = pl.DeviceIdType.MESH
F32, BF16 = jnp.float32, jnp.bfloat16
NT = (((1,), (1,)), ((), ()))


def dot(a, b, dims=(((1,), (0,)), ((), ()))):
    return lax.dot_general(a, b, dims, preferred_element_type=F32)


def flipped(index, bits, count):
    result, bit = 0, 1
    while bit < count:
        result = result + bit * (((index // bit) % 2 + (bits // bit) % 2) % 2)
        bit *= 2
    return result


def gelu_parts(hidden):
    c0, c1 = 0.7978845608028654, 0.044715
    square = hidden * hidden
    bend = jnp.tanh(hidden * (c0 + (c0 * c1) * square))
    half = 0.5 + 0.5 * bend
    slope = half + (0.5 * hidden) * (1.0 - bend * bend) * (c0 + (3.0 * c0 * c1) * square)
    return hidden * half, slope


def moe_kernel(
    n, cap, pad, experts,
    rows_ref, cots_ref, router_ref, win_hbm, wout_hbm,
    back_ret, prod_ret, gin_ref, gout_ref,
    win, wout, xin, cin, xt, rt, act, hgr, backs, prods, acc1, acc2,
    sib_send, sib_recv, stage,
    wsem, send_sem, recv_sem, ret_send, ret_recv, own_sem, sib_ss, sib_rs, out_sem,
):
    dp, me = lax.axis_index("dp"), lax.axis_index("expert")
    width, ff = win.shape
    per = 256 // cap
    groups = n // per
    rows = per * cap
    chunk = 512
    load_in = pltpu.make_async_copy(win_hbm, win, wsem.at[0])
    load_out = pltpu.make_async_copy(wout_hbm, wout, wsem.at[1])
    load_in.start()
    load_out.start()
    barrier = pltpu.get_barrier_semaphore()

    def greet(p, _):
        pl.semaphore_signal(barrier, inc=1, device_id=(dp, flipped(me, p, n)), device_id_type=MESH)
        return 0

    lax.fori_loop(1, n, greet, 0)
    pl.semaphore_signal(barrier, inc=1, device_id=(1 - dp, me), device_id_type=MESH)
    pl.semaphore_wait(barrier, n)

    def send(kind, p):
        src, dst = ((rows_ref, xin), (cots_ref, cin))[kind]
        return pltpu.make_async_remote_copy(
            src_ref=src.at[p], dst_ref=dst.at[p],
            send_sem=send_sem.at[kind, p], recv_sem=recv_sem.at[kind, p],
            device_id=(dp, flipped(me, p, n)), device_id_type=MESH,
        )

    def give(kind, p):
        src, dst = ((backs, back_ret), (prods, prod_ret))[kind]
        return pltpu.make_async_remote_copy(
            src_ref=src.at[p], dst_ref=dst.at[p],
            send_sem=ret_send.at[kind, p], recv_sem=ret_recv.at[kind, p],
            device_id=(dp, flipped(me, p, n)), device_id_type=MESH,
        )

    for kind in (0, 1):
        def start(i, _):
            send(kind, n - i).start()
            return 0
        lax.fori_loop(1, n, start, 0)
    xin[0] = rows_ref[0]
    cin[0] = cots_ref[0]
    load_in.wait()
    load_out.wait()

    def packed_rows(ref, g):
        block = ref[pl.ds(g * per, per)].reshape(per * pad, width)
        if pad == cap:
            return block
        r = lax.broadcasted_iota(jnp.int32, (rows, per * pad), 0)
        c = lax.broadcasted_iota(jnp.int32, (rows, per * pad), 1)
        return dot(((r // cap) * pad + r % cap == c).astype(BF16), block).astype(BF16)

    def spread_rows(block):
        if pad == cap:
            return block
        r = lax.broadcasted_iota(jnp.int32, (per * pad, rows), 0)
        c = lax.broadcasted_iota(jnp.int32, (per * pad, rows), 1)
        pick = (r // pad == c // cap) & (r % pad == c % cap)
        return dot(pick.astype(BF16), block).astype(BF16)

    def group(g, _):
        for kind in (0, 1):
            def arrive(j, _):
                p = g * per + j
                @pl.when(p != 0)
                def _():
                    send(kind, p).wait_recv()
                return 0
            lax.fori_loop(0, per, arrive, 0)
        here = pl.ds(pl.multiple_of(g * rows, rows), rows)
        x = packed_rows(xin, g)
        logits = dot(x, router_ref[...])
        lane = lax.broadcasted_iota(jnp.int32, logits.shape, 1)
        logits = jnp.where(lane < experts, logits, -1e30)
        chance = jnp.exp(logits - jnp.max(logits, axis=1, keepdims=True))
        gate = jnp.sum(jnp.where(lane == me, chance, 0.0), axis=1, keepdims=True) / jnp.sum(
            chance, axis=1, keepdims=True)
        r = (gate * packed_rows(cin, g).astype(F32)).astype(BF16)
        xt[:, here] = x.T
        rt[:, here] = r.T
        acc1[...] = jnp.zeros_like(acc1)
        acc2[...] = jnp.zeros_like(acc2)

        def hidden_chunk(k, _):
            cols = pl.ds(pl.multiple_of(k * chunk, chunk), chunk)
            hidden = dot(x, win[:, cols])
            value, slope = gelu_parts(hidden)
            value = value.astype(BF16)
            act[here, cols] = value
            hg = (dot(r, wout[:, cols]) * slope).astype(BF16)
            hgr[here, cols] = hg
            acc1[...] += dot(hg, win[:, cols], NT)
            acc2[...] += dot(value, wout[:, cols], NT)
            return 0

        lax.fori_loop(0, ff // chunk, hidden_chunk, 0)
        backs[pl.ds(g * per, per)] = spread_rows(acc1[...].astype(BF16)).reshape(per, pad, width)
        prods[pl.ds(g * per, per)] = spread_rows(acc2[...].astype(BF16)).reshape(per, pad, width)
        for kind in (0, 1):
            def leave(j, _):
                p = g * per + j
                @pl.when(p != 0)
                def _():
                    give(kind, p).start()
                return 0
            lax.fori_loop(0, per, leave, 0)
        return 0

    lax.fori_loop(0, groups, group, 0)
    own_back = pltpu.make_async_copy(backs.at[0], back_ret.at[0], own_sem.at[0])
    own_prod = pltpu.make_async_copy(prods.at[0], prod_ret.at[0], own_sem.at[1])
    own_back.start()
    own_prod.start()

    half = ff // 2
    part = sib_send.shape[3]
    steps = half // part

    def sibling(kind, k):
        return pltpu.make_async_remote_copy(
            src_ref=sib_send.at[kind, k], dst_ref=sib_recv.at[kind, k],
            send_sem=sib_ss.at[kind, k], recv_sem=sib_rs.at[kind, k],
            device_id=(1 - dp, me), device_id_type=MESH,
        )

    def partial(kind, owner, k):
        cols = pl.ds(pl.multiple_of(owner * half + k * part, 128), part)
        return dot(xt[...], hgr[:, cols]) if kind == 0 else dot(rt[...], act[:, cols])

    def theirs(k, _):
        for kind in (0, 1):
            sib_send[kind, k] = partial(kind, 1 - dp, k).astype(BF16)
            sibling(kind, k).start()
        return 0

    lax.fori_loop(0, steps, theirs, 0)

    def out_copy(kind, k):
        cols = pl.ds(pl.multiple_of(k * part, 128), part)
        return pltpu.make_async_copy(
            stage.at[kind, k % 2], (gin_ref, gout_ref)[kind].at[:, cols], out_sem.at[kind, k % 2])

    def ours(k, _):
        for kind in (0, 1):
            value = partial(kind, dp, k)
            sibling(kind, k).wait_recv()
            @pl.when(k >= 2)
            def _():
                out_copy(kind, k - 2).wait()
            stage[kind, k % 2] = value + sib_recv[kind, k].astype(F32)
            out_copy(kind, k).start()
        return 0

    lax.fori_loop(0, steps, ours, 0)
    for kind in (0, 1):
        for k in (steps - 2, steps - 1):
            out_copy(kind, k).wait()

    def settle(p, _):
        for kind in (0, 1):
            give(kind, p).wait_recv()
            send(kind, p).wait_send()
            give(kind, p).wait_send()
        return 0

    lax.fori_loop(1, n, settle, 0)

    def settle_sibling(k, _):
        for kind in (0, 1):
            sibling(kind, k).wait_send()
        return 0

    lax.fori_loop(0, steps, settle_sibling, 0)
    own_back.wait()
    own_prod.wait()


def moe(n, cap, pad, experts, rows, cots, router, win, wout):
    width, ff = win.shape
    total = n * cap
    part = 256
    steps = ff // 2 // part
    any_ = pl.BlockSpec(memory_space=pl.ANY)
    vmem = pl.BlockSpec(memory_space=pltpu.VMEM)
    dma = pltpu.SemaphoreType.DMA
    per = 256 // cap
    return pl.pallas_call(
        functools.partial(moe_kernel, n, cap, pad, experts),
        out_shape=(
            jax.ShapeDtypeStruct((n, pad, width), BF16),
            jax.ShapeDtypeStruct((n, pad, width), BF16),
            jax.ShapeDtypeStruct((width, ff // 2), F32),
            jax.ShapeDtypeStruct((width, ff // 2), F32),
        ),
        in_specs=[vmem, vmem, vmem, any_, any_],
        out_specs=(any_, any_, any_, any_),
        scratch_shapes=[
            pltpu.VMEM((width, ff), BF16),
            pltpu.VMEM((width, ff), BF16),
            pltpu.VMEM((n, pad, width), BF16),
            pltpu.VMEM((n, pad, width), BF16),
            pltpu.VMEM((width, total), BF16),
            pltpu.VMEM((width, total), BF16),
            pltpu.VMEM((total, ff), BF16),
            pltpu.VMEM((total, ff), BF16),
            pltpu.VMEM((n, pad, width), BF16),
            pltpu.VMEM((n, pad, width), BF16),
            pltpu.VMEM((per * cap, width), F32),
            pltpu.VMEM((per * cap, width), F32),
            pltpu.VMEM((2, steps, width, part), BF16),
            pltpu.VMEM((2, steps, width, part), BF16),
            pltpu.VMEM((2, 2, width, part), F32),
            dma((2,)), dma((2, n)), dma((2, n)), dma((2, n)), dma((2, n)), dma((2,)),
            dma((2, steps)), dma((2, steps)), dma((2, 2)),
        ],
        compiler_params=pltpu.CompilerParams(
            collective_id=2, has_side_effects=True, vmem_limit_bytes=60 * 1024 * 1024),
        cost_estimate=pl.CostEstimate(
            flops=12 * total * width * ff, bytes_accessed=8 * width * ff, transcendentals=total * ff),
        name="experts",
    )(rows, cots, router, win, wout)


EPSILON = 1e-06
PRECISE = lax.Precision.HIGHEST


def rms_scale(values, gains):
    return values * lax.rsqrt(jnp.mean(values * values, axis=-1, keepdims=True) + EPSILON) * gains


def split_heads(packed, width, heads):
    rows_here = packed.shape[0]
    head_dim = width // heads
    return (
        packed[:, :width].reshape(rows_here, heads, head_dim),
        packed[:, width : 2 * width].reshape(rows_here, heads, head_dim),
        packed[:, 2 * width :].reshape(rows_here, heads, head_dim),
    )


def shards(
    n, tokens, cotangent, routes, buckets, gain_attn, w_qkv, w_att, rel_bias, gain_moe, w_router, w_in, w_out,
):
    axes = ("dp", "expert")
    tok_count, width = tokens.shape
    experts = w_router.shape[1]
    bundle = jnp.concatenate([w_qkv, w_att, w_router, gain_attn[:, None], gain_moe[:, None]], axis=1)
    bundle = lax.all_gather(bundle, axes, axis=0, tiled=True)
    full_qkv = bundle[:, : 3 * width]
    full_att = bundle[:, 3 * width : 4 * width]
    full_router = bundle[:, 4 * width : 4 * width + experts]
    full_gain_attn = bundle[:, 4 * width + experts]
    full_gain_moe = bundle[:, 4 * width + experts + 1]
    seq_len = buckets.shape[0]
    heads = rel_bias.shape[1]
    score_scale = (width // heads) ** (-0.5)
    cap = max(2, 2 * tok_count // experts)
    pad = max(16, cap)
    kinds = jnp.arange(rel_bias.shape[0], dtype=jnp.int32)
    bucket_hits = (buckets[None, :, :] == kinds[:, None, None]).astype(jnp.bfloat16)
    bias_table = jnp.einsum(
        "bij,bh->hij", (buckets[None, :, :] == kinds[:, None, None]).astype(jnp.float32), rel_bias,
        precision=PRECISE,
    )
    inputs = tokens.astype(jnp.float32)
    normed_f, attn_norm_pull = jax.vjp(rms_scale, inputs, full_gain_attn.astype(jnp.float32))
    normed = normed_f.astype(jnp.bfloat16)
    packed = jnp.dot(normed, full_qkv, preferred_element_type=jnp.float32).astype(jnp.bfloat16)

    query_rows, key_rows, value_rows = split_heads(packed, width, heads)
    scores = jnp.einsum("qhd,khd->hqk", query_rows, key_rows, preferred_element_type=jnp.float32) * score_scale + bias_table
    log_total = jax.nn.logsumexp(scores, axis=-1, keepdims=True)
    weights = jnp.exp(scores - log_total).astype(jnp.bfloat16)
    attended = jnp.einsum("hqk,khd->qhd", weights, value_rows, preferred_element_type=jnp.float32).reshape(seq_len, width).astype(jnp.bfloat16)

    middle = inputs + jnp.dot(attended, full_att, preferred_element_type=jnp.float32)
    moe_f, moe_norm_pull = jax.vjp(rms_scale, middle, full_gain_moe.astype(jnp.float32))
    moe_in = moe_f.astype(jnp.bfloat16)
    logits = jnp.dot(moe_in, full_router, preferred_element_type=jnp.float32)
    router_prob = jax.nn.softmax(logits, axis=-1)
    chosen = routes[:, 0]
    me = lax.axis_index("expert")
    picked = (chosen[:, None] == jnp.arange(experts, dtype=jnp.int32)[None, :]).astype(jnp.int32)
    gate_value = jnp.sum(router_prob * picked, axis=-1)
    ranks = jnp.sum((jnp.cumsum(picked, axis=0, dtype=jnp.int32) - 1) * picked, axis=1, dtype=jnp.int32)
    slot = jnp.bitwise_xor(chosen, me) * pad + ranks
    hits = (slot[None, :] == jnp.arange(n * pad, dtype=jnp.int32)[:, None]).astype(jnp.bfloat16)

    def to_slots(rows):
        return jnp.dot(hits, rows, preferred_element_type=jnp.float32).astype(jnp.bfloat16).reshape(n, pad, width)

    def from_slots(rows):
        return jnp.dot(hits.T, rows.reshape(n * pad, width), preferred_element_type=jnp.float32)

    upstream = cotangent.astype(jnp.float32)
    router_wide = jnp.pad(full_router, ((0, 0), (0, -experts % 128)))
    came_back, returned, grad_in, grad_out = moe(
        n, cap, pad, experts, to_slots(moe_in), to_slots(cotangent), router_wide, w_in[0], w_out[0])
    expert_back = from_slots(returned)
    mixed = (middle + gate_value[:, None] * expert_back).astype(jnp.bfloat16)
    gate_grad = jnp.sum(upstream * expert_back, axis=-1)
    logit_grad = ((gate_value * gate_grad)[:, None] * (picked - router_prob)).astype(jnp.bfloat16)
    router_grad = jnp.einsum("td,te->de", moe_in, logit_grad, preferred_element_type=jnp.float32)
    moe_in_grad = from_slots(came_back)
    moe_in_grad = moe_in_grad + jnp.einsum("te,de->td", logit_grad, full_router, preferred_element_type=jnp.float32)
    middle_norm_grad, gain_moe_grad = moe_norm_pull(moe_in_grad)
    middle_grad = upstream + middle_norm_grad
    attn_grad = middle_grad.astype(jnp.bfloat16)
    att_weight_grad = jnp.einsum("td,te->de", attended, attn_grad, preferred_element_type=jnp.float32)
    attended_grad = jnp.einsum("te,de->td", attn_grad, full_att, preferred_element_type=jnp.float32).astype(jnp.bfloat16)

    grad_heads = attended_grad.reshape(seq_len, heads, width // heads)
    chance = jnp.exp(scores - log_total)
    weight_grad = jnp.einsum("qhd,khd->hqk", grad_heads, value_rows, preferred_element_type=jnp.float32)
    score_grad = (chance * (weight_grad - jnp.sum(chance * weight_grad, axis=-1, keepdims=True))).astype(jnp.bfloat16)
    query_grad = jnp.einsum("hqk,khd->qhd", score_grad, key_rows, preferred_element_type=jnp.float32) * score_scale
    key_grad = jnp.einsum("hqk,qhd->khd", score_grad, query_rows, preferred_element_type=jnp.float32) * score_scale
    value_grad = jnp.einsum("hqk,qhd->khd", weights, grad_heads, preferred_element_type=jnp.float32)
    packed_grad = jnp.concatenate(
        [g.reshape(seq_len, width) for g in (query_grad, key_grad, value_grad)], axis=1).astype(jnp.bfloat16)
    bias_grad = jnp.einsum("hij,bij->bh", score_grad, bucket_hits, preferred_element_type=jnp.float32)
    qkv_weight_grad = jnp.einsum("td,te->de", normed, packed_grad, preferred_element_type=jnp.float32)
    normed_grad = jnp.einsum("te,de->td", packed_grad, full_qkv, preferred_element_type=jnp.float32)
    input_norm_grad, gain_attn_grad = attn_norm_pull(normed_grad)
    grad_tokens = middle_grad + input_norm_grad
    wide = jnp.concatenate(
        [qkv_weight_grad, att_weight_grad, router_grad, gain_attn_grad[:, None], gain_moe_grad[:, None]], axis=1)
    wide = lax.psum_scatter(wide, axes, scatter_dimension=0, tiled=True)
    grad_bias = lax.psum(bias_grad, axes)
    return (
        mixed, grad_tokens, wide[:, 4 * width + experts], wide[:, : 3 * width], wide[:, 3 * width : 4 * width],
        grad_bias, wide[:, 4 * width + experts + 1], wide[:, 4 * width : 4 * width + experts],
        grad_in[None], grad_out[None],
    )


def solution(mesh):
    both = P(("dp", "expert"))
    return jax.shard_map(
        functools.partial(shards, mesh.shape["expert"]),
        mesh=mesh,
        in_specs=(both, both, both, P(), both, both, both, P(), both, both, P("expert"), P("expert")),
        out_specs=(both, both, both, both, both, P(), both, both, P("expert", None, "dp"), P("expert", None, "dp")),
        check_vma=False,
    )
```

```python
import functools
import jax
import jax.numpy as jnp
from jax import lax
from jax.experimental import pallas as pl
from jax.experimental.pallas import tpu as pltpu
from jax.sharding import PartitionSpec as P

MESH = pl.DeviceIdType.MESH
F32, BF16 = jnp.float32, jnp.bfloat16
NT = (((1,), (1,)), ((), ()))
EPSILON = 1e-06


def dot(a, b, dims=(((1,), (0,)), ((), ()))):
    return lax.dot_general(a, b, dims, preferred_element_type=F32)


def flipped(index, bits, count):
    result, bit = 0, 1
    while bit < count:
        result = result + bit * (((index // bit) % 2 + (bits // bit) % 2) % 2)
        bit *= 2
    return result


def gelu_parts(hidden):
    c0, c1 = 0.7978845608028654, 0.044715
    square = hidden * hidden
    bend = jnp.tanh(hidden * (c0 + (c0 * c1) * square))
    half = 0.5 + 0.5 * bend
    slope = half + (0.5 * hidden) * (1.0 - bend * bend) * (c0 + (3.0 * c0 * c1) * square)
    return hidden * half, slope


def slots_by_row(routes, me, pad, experts):
    count = routes.shape[1]
    picked = routes == lax.broadcasted_iota(jnp.int32, (experts, count), 0)
    first = lax.broadcasted_iota(jnp.int32, (count, count), 0)
    second = lax.broadcasted_iota(jnp.int32, (count, count), 1)
    before = dot(picked.astype(BF16), (first < second).astype(BF16))
    rank = jnp.sum(jnp.where(picked, before, 0.0), axis=0, keepdims=True).astype(jnp.int32)
    return jnp.bitwise_xor(routes, me) * pad + rank


def greet_all(dp, me, n):
    barrier = pltpu.get_barrier_semaphore()

    def greet(p, _):
        pl.semaphore_signal(barrier, inc=1, device_id=(dp, flipped(me, p, n)), device_id_type=MESH)
        return 0

    lax.fori_loop(1, n, greet, 0)
    pl.semaphore_signal(barrier, inc=1, device_id=(1 - dp, me), device_id_type=MESH)
    pl.semaphore_wait(barrier, n)


def grow_strip(strip, w8):
    strip[0:8] = w8
    have = 8
    while have < strip.shape[0]:
        strip[have : 2 * have] = pltpu.roll(strip[0:have], have, 1)
        have *= 2


def forward_kernel(
    n, pad, experts, heads, gathers, *refs,
):
    (tokens_ref, cot_ref, weights_ref, routes_ref, bias_ref,
     rows_hbm, cots_hbm, probs_hbm, packed_hbm, normed_hbm, attended_hbm, middle_hbm, moe_hbm, chance_hbm, w_hbm, gains_ref,
     w, packed, normed, attended, middle, moe_in, chance, rows, cots, probs, strip,
     shard, blocks, put_sem, cot_send, cot_recv, tree_send, tree_recv, sib_send, sib_recv, pair_sem) = refs
    dp, me = lax.axis_index("dp"), lax.axis_index("expert")
    count, width = tokens_ref.shape
    total = n * pad
    puts = []

    def put(src, dst):
        copy = pltpu.make_async_copy(src, dst, put_sem.at[len(puts)])
        copy.start()
        puts.append(copy)

    greet_all(dp, me, n)
    if gathers:
        own = weights_ref.shape[0]
        block = 2 * own
        half = weights_ref.shape[1] // 2
        pair = pltpu.make_async_remote_copy(
            src_ref=weights_ref, dst_ref=shard, send_sem=pair_sem.at[0], recv_sem=pair_sem.at[1],
            device_id=(1 - dp, me), device_id_type=MESH)
        pair.start()
    else:
        load = pltpu.make_async_copy(weights_ref, w, pair_sem.at[0])
        load.start()
    hits = (slots_by_row(routes_ref[...], me, pad, experts)
            == lax.broadcasted_iota(jnp.int32, (total, count), 0)).astype(BF16)
    cots[...] = dot(hits, cot_ref[...]).astype(BF16).reshape(n, pad, width)
    cots_own = pltpu.make_async_copy(cots.at[0], cots_hbm.at[0], pair_sem.at[2])
    cots_own.start()
    x = tokens_ref[...].astype(F32)
    unit = x * lax.rsqrt(jnp.mean(x * x, axis=1, keepdims=True) + EPSILON)

    def cot_copy(p):
        return pltpu.make_async_remote_copy(
            src_ref=cots.at[p], dst_ref=cots_hbm.at[p], send_sem=cot_send.at[p], recv_sem=cot_recv.at[p],
            device_id=(dp, flipped(me, p, n)), device_id_type=MESH)

    def start_cots(i, _):
        cot_copy(n - i).start()
        return 0

    if gathers:
        pair.wait()
        mine, other = weights_ref[...], shard[...]
        blocks[pl.ds(pl.multiple_of(me * block, 16), block)] = jnp.concatenate(
            [jnp.where(dp == 0, mine, other), jnp.where(dp == 0, other, mine)], axis=0).astype(BF16)
        cols = pl.ds(pl.multiple_of(dp * half, 128), half)
        second, third = 2 - dp, 1 + dp

        def at(r):
            return blocks.at[pl.ds(pl.multiple_of(flipped(me, r, n) * block, 16), block), cols]

        def hop(r, step):
            return pltpu.make_async_remote_copy(
                src_ref=at(r), dst_ref=at(r), send_sem=tree_send.at[r + step], recv_sem=tree_recv.at[r + step],
                device_id=(dp, flipped(me, step, n)), device_id_type=MESH)

        def direct(r):
            return pltpu.make_async_remote_copy(
                src_ref=at(0), dst_ref=at(0), send_sem=tree_send.at[r], recv_sem=tree_recv.at[r],
                device_id=(dp, flipped(me, r, n)), device_id_type=MESH)

        def arrived(r):
            pltpu.make_async_remote_copy(
                src_ref=at(r), dst_ref=at(r), send_sem=tree_send.at[r], recv_sem=tree_recv.at[r],
                device_id=(dp, me), device_id_type=MESH).wait_recv()

        def to_sibling(r):
            return pltpu.make_async_remote_copy(
                src_ref=at(r), dst_ref=at(r), send_sem=sib_send.at[r], recv_sem=sib_recv.at[r],
                device_id=(1 - dp, me), device_id_type=MESH)

        far = list(range(4, n, 4))
        for r in far:
            direct(r).start()
        hop(0, third).start()
        hop(0, second).start()
        for r in far:
            arrived(r)
            hop(r, second).start()
            hop(r, third).start()
            to_sibling(r).start()
        for r in [0] + far:
            arrived(r + second)
            hop(r + second, third).start()
            to_sibling(r + second).start()
        lax.fori_loop(1, n, start_cots, 0)
        for r in [0] + far:
            arrived(r + third)
            to_sibling(r + third).start()
            arrived(r + 3)
            to_sibling(r + 3).start()

        def settle_sibling(r, _):
            other_cols = pl.ds(pl.multiple_of((1 - dp) * half, 128), half)
            there = blocks.at[pl.ds(pl.multiple_of(flipped(me, r, n) * block, 16), block), other_cols]
            pltpu.make_async_remote_copy(
                src_ref=there, dst_ref=there, send_sem=sib_send.at[r], recv_sem=sib_recv.at[r],
                device_id=(1 - dp, me), device_id_type=MESH).wait_recv()
            return 0

        lax.fori_loop(1, n, settle_sibling, 0)
        for core in (0, 1):
            for q in range(n // 2):
                low = blocks[(2 * q) * block + core * own : (2 * q) * block + core * own + own].astype(F32)
                high = blocks[(2 * q + 1) * block + core * own : (2 * q + 1) * block + core * own + own].astype(F32)
                place = core * own * n + q * block
                w[place : place + block] = jnp.concatenate([low, high], axis=0).astype(BF16)
    else:
        lax.fori_loop(1, n, start_cots, 0)
        load.wait()
    put(w, w_hbm)
    extras = w[:, 4 * width :].astype(F32)
    gains = extras[:, 128:256].T
    gains_ref[...] = gains[0:8]
    normed[...] = (unit * gains[0:1]).astype(BF16)
    put(normed, normed_hbm)
    for c in range(3):
        cols_c = slice(c * width, (c + 1) * width)
        packed[:, cols_c] = dot(normed[...], w[:, cols_c]).astype(BF16)
    put(packed, packed_hbm)
    scale = (width // heads) ** -0.5
    lane = lax.broadcasted_iota(jnp.int32, (count, 128), 1)

    def attend(k, _):
        def part(c):
            return packed[:, pl.ds(pl.multiple_of(c * width + k * 128, 128), 128)]

        queries = (part(0).astype(F32) * scale).astype(BF16)
        keys = part(1)
        values = part(2).astype(F32).T.astype(BF16)
        outs = []
        for h in (0, 1):
            grow_strip(strip, bias_ref[2 * k + h])
            own_keys = jnp.where((lane < 64) == (h == 0), keys, jnp.zeros_like(keys))
            scores = dot(own_keys, queries, NT)
            scores = jnp.concatenate(
                [scores[128 * b : 128 * b + 128] + strip[:, 384 - 128 * b : 896 - 128 * b] for b in range(4)], axis=0)
            powers = jnp.exp(scores - jnp.max(scores, axis=0, keepdims=True))
            weights = (powers * (1.0 / jnp.sum(powers, axis=0, keepdims=True))).astype(BF16)
            probs[2 * k + h] = weights
            outs.append(dot(values[64 * h : 64 * h + 64], weights))
        attended[:, pl.ds(pl.multiple_of(k * 128, 128), 128)] = jnp.concatenate(outs, axis=0).T.astype(BF16)
        return 0

    lax.fori_loop(0, heads // 2, attend, 0)
    put(probs, probs_hbm)
    put(attended, attended_hbm)
    mid = tokens_ref[...].astype(F32) + dot(attended[...], w[:, 3 * width : 4 * width])
    middle[...] = mid
    put(middle, middle_hbm)
    moe = (mid * lax.rsqrt(jnp.mean(mid * mid, axis=1, keepdims=True) + EPSILON) * gains[1:2]).astype(BF16)
    moe_in[...] = moe
    put(moe_in, moe_hbm)
    hits = (slots_by_row(routes_ref[...], me, pad, experts)
            == lax.broadcasted_iota(jnp.int32, (total, count), 0)).astype(BF16)
    rows[...] = dot(hits, moe).astype(BF16).reshape(n, pad, width)
    put(rows, rows_hbm)
    logits = dot(moe, w[:, 4 * width : 4 * width + 128])
    logits = jnp.where(lane < experts, logits, -1e30)
    powers = jnp.exp(logits - jnp.max(logits, axis=1, keepdims=True))
    chance[...] = powers / jnp.sum(powers, axis=1, keepdims=True)
    put(chance, chance_hbm)
    if gathers:
        for r in far:
            direct(r).wait_send()
        for r in [0] + far:
            hop(r, second).wait_send()
            hop(r, third).wait_send()
            hop(r + second, third).wait_send()

        def settle_sends(r, _):
            to_sibling(r).wait_send()
            return 0

        lax.fori_loop(1, n, settle_sends, 0)

    def settle_cots(p, _):
        cot_copy(p).wait_send()
        cot_copy(p).wait_recv()
        return 0

    lax.fori_loop(1, n, settle_cots, 0)
    cots_own.wait()
    for copy in puts:
        copy.wait()


def forward(n, pad, experts, heads, gathers, tokens, cotangent, weights, routes, bias):
    count, width = tokens.shape
    wide = weights.shape[1]
    any_ = pl.BlockSpec(memory_space=pl.ANY)
    vmem = pl.BlockSpec(memory_space=pltpu.VMEM)
    dma = pltpu.SemaphoreType.DMA
    own = weights.shape[0]
    shapes = [
        ((n, pad, width), BF16), ((n, pad, width), BF16), ((heads, count, count), BF16), ((count, 3 * width), BF16),
        ((count, width), BF16), ((count, width), BF16), ((count, width), F32), ((count, width), BF16),
        ((count, 128), F32), ((width, wide), BF16), ((8, width), F32),
    ]
    return pl.pallas_call(
        functools.partial(forward_kernel, n, pad, experts, heads, gathers),
        out_shape=tuple(jax.ShapeDtypeStruct(*s) for s in shapes),
        in_specs=[vmem, vmem, vmem if gathers else any_, vmem, vmem],
        out_specs=tuple([any_] * 10 + [vmem]),
        scratch_shapes=[
            pltpu.VMEM((width, wide), BF16),
            pltpu.VMEM((count, 3 * width), BF16),
            pltpu.VMEM((count, width), BF16),
            pltpu.VMEM((count, width), BF16),
            pltpu.VMEM((count, width), F32),
            pltpu.VMEM((count, width), BF16),
            pltpu.VMEM((count, 128), F32),
            pltpu.VMEM((n, pad, width), BF16),
            pltpu.VMEM((n, pad, width), BF16),
            pltpu.VMEM((heads, count, count), BF16),
            pltpu.VMEM((128, 1024), F32),
            pltpu.VMEM((own, wide) if gathers else (8, 128), F32),
            pltpu.VMEM((width, wide) if gathers else (16, 128), BF16),
            dma((10,)), dma((n,)), dma((n,)), dma((n,)), dma((n,)), dma((n,)), dma((n,)), dma((3,)),
        ],
        compiler_params=pltpu.CompilerParams(
            collective_id=1, has_side_effects=True, vmem_limit_bytes=60 * 1024 * 1024),
        name="forward",
    )(tokens, cotangent, weights, routes, bias)


def moe_kernel(
    n, cap, pad, experts,
    rows_ref, cin, w_hbm, win_hbm, wout_hbm,
    back_ret, tie_ret, prod_out, gin_ref, gout_ref,
    win, wout, router, xin, xt, rt, act, hgr, backs, ties, prods, acc1, acc2,
    sib_send, sib_recv, stage,
    wsem, send_sem, recv_sem, ret_send, ret_recv, own_sem, sib_ss, sib_rs, out_sem,
):
    dp, me = lax.axis_index("dp"), lax.axis_index("expert")
    width, ff = win.shape
    per = 256 // cap
    groups = n // per
    rows = per * cap
    chunk = 512
    load_in = pltpu.make_async_copy(win_hbm, win, wsem.at[0])
    load_out = pltpu.make_async_copy(wout_hbm, wout, wsem.at[1])
    load_router = pltpu.make_async_copy(w_hbm.at[:, pl.ds(4 * width, 128)], router, wsem.at[2])
    load_router.start()
    load_in.start()
    load_out.start()
    greet_all(dp, me, n)

    def send(p):
        return pltpu.make_async_remote_copy(
            src_ref=rows_ref.at[p], dst_ref=xin.at[p], send_sem=send_sem.at[p], recv_sem=recv_sem.at[p],
            device_id=(dp, flipped(me, p, n)), device_id_type=MESH,
        )

    def give(kind, p):
        src, dst = ((backs, back_ret), (ties, tie_ret))[kind]
        return pltpu.make_async_remote_copy(
            src_ref=src.at[p], dst_ref=dst.at[p],
            send_sem=ret_send.at[kind, p], recv_sem=ret_recv.at[kind, p],
            device_id=(dp, flipped(me, p, n)), device_id_type=MESH,
        )

    def start(i, _):
        send(n - i).start()
        return 0

    lax.fori_loop(1, n, start, 0)
    xin[0] = rows_ref[0]
    load_router.wait()
    load_in.wait()
    load_out.wait()

    def packed_rows(ref, g):
        block = ref[pl.ds(g * per, per)].reshape(per * pad, width)
        if pad == cap:
            return block
        r = lax.broadcasted_iota(jnp.int32, (rows, per * pad), 0)
        c = lax.broadcasted_iota(jnp.int32, (rows, per * pad), 1)
        return dot(((r // cap) * pad + r % cap == c).astype(BF16), block).astype(BF16)

    def spread_rows(block):
        if pad == cap:
            return block
        r = lax.broadcasted_iota(jnp.int32, (per * pad, rows), 0)
        c = lax.broadcasted_iota(jnp.int32, (per * pad, rows), 1)
        pick = (r // pad == c // cap) & (r % pad == c % cap)
        return dot(pick.astype(BF16), block).astype(BF16)

    def group(g, _):
        def arrive(j, _):
            p = g * per + j

            @pl.when(p != 0)
            def _():
                send(p).wait_recv()
            return 0

        lax.fori_loop(0, per, arrive, 0)
        here = pl.ds(pl.multiple_of(g * rows, rows), rows)
        x = packed_rows(xin, g)
        logits = dot(x, router[...])
        lane = lax.broadcasted_iota(jnp.int32, logits.shape, 1)
        logits = jnp.where(lane < experts, logits, -1e30)
        chance = jnp.exp(logits - jnp.max(logits, axis=1, keepdims=True))
        gate = jnp.sum(jnp.where(lane == me, chance, 0.0), axis=1, keepdims=True) / jnp.sum(
            chance, axis=1, keepdims=True)
        r = (gate * packed_rows(cin, g).astype(F32)).astype(BF16)
        xt[:, here] = x.T
        rt[:, here] = r.T
        acc1[...] = jnp.zeros_like(acc1)
        acc2[...] = jnp.zeros_like(acc2)

        def hidden_chunk(k, _):
            cols = pl.ds(pl.multiple_of(k * chunk, chunk), chunk)
            hidden = dot(x, win[:, cols])
            value, slope = gelu_parts(hidden)
            value = value.astype(BF16)
            act[here, cols] = value
            hg = (dot(r, wout[:, cols]) * slope).astype(BF16)
            hgr[here, cols] = hg
            acc1[...] += dot(hg, win[:, cols], NT)
            acc2[...] += dot(value, wout[:, cols], NT)
            return 0

        lax.fori_loop(0, ff // chunk, hidden_chunk, 0)
        backs[pl.ds(g * per, per)] = spread_rows(acc1[...].astype(BF16)).reshape(per, pad, width)
        produced = acc2[...].astype(BF16)
        prods[pl.ds(g * per, per)] = spread_rows(produced).reshape(per, pad, width)
        tie = jnp.sum(r.astype(F32) * produced.astype(F32), axis=1, keepdims=True)
        for j in range(per):
            row = jnp.broadcast_to(tie[j * cap : (j + 1) * cap], (cap, 128)).T[0:8]
            ties[g * per + j] = jnp.concatenate([row, jnp.zeros((8, 128 - cap), F32)], axis=1)

        def leave(j, _):
            p = g * per + j

            @pl.when(p != 0)
            def _():
                for kind in (0, 1):
                    give(kind, p).start()
            return 0

        lax.fori_loop(0, per, leave, 0)
        return 0

    lax.fori_loop(0, groups, group, 0)
    own_back = pltpu.make_async_copy(backs.at[0], back_ret.at[0], own_sem.at[0])
    own_tie = pltpu.make_async_copy(ties.at[0], tie_ret.at[0], own_sem.at[1])
    out_prod = pltpu.make_async_copy(prods, prod_out, own_sem.at[2])
    own_back.start()
    own_tie.start()
    out_prod.start()

    half = ff // 2
    part = sib_send.shape[3]
    steps = half // part

    def sibling(kind, k):
        return pltpu.make_async_remote_copy(
            src_ref=sib_send.at[kind, k], dst_ref=sib_recv.at[kind, k],
            send_sem=sib_ss.at[kind, k], recv_sem=sib_rs.at[kind, k],
            device_id=(1 - dp, me), device_id_type=MESH,
        )

    def partial(kind, owner, k):
        cols = pl.ds(pl.multiple_of(owner * half + k * part, 128), part)
        return dot(xt[...], hgr[:, cols]) if kind == 0 else dot(rt[...], act[:, cols])

    def theirs(k, _):
        for kind in (0, 1):
            sib_send[kind, k] = partial(kind, 1 - dp, k).astype(BF16)
            sibling(kind, k).start()
        return 0

    lax.fori_loop(0, steps, theirs, 0)

    def out_copy(kind, k):
        cols = pl.ds(pl.multiple_of(k * part, 128), part)
        return pltpu.make_async_copy(
            stage.at[kind, k % 2], (gin_ref, gout_ref)[kind].at[:, cols], out_sem.at[kind, k % 2])

    def ours(k, _):
        for kind in (0, 1):
            value = partial(kind, dp, k)
            sibling(kind, k).wait_recv()
            @pl.when(k >= 2)
            def _():
                out_copy(kind, k - 2).wait()
            stage[kind, k % 2] = value + sib_recv[kind, k].astype(F32)
            out_copy(kind, k).start()
        return 0

    lax.fori_loop(0, steps, ours, 0)
    for kind in (0, 1):
        for k in (steps - 2, steps - 1):
            out_copy(kind, k).wait()

    def settle(p, _):
        send(p).wait_send()
        for kind in (0, 1):
            give(kind, p).wait_recv()
            give(kind, p).wait_send()
        return 0

    lax.fori_loop(1, n, settle, 0)

    def settle_sibling(k, _):
        for kind in (0, 1):
            sibling(kind, k).wait_send()
        return 0

    lax.fori_loop(0, steps, settle_sibling, 0)
    own_back.wait()
    own_tie.wait()
    out_prod.wait()


def moe(n, cap, pad, experts, rows, cots, w, win, wout):
    width, ff = win.shape
    total = n * cap
    part = 256
    steps = ff // 2 // part
    any_ = pl.BlockSpec(memory_space=pl.ANY)
    vmem = pl.BlockSpec(memory_space=pltpu.VMEM)
    dma = pltpu.SemaphoreType.DMA
    per = 256 // cap
    return pl.pallas_call(
        functools.partial(moe_kernel, n, cap, pad, experts),
        out_shape=(
            jax.ShapeDtypeStruct((n, pad, width), BF16),
            jax.ShapeDtypeStruct((n, 8, 128), F32),
            jax.ShapeDtypeStruct((n, pad, width), BF16),
            jax.ShapeDtypeStruct((width, ff // 2), F32),
            jax.ShapeDtypeStruct((width, ff // 2), F32),
        ),
        in_specs=[vmem, vmem, any_, any_, any_],
        out_specs=(any_, any_, any_, any_, any_),
        scratch_shapes=[
            pltpu.VMEM((width, ff), BF16),
            pltpu.VMEM((width, ff), BF16),
            pltpu.VMEM((width, 128), BF16),
            pltpu.VMEM((n, pad, width), BF16),
            pltpu.VMEM((width, total), BF16),
            pltpu.VMEM((width, total), BF16),
            pltpu.VMEM((total, ff), BF16),
            pltpu.VMEM((total, ff), BF16),
            pltpu.VMEM((n, pad, width), BF16),
            pltpu.VMEM((n, 8, 128), F32),
            pltpu.VMEM((n, pad, width), BF16),
            pltpu.VMEM((per * cap, width), F32),
            pltpu.VMEM((per * cap, width), F32),
            pltpu.VMEM((2, steps, width, part), BF16),
            pltpu.VMEM((2, steps, width, part), BF16),
            pltpu.VMEM((2, 2, width, part), F32),
            dma((3,)), dma((n,)), dma((n,)), dma((2, n)), dma((2, n)), dma((3,)),
            dma((2, steps)), dma((2, steps)), dma((2, 2)),
        ],
        compiler_params=pltpu.CompilerParams(
            collective_id=2, has_side_effects=True, vmem_limit_bytes=60 * 1024 * 1024),
        cost_estimate=pl.CostEstimate(
            flops=12 * total * width * ff, bytes_accessed=8 * width * ff, transcendentals=total * ff),
        name="experts",
    )(rows, cots, w, win, wout)


def backward_kernel(n, pad, experts, heads, scatters, *refs):
    (back_ref, tie_ref, prods_ref, routes_ref, cot_ref, tokens_ref, middle_ref, moe_ref, chance_ref, attended_ref,
     normed_ref, packed_ref, gains_ref, hot_ref, own_ref, gain_ref, probs_hbm, w_hbm,
     *rest) = refs
    (mixed_ref, tokens_grad_ref, qkv_grad_ref, att_grad_ref, extra_grad_ref, gain_grad_ref, bias_grad_ref,
     w, prob, returned, mid_grad, att_cot, packed_grad, normed_t, chunk, strip, bias_rows,
     sib_out, sib_in, mine, out1, in1, keep, out2, in2, out3, in3, in4, bias_out, bias_in,
     load_sem, prob_sem, prod_send, prod_recv, sib_s, sib_r, s1, r1, s2, r2, s3, r3, s4, r4, bias_s, bias_r, own_sem) = rest
    dp, me = lax.axis_index("dp"), lax.axis_index("expert")
    count, width = tokens_ref.shape
    total = n * pad
    part = 3 * 128
    lead = (width + 256 + part - 1) // part
    chunks = lead + heads // 2
    load = pltpu.make_async_copy(w_hbm, w, load_sem.at[0])
    load.start()

    def fetch(k):
        return pltpu.make_async_copy(probs_hbm.at[pl.ds(2 * k, 2)], prob.at[k % 2], prob_sem.at[k % 2])

    fetch(0).start()
    greet_all(dp, me, n)

    def give(p):
        return pltpu.make_async_remote_copy(
            src_ref=prods_ref.at[p], dst_ref=returned.at[p], send_sem=prod_send.at[p], recv_sem=prod_recv.at[p],
            device_id=(dp, flipped(me, p, n)), device_id_type=MESH)

    def start_prods(i, _):
        give(n - i).start()
        return 0

    lax.fori_loop(1, n, start_prods, 0)
    own_prod = pltpu.make_async_copy(prods_ref.at[0], returned.at[0], own_sem.at[0])
    own_prod.start()

    if scatters:
        own = own_ref.shape[0]
        half = own * n
        second, third = 2 - dp, 1 + dp

        def remote(src, dst, send, recv, k, device):
            return pltpu.make_async_remote_copy(
                src_ref=src, dst_ref=dst, send_sem=send.at[k], recv_sem=recv.at[k], device_id=device, device_id_type=MESH)

        def hop(stage, k):
            if stage == 0:
                return remote(sib_out.at[k], sib_in.at[k], sib_s, sib_r, k, (1 - dp, me))
            if stage == 1:
                return remote(out1.at[k], in1.at[k], s1, r1, k, (dp, flipped(me, third, n)))
            if stage == 2:
                return remote(out2.at[k], in2.at[k], s2, r2, k, (dp, flipped(me, second, n)))
            if stage == 3:
                return remote(out3.at[k], in3.at[k], s3, r3, k, (dp, flipped(me, 8, n)))
            return remote(keep.at[k, own : 2 * own], in4.at[k], s4, r4, k, (dp, flipped(me, 4, n)))

        def unit(k, u):
            r = third * (u // 4) + second * ((u // 2) % 2) + 8 * (u % 2)
            places = [pl.multiple_of(flipped(me, r + z, n) * own, 8) for z in (0, 4)]
            return jnp.concatenate([mine[k, pl.ds(place, own)] for place in places], axis=0)

        def stage(s, k):
            if s == 0:
                there = pl.ds(pl.multiple_of((1 - dp) * half, 8), half)
                here = pl.ds(pl.multiple_of(dp * half, 8), half)
                sib_out[k] = chunk[there].astype(BF16)
                hop(0, k).start()
                mine[k] = chunk[here]
            elif s == 1:
                hop(0, k).wait_recv()
                mine[k] = mine[k] + sib_in[k].astype(F32)
                for u in range(4):
                    out1[k, 2 * own * u : 2 * own * (u + 1)] = unit(k, u + 4).astype(BF16)
                hop(1, k).start()
                for u in range(4):
                    keep[k, 2 * own * u : 2 * own * (u + 1)] = unit(k, u)
            elif s == 2:
                hop(1, k).wait_recv()
                keep[k] = keep[k] + in1[k].astype(F32)
                out2[k] = keep[k, 4 * own :].astype(BF16)
                hop(2, k).start()
            elif s == 3:
                hop(2, k).wait_recv()
                keep[k, : 4 * own] = keep[k, : 4 * own] + in2[k].astype(F32)
                out3[k] = keep[k, 2 * own : 4 * own].astype(BF16)
                hop(3, k).start()
            elif s == 4:
                hop(3, k).wait_recv()
                keep[k, : 2 * own] = keep[k, : 2 * own] + in3[k].astype(F32)
                hop(4, k).start()
            else:
                hop(4, k).wait_recv()
                keep[k, :own] = keep[k, :own] + in4[k]

        def advance(k, newest):
            for s in (5, 4, 3, 2, 1):
                @pl.when((k - s >= 0) & (k - s < chunks))
                def _():
                    stage(s, k - s)
            if newest:
                stage(0, k)
    else:
        def advance(k, newest):
            if newest:
                copy = pltpu.make_async_copy(chunk, qkv_grad_ref.at[k], own_sem.at[1])
                copy.start()
                copy.wait()

    expert_of = routes_ref[...]
    lane = lax.broadcasted_iota(jnp.int32, (count, 128), 1)
    picked = expert_of == lane
    first = lax.broadcasted_iota(jnp.int32, (count, count), 0)
    other = lax.broadcasted_iota(jnp.int32, (count, count), 1)
    before = dot((other < first).astype(BF16), picked.astype(BF16))
    rank = jnp.sum(jnp.where(picked, before, 0.0), axis=1, keepdims=True).astype(jnp.int32)
    block = jnp.bitwise_xor(expert_of, me)
    hits = (block * pad + rank == lax.broadcasted_iota(jnp.int32, (count, total), 1)).astype(BF16)
    ties = lax.dot_general((block == lax.broadcasted_iota(jnp.int32, (count, n), 1)).astype(F32), tie_ref[...],
                           (((1,), (0,)), ((), ())), preferred_element_type=F32, precision=lax.Precision.HIGHEST)
    tie = jnp.sum(jnp.where(lane == rank, ties, 0.0), axis=1, keepdims=True)
    chance = chance_ref[...]
    logit_grad = (tie * (picked.astype(F32) - chance)).astype(BF16)
    grad = dot(hits, back_ref[...].reshape(total, width))
    load.wait()
    grad = grad + dot(logit_grad, w[:, 4 * width : 4 * width + 128], NT)
    mid = middle_ref[...]
    root = lax.rsqrt(jnp.mean(mid * mid, axis=1, keepdims=True) + EPSILON)
    unit_mid = mid * root
    gain_rows = jnp.sum(grad * unit_mid, axis=0, keepdims=True)
    scaled = grad * gains_ref[1:2]
    mid_g = cot_ref[...].astype(F32) + root * (scaled - unit_mid * jnp.mean(scaled * unit_mid, axis=1, keepdims=True))
    mid_grad[...] = mid_g
    attn_grad = mid_g.astype(BF16)
    att_cot[...] = dot(attn_grad, w[:, 3 * width : 4 * width], NT).astype(BF16)
    attended_t = attended_ref[...].T
    for k in range(lead):
        if (k + 1) * part <= width:
            chunk[...] = dot(attended_t, attn_grad[:, k * part : (k + 1) * part])
        else:
            chunk[:, 0:128] = dot(moe_ref[...].T, logit_grad)
            chunk[:, 128:256] = jnp.broadcast_to(gain_rows, (128, width)).T
            chunk[:, 256:] = jnp.zeros((width, part - 256), F32)
        advance(k, True)
    normed_t[...] = normed_ref[...].T

    scale = (width // heads) ** -0.5

    def attend_back(k, _):
        fetch(k).wait()

        @pl.when(k + 1 < heads // 2)
        def _():
            fetch(k + 1).start()

        def piece(c):
            return packed_ref[:, pl.ds(pl.multiple_of(c * width + k * 128, 128), 128)]

        queries, keys, values = piece(0), piece(1), piece(2)
        keys_t = (keys.astype(F32) * scale).T.astype(BF16)
        cot = att_cot[:, pl.ds(pl.multiple_of(k * 128, 128), 128)]
        query_t, key_g, value_g = [], None, None
        for h in (0, 1):
            mask = (lane < 64) == (h == 0)
            own_cot = jnp.where(mask, cot, jnp.zeros_like(cot))
            own_queries = jnp.where(mask, queries, jnp.zeros_like(queries))
            weights = prob[k % 2, h]
            chances = weights.astype(F32)
            weight_grad = dot(values, own_cot, NT)
            product = chances * weight_grad
            score_grad = product - chances * jnp.sum(product, axis=0, keepdims=True)
            score_grad = score_grad.astype(BF16)
            wide = score_grad.astype(F32)
            for b in range(4):
                rows = wide[128 * b : 128 * b + 128]
                cols = slice(384 - 128 * b, 896 - 128 * b)
                if b == 0:
                    strip[:, cols] = rows
                    strip[:, 0:384] = jnp.zeros((128, 384), F32)
                    strip[:, 896:1024] = jnp.zeros((128, 128), F32)
                else:
                    strip[:, cols] += rows
            have = 64
            folded = strip[...]
            while have >= 8:
                folded = folded[:have] + pltpu.roll(folded[have:], 1024 - have, 1)
                have //= 2
            for s in range(1, 8):
                folded = jnp.where(lax.broadcasted_iota(jnp.int32, folded.shape, 0) == s, pltpu.roll(folded, 1024 - s, 1), folded)
            bias_rows[2 * k + h] = folded
            v = dot(weights, own_cot)
            q = dot(score_grad, own_queries)
            value_g = v if h == 0 else value_g + v
            key_g = q if h == 0 else key_g + q
            query_t.append(dot(keys_t[64 * h : 64 * h + 64], score_grad))
        query_g = jnp.concatenate(query_t, axis=0).T.astype(BF16)
        grads = jnp.concatenate([query_g, (key_g * scale).astype(BF16), value_g.astype(BF16)], axis=1)
        for c in range(3):
            packed_grad[:, pl.ds(pl.multiple_of(c * width + k * 128, 128), 128)] = grads[:, c * 128 : (c + 1) * 128]
        chunk[...] = dot(normed_t[...], grads)
        advance(k + lead, True)
        return 0

    lax.fori_loop(0, heads // 2, attend_back, 0)
    sums = jnp.concatenate([jnp.sum(bias_rows[h], axis=0, keepdims=True) for h in range(heads)]
                           + [jnp.zeros((16 - heads, 1024), F32)], axis=0)
    bias_sum = lax.dot_general(sums, hot_ref[...], (((1,), (0,)), ((), ())), preferred_element_type=F32,
                               precision=lax.Precision.HIGHEST)
    if scatters:
        bias_out[0] = bias_sum

        def bias_hop(s):
            device = (1 - dp, me) if s == 0 else (dp, flipped(me, 1 << (s - 1), n))
            return remote(bias_out.at[s], bias_in.at[s], bias_s, bias_r, s, device)

        steps = n.bit_length()
        bias_hop(0).start()

    def settle(s):
        if scatters:
            advance(chunks + s, False)
            if s < steps:
                bias_hop(s).wait_recv()
                total_bias = bias_out[s] + bias_in[s]
                if s + 1 < steps:
                    bias_out[s + 1] = total_bias
                    bias_hop(s + 1).start()
                else:
                    bias_grad_ref[...] = total_bias

    settle(0)
    normed_grad = dot(packed_grad[...], w[:, : 3 * width], NT)
    settle(1)
    x = tokens_ref[...].astype(F32)
    root = lax.rsqrt(jnp.mean(x * x, axis=1, keepdims=True) + EPSILON)
    unit_x = x * root
    scaled = normed_grad * gains_ref[0:1]
    tokens_grad_ref[...] = mid_grad[...] + root * (
        scaled - unit_x * jnp.mean(scaled * unit_x, axis=1, keepdims=True))
    settle(2)

    def settle_prods(p, _):
        give(p).wait_recv()
        return 0

    own_prod.wait()
    lax.fori_loop(1, n, settle_prods, 0)
    gate = jnp.sum(jnp.where(picked, chance, 0.0), axis=1, keepdims=True)
    mixed_ref[...] = (middle_ref[...] + gate * dot(hits, returned[...].reshape(total, width))).astype(BF16)
    settle(3)
    settle(4)
    if scatters:
        for k in range(chunks):
            done = keep[k, :own]
            if k < lead:
                if (k + 1) * part <= width:
                    att_grad_ref[:, k * part : (k + 1) * part] = done
                else:
                    extra_grad_ref[...] = done[:, :256]
            else:
                for c in range(3):
                    start = c * width + (k - lead) * 128
                    qkv_grad_ref[:, start : start + 128] = done[:, c * 128 : (c + 1) * 128]
        total_gain = jnp.sum(qkv_grad_ref[...] * own_ref[...][:, : 3 * width], axis=1, keepdims=True)
        gain_grad_ref[...] = jnp.broadcast_to(total_gain / gain_ref[...], gain_grad_ref.shape)

        def settle_sends(k, _):
            for s in range(5):
                hop(s, k).wait_send()
            return 0

        lax.fori_loop(0, chunks, settle_sends, 0)
        for s in range(steps):
            bias_hop(s).wait_send()
    else:
        bias_grad_ref[...] = bias_sum

    def settle_sent(p, _):
        give(p).wait_send()
        return 0

    lax.fori_loop(1, n, settle_sent, 0)


def backward(n, pad, experts, heads, scatters, back, ties, prods, routes, cot, tokens, middle, moe_in, chance, attended,
             normed, packed, gains, hot, own, gain, probs, w):
    count, width = tokens.shape
    wide = w.shape[1]
    rows = own.shape[0]
    half = rows * n
    part = 3 * 128
    chunks = (width + 256 + part - 1) // part + heads // 2
    any_ = pl.BlockSpec(memory_space=pl.ANY)
    vmem = pl.BlockSpec(memory_space=pltpu.VMEM)
    dma = pltpu.SemaphoreType.DMA
    small = (1, 8, 128)

    def buffer(shape, kind):
        return pltpu.VMEM(shape if scatters else small, kind)

    return pl.pallas_call(
        functools.partial(backward_kernel, n, pad, experts, heads, scatters),
        out_shape=(
            jax.ShapeDtypeStruct((count, width), BF16),
            jax.ShapeDtypeStruct((count, width), F32),
            jax.ShapeDtypeStruct((rows, 3 * width) if scatters else (chunks, width, part), F32),
            jax.ShapeDtypeStruct((rows, width), F32),
            jax.ShapeDtypeStruct((rows, 256), F32),
            jax.ShapeDtypeStruct((rows, 128), F32),
            jax.ShapeDtypeStruct((16, 128), F32),
        ),
        in_specs=[vmem] * 16 + [any_, any_],
        out_specs=(vmem, vmem, vmem if scatters else any_, vmem, vmem, vmem, vmem),
        scratch_shapes=[
            pltpu.VMEM((width, wide), BF16),
            pltpu.VMEM((2, 2, count, count), BF16),
            pltpu.VMEM((n, pad, width), BF16),
            pltpu.VMEM((count, width), F32),
            pltpu.VMEM((count, width), BF16),
            pltpu.VMEM((count, 3 * width), BF16),
            pltpu.VMEM((width, count), BF16),
            pltpu.VMEM((width, part), F32),
            pltpu.VMEM((128, 1024), F32),
            pltpu.VMEM((heads, 8, 1024), F32),
            buffer((chunks, half, part), BF16),
            buffer((chunks, half, part), BF16),
            buffer((chunks, half, part), F32),
            buffer((chunks, half // 2, part), BF16),
            buffer((chunks, half // 2, part), BF16),
            buffer((chunks, half // 2, part), F32),
            buffer((chunks, half // 4, part), BF16),
            buffer((chunks, half // 4, part), BF16),
            buffer((chunks, half // 8, part), BF16),
            buffer((chunks, half // 8, part), BF16),
            buffer((chunks, rows, part), F32),
            pltpu.VMEM((5, 16, 128), F32),
            pltpu.VMEM((5, 16, 128), F32),
            dma((1,)), dma((2,)), dma((n,)), dma((n,)),
            *[dma((chunks,)) for _ in range(10)],
            dma((5,)), dma((5,)), dma((2,)),
        ],
        compiler_params=pltpu.CompilerParams(
            collective_id=3, has_side_effects=True, vmem_limit_bytes=62 * 1024 * 1024),
        name="backward",
    )(back, ties, prods, routes, cot, tokens, middle, moe_in, chance, attended, normed, packed, gains, hot, own, gain,
      probs, w)


def shards(
    n, tokens, cotangent, routes, buckets, gain_attn, w_qkv, w_att, rel_bias, gain_moe, w_router, w_in, w_out,
):
    axes = ("dp", "expert")
    count, width = tokens.shape
    experts = w_router.shape[1]
    heads = rel_bias.shape[1]
    own = w_qkv.shape[0]
    cap = max(2, 2 * count // experts)
    pad = max(16, cap)
    direct = n == 16 and own % 8 == 0
    blank = jnp.zeros((own, 128 - experts), w_qkv.dtype), jnp.zeros((own, 126), w_qkv.dtype)
    bundle = jnp.concatenate([w_qkv, w_att, w_router, blank[0], gain_attn[:, None], gain_moe[:, None], blank[1]], axis=1)
    weights = bundle.astype(F32) if direct else lax.all_gather(bundle, axes, axis=0, tiled=True)
    line = jnp.concatenate([buckets[0, :385][::-1], buckets[1:, 0], buckets[0, -1:], buckets[0, 385:][::-1]])
    hot = (line[:, None] == jnp.arange(128, dtype=jnp.int32)[None, :]).astype(F32)
    bias = jnp.dot(rel_bias.T, hot[:, : rel_bias.shape[0]].T, precision=lax.Precision.HIGHEST)
    bias = jnp.stack([jnp.roll(bias, s, axis=1) for s in range(8)], axis=1)
    rows, cots, probs, packed, normed, attended, middle, moe_in, chance, w, gains = forward(
        n, pad, experts, heads, direct, tokens, cotangent, weights, routes.reshape(1, count), bias)
    back, ties, prods, grad_in, grad_out = moe(n, cap, pad, experts, rows, cots, w, w_in[0], w_out[0])
    gain_column = gain_attn.astype(F32)[:, None]
    mixed, grad_tokens, grad_qkv, grad_att, grad_extra, grad_gain, grad_bias = backward(
        n, pad, experts, heads, direct, back, ties[:, 0], prods, routes, cotangent, tokens, middle, moe_in, chance,
        attended, normed, packed, gains, hot, bundle.astype(F32), gain_column, probs, w)
    if not direct:
        lead = grad_qkv.shape[0] - heads // 2
        early = jnp.concatenate([grad_qkv[k] for k in range(lead)], axis=1)
        late = [grad_qkv[lead:, :, c * 128 : (c + 1) * 128].transpose(1, 0, 2).reshape(width, width) for c in range(3)]
        both = lax.psum_scatter(jnp.concatenate([early, *late], axis=1), axes, scatter_dimension=0, tiled=True)
        grad_att, grad_extra = both[:, :width], both[:, width : width + 256]
        grad_qkv = both[:, early.shape[1] :]
        grad_gain = jnp.sum(grad_qkv * w_qkv.astype(F32), axis=1, keepdims=True) / gain_column
        grad_bias = lax.psum(grad_bias, axes)
    return (
        mixed, grad_tokens, grad_gain[:, 0], grad_qkv, grad_att, grad_bias[:heads, : rel_bias.shape[0]].T,
        grad_extra[:, 128], grad_extra[:, :experts], grad_in[None], grad_out[None],
    )


def solution(mesh):
    both = P(("dp", "expert"))
    return jax.shard_map(
        functools.partial(shards, mesh.shape["expert"]),
        mesh=mesh,
        in_specs=(both, both, both, P(), both, both, both, P(), both, both, P("expert"), P("expert")),
        out_specs=(both, both, both, both, both, P(), both, both, P("expert", None, "dp"), P("expert", None, "dp")),
        check_vma=False,
    )
```

```python
import functools
import jax
import jax.numpy as jnp
from jax import lax
from jax.experimental import pallas as pl
from jax.experimental.pallas import tpu as pltpu
from jax.sharding import PartitionSpec as P

MESH = pl.DeviceIdType.MESH
F32, BF16 = jnp.float32, jnp.bfloat16
NT = (((1,), (1,)), ((), ()))
EPSILON = 1e-06


def dot(a, b, dims=(((1,), (0,)), ((), ()))):
    return lax.dot_general(a, b, dims, preferred_element_type=F32)


def flipped(index, bits, count):
    result, bit = 0, 1
    while bit < count:
        result = result + bit * (((index // bit) % 2 + (bits // bit) % 2) % 2)
        bit *= 2
    return result


def gelu_parts(hidden):
    c0, c1 = 0.7978845608028654, 0.044715
    square = hidden * hidden
    bend = jnp.tanh(hidden * (c0 + (c0 * c1) * square))
    half = 0.5 + 0.5 * bend
    slope = half + (0.5 * hidden) * (1.0 - bend * bend) * (c0 + (3.0 * c0 * c1) * square)
    return hidden * half, slope


def slots_by_row(routes, me, pad, experts):
    count = routes.shape[1]
    picked = routes == lax.broadcasted_iota(jnp.int32, (experts, count), 0)
    first = lax.broadcasted_iota(jnp.int32, (count, count), 0)
    second = lax.broadcasted_iota(jnp.int32, (count, count), 1)
    before = dot(picked.astype(BF16), (first < second).astype(BF16))
    rank = jnp.sum(jnp.where(picked, before, 0.0), axis=0, keepdims=True).astype(jnp.int32)
    return jnp.bitwise_xor(routes, me) * pad + rank


def greet_all(dp, me, n):
    barrier = pltpu.get_barrier_semaphore()

    def greet(p, _):
        pl.semaphore_signal(barrier, inc=1, device_id=(dp, flipped(me, p, n)), device_id_type=MESH)
        return 0

    lax.fori_loop(1, n, greet, 0)
    pl.semaphore_signal(barrier, inc=1, device_id=(1 - dp, me), device_id_type=MESH)
    pl.semaphore_wait(barrier, n)


def grow_strip(strip, w8):
    strip[0:8] = w8
    have = 8
    while have < strip.shape[0]:
        strip[have : 2 * have] = pltpu.roll(strip[0:have], have, 1)
        have *= 2


def forward_kernel(
    n, pad, experts, heads, gathers, *refs,
):
    (tokens_ref, cot_ref, qkv_ref, att_ref, extra_ref, full_hbm, routes_ref, table_ref, buckets_hbm,
     rows_hbm, cots_hbm, probs_hbm, packed_hbm, normed_hbm, attended_hbm, middle_hbm, moe_hbm, chance_hbm, w_hbm, gains_ref, hot_ref,
     w, packed, normed, attended, middle, moe_in, chance, rows, cots, probs, strip,
     bias, ends, weights_ref, shard, blocks, put_sem, cot_send, cot_recv, tree_send, tree_recv, sib_send, sib_recv, pair_sem) = refs
    dp, me = lax.axis_index("dp"), lax.axis_index("expert")
    count, width = tokens_ref.shape
    total = n * pad
    puts = []

    def put(src, dst):
        copy = pltpu.make_async_copy(src, dst, put_sem.at[len(puts)])
        copy.start()
        puts.append(copy)

    offsets = [pltpu.make_async_copy(buckets_hbm.at[:, pl.ds(c, 128)], ends.at[i], put_sem.at[9 + i])
               for i, c in enumerate((0, count - 128))]
    for copy in offsets:
        copy.start()
    if gathers:
        weights_ref[:, : 3 * width] = qkv_ref[...].astype(F32)
        weights_ref[:, 3 * width : 3 * width + 256] = extra_ref[...].T[: weights_ref.shape[0]]
        weights_ref[:, 3 * width + 256 :] = att_ref[...].astype(F32)
    greet_all(dp, me, n)
    if gathers:
        own = weights_ref.shape[0]
        block = 2 * own
        early = 3 * width + 256
        pair = pltpu.make_async_remote_copy(
            src_ref=weights_ref, dst_ref=shard, send_sem=pair_sem.at[0], recv_sem=pair_sem.at[1],
            device_id=(1 - dp, me), device_id_type=MESH)
        pair.start()
    else:
        load = pltpu.make_async_copy(full_hbm, w, pair_sem.at[0])
        load.start()
    slots = slots_by_row(routes_ref[...], me, pad, experts)
    hits = (slots == lax.broadcasted_iota(jnp.int32, (total, count), 0)).astype(BF16)
    cots[...] = dot(hits, cot_ref[...]).astype(BF16).reshape(n, pad, width)
    cots_own = pltpu.make_async_copy(cots.at[0], cots_hbm.at[0], pair_sem.at[2])
    cots_own.start()
    for copy in offsets:
        copy.wait()
    last, first = ends[1].astype(F32).T[127:128], ends[0].astype(F32).T[0:1]
    line = jnp.concatenate([last, pltpu.roll(first, count - 1, 1)], axis=1)
    line = pltpu.roll(jnp.broadcast_to(line, (8, 2 * count)), 2 * count - 127, 1)[0:1]
    kinds = table_ref.shape[1]
    hot = (line.astype(jnp.int32) == lax.broadcasted_iota(jnp.int32, (kinds, 2 * count), 0)).astype(F32)
    hot_ref[...] = hot
    table = lax.dot_general(table_ref[...], hot, (((1,), (0,)), ((), ())), preferred_element_type=F32,
                            precision=lax.Precision.HIGHEST)
    for h in range(heads):
        row = jnp.broadcast_to(table[h : h + 1], (8, 2 * count))
        place = lax.broadcasted_iota(jnp.int32, row.shape, 0)
        shifted = row
        for r in range(1, 8):
            shifted = jnp.where(place == r, pltpu.roll(row, r, 1), shifted)
        bias[h] = shifted
    x = tokens_ref[...].astype(F32)
    unit = x * lax.rsqrt(jnp.mean(x * x, axis=1, keepdims=True) + EPSILON)

    def cot_copy(p):
        return pltpu.make_async_remote_copy(
            src_ref=cots.at[p], dst_ref=cots_hbm.at[p], send_sem=cot_send.at[p], recv_sem=cot_recv.at[p],
            device_id=(dp, flipped(me, p, n)), device_id_type=MESH)

    def start_cots(early):
        def one(p, _):
            @pl.when((p % 4 == 0) == early)
            def _():
                cot_copy(p).start()
            return 0

        lax.fori_loop(1, n, one, 0)

    if gathers:
        pair.wait()
        mine, other = weights_ref[...], shard[...]
        blocks[pl.ds(pl.multiple_of(me * block, 16), block)] = jnp.concatenate(
            [jnp.where(dp == 0, mine, other), jnp.where(dp == 0, other, mine)], axis=0).astype(BF16)
        second, third = 2 - dp, 1 + dp
        far = list(range(4, n, 4))
        near = [0] + far

        def at(t, r, core):
            start, size = ((0, early // 2), (early, width // 2))[t]
            return blocks.at[pl.ds(pl.multiple_of(flipped(me, r, n) * block, 16), block),
                             pl.ds(pl.multiple_of(start + core * size, 128), size)]

        def hop(t, r, step):
            return pltpu.make_async_remote_copy(
                src_ref=at(t, r, dp), dst_ref=at(t, r, dp),
                send_sem=tree_send.at[t, r + step], recv_sem=tree_recv.at[t, r + step],
                device_id=(dp, flipped(me, step, n)), device_id_type=MESH)

        def arrived(t, r):
            pltpu.make_async_remote_copy(
                src_ref=at(t, r, dp), dst_ref=at(t, r, dp), send_sem=tree_send.at[t, r], recv_sem=tree_recv.at[t, r],
                device_id=(dp, flipped(me, r, n)), device_id_type=MESH).wait_recv()

        def to_sibling(t, r):
            return pltpu.make_async_remote_copy(
                src_ref=at(t, r, dp), dst_ref=at(t, r, dp), send_sem=sib_send.at[t, r], recv_sem=sib_recv.at[t, r],
                device_id=(1 - dp, me), device_id_type=MESH)

        def from_sibling(t, r):
            return pltpu.make_async_remote_copy(
                src_ref=at(t, r, 1 - dp), dst_ref=at(t, r, 1 - dp), send_sem=sib_send.at[t, r], recv_sem=sib_recv.at[t, r],
                device_id=(1 - dp, me), device_id_type=MESH)

        def turn(t, step):
            if step == 0:
                for r in far:
                    hop(t, 0, r).start()
                hop(t, 0, third).start()
                hop(t, 0, second).start()
            elif step == 1:
                for r in far:
                    arrived(t, r)
                    hop(t, r, third).start()
                    hop(t, r, second).start()
                    to_sibling(t, r).start()
            elif step == 2:
                for r in near:
                    arrived(t, r + second)
                    hop(t, r + second, third).start()
                    to_sibling(t, r + second).start()
            elif step == 3:
                for r in near:
                    arrived(t, r + third)
                    to_sibling(t, r + third).start()
                    arrived(t, r + 3)
                    to_sibling(t, r + 3).start()
            else:
                def settle(r, _):
                    from_sibling(t, r).wait_recv()
                    return 0

                lax.fori_loop(1, n, settle, 0)
                place = (slice(0, early), slice(early, w.shape[1]))[t]
                for core in (0, 1):
                    for q in range(n // 2):
                        low = 2 * q * block + core * own
                        pair_rows = [blocks[p : p + own, place].astype(F32) for p in (low, low + block)]
                        w[core * own * n + q * block : core * own * n + (q + 1) * block, place] = jnp.concatenate(
                            pair_rows, axis=0).astype(BF16)

        turn(0, 0)
        turn(0, 1)
        turn(1, 0)
        turn(0, 2)
        start_cots(True)
        turn(1, 1)
        turn(0, 3)
        turn(1, 2)
        start_cots(False)
        turn(0, 4)
    else:
        start_cots(True)
        start_cots(False)
        load.wait()
    gains_ref[...] = w[:, 3 * width + 128 : 3 * width + 256].astype(F32).T[0:8]
    normed[...] = (unit * gains_ref[0:1]).astype(BF16)
    put(normed, normed_hbm)
    for c in range(3):
        cols_c = slice(c * width, (c + 1) * width)
        packed[:, cols_c] = dot(normed[...], w[:, cols_c]).astype(BF16)
    put(packed, packed_hbm)
    scale = (width // heads) ** -0.5
    lane = lax.broadcasted_iota(jnp.int32, (count, 128), 1)

    def attend(k, _):
        def part(c):
            return packed[:, pl.ds(pl.multiple_of(c * width + k * 128, 128), 128)]

        queries = (part(0).astype(F32) * scale).astype(BF16)
        keys = part(1)
        values = part(2).astype(F32).T.astype(BF16)
        outs = []
        for h in (0, 1):
            grow_strip(strip, bias[2 * k + h])
            own_keys = jnp.where((lane < 64) == (h == 0), keys, jnp.zeros_like(keys))
            scores = dot(own_keys, queries, NT)
            scores = jnp.concatenate(
                [scores[128 * b : 128 * b + 128] + strip[:, 384 - 128 * b : 896 - 128 * b] for b in range(4)], axis=0)
            powers = jnp.exp(scores - jnp.max(scores, axis=0, keepdims=True))
            weights = (powers * (1.0 / jnp.sum(powers, axis=0, keepdims=True))).astype(BF16)
            probs[2 * k + h] = weights
            outs.append(dot(values[64 * h : 64 * h + 64], weights))
        attended[:, pl.ds(pl.multiple_of(k * 128, 128), 128)] = jnp.concatenate(outs, axis=0).T.astype(BF16)
        if gathers:
            for step in (3, 4):
                @pl.when(k == step - 2)
                def _():
                    turn(1, step)
        return 0

    lax.fori_loop(0, heads // 2, attend, 0)
    put(w, w_hbm)
    put(probs, probs_hbm)
    put(attended, attended_hbm)
    mid = tokens_ref[...].astype(F32) + dot(attended[...], w[:, 3 * width + 256 :])
    middle[...] = mid
    put(middle, middle_hbm)
    moe = (mid * lax.rsqrt(jnp.mean(mid * mid, axis=1, keepdims=True) + EPSILON) * gains_ref[1:2]).astype(BF16)
    moe_in[...] = moe
    put(moe_in, moe_hbm)
    hits = (slots == lax.broadcasted_iota(jnp.int32, (total, count), 0)).astype(BF16)
    rows[...] = dot(hits, moe).astype(BF16).reshape(n, pad, width)
    put(rows, rows_hbm)
    logits = dot(moe, w[:, 3 * width : 3 * width + 128])
    logits = jnp.where(lane < experts, logits, -1e30)
    powers = jnp.exp(logits - jnp.max(logits, axis=1, keepdims=True))
    chance[...] = powers / jnp.sum(powers, axis=1, keepdims=True)
    put(chance, chance_hbm)
    if gathers:
        for t in (0, 1):
            for r in far:
                hop(t, 0, r).wait_send()
            for r in near:
                hop(t, r, second).wait_send()
                hop(t, r, third).wait_send()
                hop(t, r + second, third).wait_send()

            def settle_sends(r, _):
                to_sibling(t, r).wait_send()
                return 0

            lax.fori_loop(1, n, settle_sends, 0)

    def settle_cots(p, _):
        cot_copy(p).wait_send()
        cot_copy(p).wait_recv()
        return 0

    lax.fori_loop(1, n, settle_cots, 0)
    cots_own.wait()
    for copy in puts:
        copy.wait()


def forward(n, pad, experts, heads, gathers, tokens, cotangent, qkv, att, extra, full, routes, table, buckets):
    count, width = tokens.shape
    wide = 4 * width + 256
    any_ = pl.BlockSpec(memory_space=pl.ANY)
    vmem = pl.BlockSpec(memory_space=pltpu.VMEM)
    dma = pltpu.SemaphoreType.DMA
    own = qkv.shape[0]
    shapes = [
        ((n, pad, width), BF16), ((n, pad, width), BF16), ((heads, count, count), BF16), ((count, 3 * width), BF16),
        ((count, width), BF16), ((count, width), BF16), ((count, width), F32), ((count, width), BF16),
        ((count, 128), F32), ((width, wide), BF16), ((8, width), F32), ((table.shape[1], 2 * count), F32),
    ]
    return pl.pallas_call(
        functools.partial(forward_kernel, n, pad, experts, heads, gathers),
        out_shape=tuple(jax.ShapeDtypeStruct(*s) for s in shapes),
        in_specs=[vmem] * 5 + [any_, vmem, vmem, any_],
        out_specs=tuple([any_] * 10 + [vmem] * 2),
        scratch_shapes=[
            pltpu.VMEM((width, wide), BF16),
            pltpu.VMEM((count, 3 * width), BF16),
            pltpu.VMEM((count, width), BF16),
            pltpu.VMEM((count, width), BF16),
            pltpu.VMEM((count, width), F32),
            pltpu.VMEM((count, width), BF16),
            pltpu.VMEM((count, 128), F32),
            pltpu.VMEM((n, pad, width), BF16),
            pltpu.VMEM((n, pad, width), BF16),
            pltpu.VMEM((heads, count, count), BF16),
            pltpu.VMEM((128, 1024), F32),
            pltpu.VMEM((heads, 8, 2 * count), F32),
            pltpu.VMEM((2, count, 128), jnp.int32),
            pltpu.VMEM((own, wide) if gathers else (8, 128), F32),
            pltpu.VMEM((own, wide) if gathers else (8, 128), F32),
            pltpu.VMEM((width, wide) if gathers else (16, 128), BF16),
            dma((11,)), dma((n,)), dma((n,)), dma((2, n)), dma((2, n)), dma((2, n)), dma((2, n)), dma((3,)),
        ],
        compiler_params=pltpu.CompilerParams(
            collective_id=1, has_side_effects=True, vmem_limit_bytes=60 * 1024 * 1024),
        name="forward",
    )(tokens, cotangent, qkv, att, extra, full, routes, table, buckets)


def moe_kernel(
    n, cap, pad, experts,
    rows_ref, cin, w_hbm, win_hbm, wout_hbm,
    back_ret, tie_ret, prod_out, gin_ref, gout_ref,
    win, wout, router, xin, xt, rt, act, hgr, backs, ties, prods,
    sib_send, sib_recv, stage,
    wsem, send_sem, recv_sem, ret_send, ret_recv, own_sem, sib_ss, sib_rs, out_sem,
):
    dp, me = lax.axis_index("dp"), lax.axis_index("expert")
    width, ff = win.shape
    per = 256 // cap
    groups = n // per
    rows = per * cap
    chunk = 1024
    load_in = pltpu.make_async_copy(win_hbm, win, wsem.at[0])
    load_out = pltpu.make_async_copy(wout_hbm, wout, wsem.at[1])
    load_router = pltpu.make_async_copy(w_hbm.at[:, pl.ds(3 * width, 128)], router, wsem.at[2])
    load_router.start()
    load_in.start()
    load_out.start()
    greet_all(dp, me, n)

    def send(p):
        return pltpu.make_async_remote_copy(
            src_ref=rows_ref.at[p], dst_ref=xin.at[p], send_sem=send_sem.at[p], recv_sem=recv_sem.at[p],
            device_id=(dp, flipped(me, p, n)), device_id_type=MESH,
        )

    def give(kind, p):
        src, dst = ((backs, back_ret), (ties, tie_ret))[kind]
        return pltpu.make_async_remote_copy(
            src_ref=src.at[p], dst_ref=dst.at[p],
            send_sem=ret_send.at[kind, p], recv_sem=ret_recv.at[kind, p],
            device_id=(dp, flipped(me, p, n)), device_id_type=MESH,
        )

    def start(early):
        def one(p, _):
            @pl.when(((p < 4) | (p % 4 == 0)) == early)
            def _():
                send(p).start()
            return 0

        lax.fori_loop(1, n, one, 0)

    start(True)
    xin[0] = rows_ref[0]
    load_router.wait()
    load_in.wait()
    load_out.wait()

    def packed_rows(ref, g):
        block = ref[pl.ds(g * per, per)].reshape(per * pad, width)
        if pad == cap:
            return block
        r = lax.broadcasted_iota(jnp.int32, (rows, per * pad), 0)
        c = lax.broadcasted_iota(jnp.int32, (rows, per * pad), 1)
        return dot(((r // cap) * pad + r % cap == c).astype(BF16), block).astype(BF16)

    def spread_rows(block):
        if pad == cap:
            return block
        r = lax.broadcasted_iota(jnp.int32, (per * pad, rows), 0)
        c = lax.broadcasted_iota(jnp.int32, (per * pad, rows), 1)
        pick = (r // pad == c // cap) & (r % pad == c % cap)
        return dot(pick.astype(BF16), block).astype(BF16)

    def group(g, _):
        def arrive(j, _):
            send(g * per + j).wait_recv()
            return 0

        @pl.when(g == 0)
        def _():
            lax.fori_loop(1, 4, arrive, 0)
            start(False)
            lax.fori_loop(4, per, arrive, 0)

        @pl.when(g != 0)
        def _():
            lax.fori_loop(0, per, arrive, 0)

        here = pl.ds(pl.multiple_of(g * rows, rows), rows)
        x = packed_rows(xin, g)
        logits = dot(x, router[...])
        lane = lax.broadcasted_iota(jnp.int32, logits.shape, 1)
        logits = jnp.where(lane < experts, logits, -1e30)
        chance = jnp.exp(logits - jnp.max(logits, axis=1, keepdims=True))
        gate = jnp.sum(jnp.where(lane == me, chance, 0.0), axis=1, keepdims=True) / jnp.sum(
            chance, axis=1, keepdims=True)
        r = (gate * packed_rows(cin, g).astype(F32)).astype(BF16)
        xt[:, here] = x.T
        rt[:, here] = r.T

        def hidden_chunk(k, _):
            cols = pl.ds(pl.multiple_of(k * chunk, chunk), chunk)
            hidden = dot(x, win[:, cols])
            value, slope = gelu_parts(hidden)
            value = value.astype(BF16)
            act[here, cols] = value
            hg = (dot(r, wout[:, cols]) * slope).astype(BF16)
            hgr[here, cols] = hg
            return 0

        lax.fori_loop(0, ff // chunk, hidden_chunk, 0)
        backs[pl.ds(g * per, per)] = spread_rows(dot(hgr[here], win[...], NT).astype(BF16)).reshape(per, pad, width)

        def leave(kind):
            def one(j, _):
                p = g * per + j

                @pl.when(p != 0)
                def _():
                    give(kind, p).start()
                return 0

            lax.fori_loop(0, per, one, 0)

        leave(0)
        produced = dot(act[here], wout[...], NT).astype(BF16)
        prods[pl.ds(g * per, per)] = spread_rows(produced).reshape(per, pad, width)
        tie = jnp.sum(r.astype(F32) * produced.astype(F32), axis=1, keepdims=True)
        for j in range(per):
            row = jnp.broadcast_to(tie[j * cap : (j + 1) * cap], (cap, 128)).T[0:8]
            ties[g * per + j] = jnp.concatenate([row, jnp.zeros((8, 128 - cap), F32)], axis=1)
        leave(1)
        return 0

    lax.fori_loop(0, groups, group, 0)
    own_back = pltpu.make_async_copy(backs.at[0], back_ret.at[0], own_sem.at[0])
    own_tie = pltpu.make_async_copy(ties.at[0], tie_ret.at[0], own_sem.at[1])
    out_prod = pltpu.make_async_copy(prods, prod_out, own_sem.at[2])
    own_back.start()
    own_tie.start()
    out_prod.start()

    half = ff // 2
    part = sib_send.shape[3]
    steps = half // part

    def sibling(kind, k):
        return pltpu.make_async_remote_copy(
            src_ref=sib_send.at[kind, k], dst_ref=sib_recv.at[kind, k],
            send_sem=sib_ss.at[kind, k], recv_sem=sib_rs.at[kind, k],
            device_id=(1 - dp, me), device_id_type=MESH,
        )

    def partial(kind, owner, k):
        cols = pl.ds(pl.multiple_of(owner * half + k * part, 128), part)
        return dot(xt[...], hgr[:, cols]) if kind == 0 else dot(rt[...], act[:, cols])

    def theirs(k, _):
        for kind in (0, 1):
            sib_send[kind, k] = partial(kind, 1 - dp, k).astype(BF16)
            sibling(kind, k).start()
        return 0

    lax.fori_loop(0, steps, theirs, 0)

    def out_copy(kind, k):
        cols = pl.ds(pl.multiple_of(k * part, 128), part)
        return pltpu.make_async_copy(
            stage.at[kind, k % 2], (gin_ref, gout_ref)[kind].at[:, cols], out_sem.at[kind, k % 2])

    def ours(k, _):
        for kind in (0, 1):
            value = partial(kind, dp, k)
            sibling(kind, k).wait_recv()
            @pl.when(k >= 2)
            def _():
                out_copy(kind, k - 2).wait()
            stage[kind, k % 2] = (value + sib_recv[kind, k].astype(F32)).astype(BF16)
            out_copy(kind, k).start()
        return 0

    lax.fori_loop(0, steps, ours, 0)
    for kind in (0, 1):
        for k in (steps - 2, steps - 1):
            out_copy(kind, k).wait()

    def settle(p, _):
        send(p).wait_send()
        for kind in (0, 1):
            give(kind, p).wait_recv()
            give(kind, p).wait_send()
        return 0

    lax.fori_loop(1, n, settle, 0)

    def settle_sibling(k, _):
        for kind in (0, 1):
            sibling(kind, k).wait_send()
        return 0

    lax.fori_loop(0, steps, settle_sibling, 0)
    own_back.wait()
    own_tie.wait()
    out_prod.wait()


def moe(n, cap, pad, experts, rows, cots, w, win, wout):
    width, ff = win.shape
    total = n * cap
    part = 768
    steps = ff // 2 // part
    any_ = pl.BlockSpec(memory_space=pl.ANY)
    vmem = pl.BlockSpec(memory_space=pltpu.VMEM)
    dma = pltpu.SemaphoreType.DMA
    return pl.pallas_call(
        functools.partial(moe_kernel, n, cap, pad, experts),
        out_shape=(
            jax.ShapeDtypeStruct((n, pad, width), BF16),
            jax.ShapeDtypeStruct((n, 8, 128), F32),
            jax.ShapeDtypeStruct((n, pad, width), BF16),
            jax.ShapeDtypeStruct((width, ff // 2), BF16),
            jax.ShapeDtypeStruct((width, ff // 2), BF16),
        ),
        in_specs=[vmem, vmem, any_, any_, any_],
        out_specs=(any_, any_, any_, any_, any_),
        scratch_shapes=[
            pltpu.VMEM((width, ff), BF16),
            pltpu.VMEM((width, ff), BF16),
            pltpu.VMEM((width, 128), BF16),
            pltpu.VMEM((n, pad, width), BF16),
            pltpu.VMEM((width, total), BF16),
            pltpu.VMEM((width, total), BF16),
            pltpu.VMEM((total, ff), BF16),
            pltpu.VMEM((total, ff), BF16),
            pltpu.VMEM((n, pad, width), BF16),
            pltpu.VMEM((n, 8, 128), F32),
            pltpu.VMEM((n, pad, width), BF16),
            pltpu.VMEM((2, steps, width, part), BF16),
            pltpu.VMEM((2, steps, width, part), BF16),
            pltpu.VMEM((2, 2, width, part), BF16),
            dma((3,)), dma((n,)), dma((n,)), dma((2, n)), dma((2, n)), dma((3,)),
            dma((2, steps)), dma((2, steps)), dma((2, 2)),
        ],
        compiler_params=pltpu.CompilerParams(
            collective_id=2, has_side_effects=True, vmem_limit_bytes=60 * 1024 * 1024),
        cost_estimate=pl.CostEstimate(
            flops=12 * total * width * ff, bytes_accessed=8 * width * ff, transcendentals=total * ff),
        name="experts",
    )(rows, cots, w, win, wout)


LOADS = 11
LAG = (0, 1, 7, 9)


def backward_kernel(n, pad, experts, heads, scatters, *refs):
    (routes_ref, gains_ref, hot_ref, own_ref, gain_ref, probs_hbm, prods_hbm, *rest) = refs
    sources, rest = rest[:LOADS], rest[LOADS:]
    (mixed_ref, tokens_grad_ref, qkv_grad_ref, att_grad_ref, extra_grad_ref, gain_grad_ref, bias_grad_ref, *rest) = rest
    loaded, rest = rest[:LOADS], rest[LOADS:]
    (prob, returned, mid_grad, att_cot, packed_grad, normed_t, chunk, strip, bias_rows,
     sib_out, sib_in, mine, out1, in1, keep, out2, in2, bias_out, bias_in, bias_pair,
     load_sem, prob_sem, prod_send, prod_recv, sib_s, sib_r, s1, r1, s2, r2, bias_s, bias_r, own_sem) = rest
    (back_ref, tie_ref, chance_ref, middle_ref, w, cot_ref, attended_ref, moe_ref, normed_ref, packed_ref, tokens_ref) = loaded
    loads = [pltpu.make_async_copy(sources[i], loaded[i], load_sem.at[i]) for i in range(LOADS)]
    for load in loads:
        load.start()
    dp, me = lax.axis_index("dp"), lax.axis_index("expert")
    count, width = tokens_ref.shape
    total = n * pad
    part = 3 * 128
    lead = (width + 256 + part - 1) // part
    chunks = lead + heads // 2

    def fetch(k):
        return pltpu.make_async_copy(probs_hbm.at[pl.ds(2 * k, 2)], prob.at[k % 2], prob_sem.at[k % 2])

    fetch(0).start()
    greet_all(dp, me, n)

    def give(p):
        return pltpu.make_async_remote_copy(
            src_ref=prods_hbm.at[p], dst_ref=returned.at[p], send_sem=prod_send.at[p], recv_sem=prod_recv.at[p],
            device_id=(dp, flipped(me, p, n)), device_id_type=MESH)

    def start_prods(i, _):
        give(n - i).start()
        return 0

    lax.fori_loop(1, n, start_prods, 0)
    own_prod = pltpu.make_async_copy(prods_hbm.at[0], returned.at[0], own_sem.at[0])
    own_prod.start()

    if scatters:
        own = own_ref.shape[0]
        half = own * n

        def remote(src, dst, send, recv, device):
            return pltpu.make_async_remote_copy(
                src_ref=src, dst_ref=dst, send_sem=send, recv_sem=recv, device_id=device, device_id_type=MESH)

        def hop(stage, k, d):
            if stage == 0:
                return remote(sib_out.at[k], sib_in.at[k], sib_s.at[k], sib_r.at[k], (1 - dp, me))
            if stage == 1:
                return remote(out1.at[k, d - 1], in1.at[k, d - 1], s1.at[k, d - 1], r1.at[k, d - 1],
                              (dp, flipped(me, d, n)))
            return remote(out2.at[k, d - 1], in2.at[k, d - 1], s2.at[k, d - 1], r2.at[k, d - 1],
                          (dp, flipped(me, 4 * d, n)))

        def owners(k, d):
            places = [pl.multiple_of(flipped(me, d + 4 * z, n) * own, 8) for z in range(4)]
            return jnp.concatenate([mine[k, pl.ds(place, own)] for place in places], axis=0)

        def stage(s, k):
            if s == 0:
                there = pl.ds(pl.multiple_of((1 - dp) * half, 8), half)
                here = pl.ds(pl.multiple_of(dp * half, 8), half)
                sib_out[k] = chunk[there].astype(BF16)
                hop(0, k, 0).start()
                mine[k] = chunk[here]
            elif s == 1:
                hop(0, k, 0).wait_recv()
                mine[k] = mine[k] + sib_in[k].astype(F32)
                for d in (3, 1, 2):
                    out1[k, d - 1] = owners(k, d).astype(BF16)
                    hop(1, k, d).start()
                keep[k] = owners(k, 0)
            elif s == 2:
                for d in (1, 2, 3):
                    hop(1, k, d).wait_recv()
                total_rows = keep[k] + (in1[k, 0].astype(F32) + in1[k, 1].astype(F32)) + in1[k, 2].astype(F32)
                for z in (3, 2, 1):
                    block = total_rows[own * z : own * (z + 1)]
                    out2[k, z - 1] = jnp.concatenate(
                        [block[:, 128 * c : 128 * (c + 1)] for c in range(3)]
                        + [jnp.zeros((out2.shape[2] - 3 * own, 128), F32)], axis=0).astype(BF16)
                    hop(2, k, z).start()
                keep[k, :own] = total_rows[:own]
            else:
                for z in (1, 2, 3):
                    hop(2, k, z).wait_recv()
                far = (in2[k, 0].astype(F32) + in2[k, 1].astype(F32)) + in2[k, 2].astype(F32)
                keep[k, :own] = keep[k, :own] + jnp.concatenate(
                    [far[own * c : own * (c + 1)] for c in range(3)], axis=1)

        def advance(k):
            stage(0, k)
            for s in range(1, 4):
                @pl.when((k - LAG[s] >= 0) & (k - LAG[s] < chunks))
                def _():
                    stage(s, k - LAG[s])

        at = {k: max(s for s in range(4) if LAG[s] <= chunks - 1 - k) for k in range(chunks)}

        def drain():
            for k in sorted((k for k in range(chunks) if at[k] < 3), key=lambda k: (at[k] > 0, k)):
                at[k] += 1
                stage(at[k], k)
    else:
        def advance(k):
            copy = pltpu.make_async_copy(chunk, qkv_grad_ref.at[k], own_sem.at[1])
            copy.start()
            copy.wait()

    expert_of = jnp.broadcast_to(routes_ref[...].astype(F32), (128, count)).T[:, 0:1].astype(jnp.int32)
    lane = lax.broadcasted_iota(jnp.int32, (count, 128), 1)
    picked = expert_of == lane
    first = lax.broadcasted_iota(jnp.int32, (count, count), 0)
    other = lax.broadcasted_iota(jnp.int32, (count, count), 1)
    before = dot((other < first).astype(BF16), picked.astype(BF16))
    rank = jnp.sum(jnp.where(picked, before, 0.0), axis=1, keepdims=True).astype(jnp.int32)
    block = jnp.bitwise_xor(expert_of, me)
    for load in loads[:3]:
        load.wait()
    hits = (block * pad + rank == lax.broadcasted_iota(jnp.int32, (count, total), 1)).astype(BF16)
    ties = lax.dot_general((block == lax.broadcasted_iota(jnp.int32, (count, n), 1)).astype(F32), jnp.max(tie_ref[...], axis=1),
                           (((1,), (0,)), ((), ())), preferred_element_type=F32, precision=lax.Precision.HIGHEST)
    tie = jnp.sum(jnp.where(lane == rank, ties, 0.0), axis=1, keepdims=True)
    chance = chance_ref[...]
    logit_grad = (tie * (picked.astype(F32) - chance)).astype(BF16)
    grad = dot(hits, back_ref[...].reshape(total, width))
    for load in loads[3:]:
        load.wait()
    grad = grad + dot(logit_grad, w[:, 3 * width : 3 * width + 128], NT)
    mid = middle_ref[...]
    root = lax.rsqrt(jnp.mean(mid * mid, axis=1, keepdims=True) + EPSILON)
    unit_mid = mid * root
    gain_rows = jnp.sum(grad * unit_mid, axis=0, keepdims=True)
    scaled = grad * gains_ref[1:2]
    mid_g = cot_ref[...].astype(F32) + root * (scaled - unit_mid * jnp.mean(scaled * unit_mid, axis=1, keepdims=True))
    mid_grad[...] = mid_g
    attn_grad = mid_g.astype(BF16)
    att_cot[...] = dot(attn_grad, w[:, 3 * width + 256 :], NT).astype(BF16)
    attended_t = attended_ref[...].T
    for k in range(lead):
        if (k + 1) * part <= width:
            chunk[...] = dot(attended_t, attn_grad[:, k * part : (k + 1) * part])
        else:
            chunk[:, 0:128] = dot(moe_ref[...].T, logit_grad)
            chunk[:, 128:256] = jnp.broadcast_to(gain_rows, (128, width)).T
            chunk[:, 256:] = jnp.zeros((width, part - 256), F32)
        advance(k)
    normed_t[...] = normed_ref[...].T

    scale = (width // heads) ** -0.5

    def attend_back(k, _):
        fetch(k).wait()

        @pl.when(k + 1 < heads // 2)
        def _():
            fetch(k + 1).start()

        def piece(c):
            return packed_ref[:, pl.ds(pl.multiple_of(c * width + k * 128, 128), 128)]

        queries, keys, values = piece(0), piece(1), piece(2)
        keys_t = (keys.astype(F32) * scale).T.astype(BF16)
        cot = att_cot[:, pl.ds(pl.multiple_of(k * 128, 128), 128)]
        query_t, key_g, value_g = [], None, None
        for h in (0, 1):
            mask = (lane < 64) == (h == 0)
            own_cot = jnp.where(mask, cot, jnp.zeros_like(cot))
            own_queries = jnp.where(mask, queries, jnp.zeros_like(queries))
            weights = prob[k % 2, h]
            chances = weights.astype(F32)
            weight_grad = dot(values, own_cot, NT)
            product = chances * weight_grad
            score_grad = product - chances * jnp.sum(product, axis=0, keepdims=True)
            score_grad = score_grad.astype(BF16)
            wide = score_grad.astype(F32)
            for b in range(4):
                rows = wide[128 * b : 128 * b + 128]
                cols = slice(384 - 128 * b, 896 - 128 * b)
                if b == 0:
                    strip[:, cols] = rows
                    strip[:, 0:384] = jnp.zeros((128, 384), F32)
                    strip[:, 896:1024] = jnp.zeros((128, 128), F32)
                else:
                    strip[:, cols] += rows
            have = 64
            folded = strip[...]
            while have >= 8:
                folded = folded[:have] + pltpu.roll(folded[have:], 1024 - have, 1)
                have //= 2
            for s in range(1, 8):
                folded = jnp.where(lax.broadcasted_iota(jnp.int32, folded.shape, 0) == s, pltpu.roll(folded, 1024 - s, 1), folded)
            bias_rows[2 * k + h] = folded
            v = dot(weights, own_cot)
            q = dot(score_grad, own_queries)
            value_g = v if h == 0 else value_g + v
            key_g = q if h == 0 else key_g + q
            query_t.append(dot(keys_t[64 * h : 64 * h + 64], score_grad))
        query_g = jnp.concatenate(query_t, axis=0).T.astype(BF16)
        grads = jnp.concatenate([query_g, (key_g * scale).astype(BF16), value_g.astype(BF16)], axis=1)
        for c in range(3):
            packed_grad[:, pl.ds(pl.multiple_of(c * width + k * 128, 128), 128)] = grads[:, c * 128 : (c + 1) * 128]
        chunk[...] = dot(normed_t[...], grads)
        advance(k + lead)
        return 0

    lax.fori_loop(0, heads // 2, attend_back, 0)
    if scatters:
        drain()
    sums = jnp.concatenate([jnp.sum(bias_rows[h], axis=0, keepdims=True) for h in range(heads)], axis=0)
    bias_sum = lax.dot_general(sums, hot_ref[...], NT, preferred_element_type=F32, precision=lax.Precision.HIGHEST)
    if scatters:
        bias_out[...] = bias_sum
        pair_hop = remote(bias_out, bias_pair, own_sem.at[1], own_sem.at[2], (1 - dp, me))
        pair_hop.start()

        def bias_hop(p):
            return remote(bias_in.at[me], bias_in.at[me], bias_s.at[p], bias_r.at[p], (dp, flipped(me, p, n)))

        def bias_arrived(p):
            there = flipped(me, p, n)
            return remote(bias_in.at[there], bias_in.at[there], bias_s.at[p], bias_r.at[p], (dp, there))

    normed_grad = dot(packed_grad[...], w[:, : 3 * width], NT)
    if scatters:
        drain()
        pair_hop.wait()
        bias_in[me] = bias_out[...] + bias_pair[...]

        def start_bias(p, _):
            bias_hop(p).start()
            return 0

        lax.fori_loop(1, n, start_bias, 0)
    x = tokens_ref[...].astype(F32)
    root = lax.rsqrt(jnp.mean(x * x, axis=1, keepdims=True) + EPSILON)
    unit_x = x * root
    scaled = normed_grad * gains_ref[0:1]
    tokens_grad_ref[...] = mid_grad[...] + root * (
        scaled - unit_x * jnp.mean(scaled * unit_x, axis=1, keepdims=True))
    if scatters:
        drain()

    def settle_prods(p, _):
        give(p).wait_recv()
        return 0

    own_prod.wait()
    lax.fori_loop(1, n, settle_prods, 0)
    gate = jnp.sum(jnp.where(picked, chance, 0.0), axis=1, keepdims=True)
    mixed_ref[...] = (middle_ref[...] + gate * dot(hits, returned[...].reshape(total, width))).astype(BF16)
    if scatters:
        drain()

        def settle_bias(p, _):
            bias_arrived(p).wait_recv()
            return 0

        lax.fori_loop(1, n, settle_bias, 0)
        total_bias = bias_in[0]
        for p in range(1, n):
            total_bias = total_bias + bias_in[p]
        bias_grad_ref[...] = total_bias
        for k in range(chunks):
            done = keep[k, :own]
            if k < lead:
                if (k + 1) * part <= width:
                    att_grad_ref[:, k * part : (k + 1) * part] = done
                else:
                    extra_grad_ref[...] = done[:, :256]
            else:
                for c in range(3):
                    start = c * width + (k - lead) * 128
                    qkv_grad_ref[:, start : start + 128] = done[:, c * 128 : (c + 1) * 128]
        total_gain = jnp.sum(qkv_grad_ref[...] * own_ref[...].astype(F32), axis=1, keepdims=True)
        gain_grad_ref[...] = jnp.broadcast_to(total_gain / gain_ref[128:256].T[:own, 0:1], gain_grad_ref.shape)

        def settle_sends(k, _):
            hop(0, k, 0).wait_send()
            for d in (1, 2, 3):
                hop(1, k, d).wait_send()
                hop(2, k, d).wait_send()
            return 0

        lax.fori_loop(0, chunks, settle_sends, 0)

        def settle_bias_sends(p, _):
            bias_hop(p).wait_send()
            return 0

        lax.fori_loop(1, n, settle_bias_sends, 0)
    else:
        bias_grad_ref[...] = bias_sum

    def settle_sent(p, _):
        give(p).wait_send()
        return 0

    lax.fori_loop(1, n, settle_sent, 0)


def backward(n, pad, experts, heads, scatters, routes, gains, hot, own, gain, probs, prods, *sources):
    count, width = routes.shape[1], gains.shape[1]
    buckets = hot.shape[0]
    rows = own.shape[0]
    half = rows * n
    part = 3 * 128
    chunks = (width + 256 + part - 1) // part + heads // 2
    any_ = pl.BlockSpec(memory_space=pl.ANY)
    vmem = pl.BlockSpec(memory_space=pltpu.VMEM)
    dma = pltpu.SemaphoreType.DMA
    small = (1, 8, 128)

    def buffer(shape, kind):
        return pltpu.VMEM(shape if scatters else small, kind)

    return pl.pallas_call(
        functools.partial(backward_kernel, n, pad, experts, heads, scatters),
        out_shape=(
            jax.ShapeDtypeStruct((count, width), BF16),
            jax.ShapeDtypeStruct((count, width), F32),
            jax.ShapeDtypeStruct((rows, 3 * width) if scatters else (chunks, width, part), F32),
            jax.ShapeDtypeStruct((rows, width), F32),
            jax.ShapeDtypeStruct((rows, 256), F32),
            jax.ShapeDtypeStruct((rows, 128), F32),
            jax.ShapeDtypeStruct((heads, buckets), F32),
        ),
        in_specs=[vmem] * 5 + [any_] * (2 + LOADS),
        out_specs=(vmem, vmem, vmem if scatters else any_, vmem, vmem, vmem, vmem),
        scratch_shapes=[
            *[pltpu.VMEM(source.shape, source.dtype) for source in sources],
            pltpu.VMEM((2, 2, count, count), BF16),
            pltpu.VMEM((n, pad, width), BF16),
            pltpu.VMEM((count, width), F32),
            pltpu.VMEM((count, width), BF16),
            pltpu.VMEM((count, 3 * width), BF16),
            pltpu.VMEM((width, count), BF16),
            pltpu.VMEM((width, part), F32),
            pltpu.VMEM((128, 1024), F32),
            pltpu.VMEM((heads, 8, 1024), F32),
            buffer((chunks, half, part), BF16),
            buffer((chunks, half, part), BF16),
            buffer((chunks, half, part), F32),
            buffer((chunks, 3, 4 * rows, part), BF16),
            buffer((chunks, 3, 4 * rows, part), BF16),
            buffer((chunks, 4 * rows, part), F32),
            buffer((chunks, 3, -(-3 * rows // 16) * 16, 128), BF16),
            buffer((chunks, 3, -(-3 * rows // 16) * 16, 128), BF16),
            pltpu.VMEM((heads, buckets), F32),
            pltpu.VMEM((n, heads, buckets), F32),
            pltpu.VMEM((heads, buckets), F32),
            dma((LOADS,)), dma((2,)), dma((n,)), dma((n,)), dma((chunks,)), dma((chunks,)),
            *[dma((chunks, 3)) for _ in range(4)],
            dma((n,)), dma((n,)), dma((3,)),
        ],
        compiler_params=pltpu.CompilerParams(
            collective_id=3, has_side_effects=True, vmem_limit_bytes=62 * 1024 * 1024),
        name="backward",
    )(routes, gains, hot, own, gain, probs, prods, *sources)


def finish_kernel(
    mixed_in, tokens_in, in_hbm, out_hbm, qkv_in, att_in, extra_in, gain_in, bias_in,
    mixed_out, tokens_out, in_out, out_out, qkv_out, att_out, router_out, gain_out, gain_moe_out, bias_out,
    mixed, tokens, narrow, wide, sem, load_sem, store_sem,
):
    ins = [pltpu.make_async_copy(mixed_in, mixed, sem.at[0]), pltpu.make_async_copy(tokens_in, tokens, sem.at[1])]
    outs = [pltpu.make_async_copy(mixed, mixed_out, sem.at[2]), pltpu.make_async_copy(tokens, tokens_out, sem.at[3])]
    parts, rows = narrow.shape[1], narrow.shape[2]

    def load(kind, k):
        return pltpu.make_async_copy(
            (in_hbm, out_hbm)[kind].at[pl.ds(k * rows, rows)], narrow.at[kind, k], load_sem.at[kind, k])

    def store(kind, k):
        return pltpu.make_async_copy(
            wide.at[kind, k], (in_out, out_out)[kind].at[0, pl.ds(k * rows, rows)], store_sem.at[kind, k])

    for k in range(parts):
        for kind in (0, 1):
            load(kind, k).start()
    for copy in ins:
        copy.start()
    qkv_out[...] = qkv_in[...]
    att_out[...] = att_in[...]
    router_out[...] = extra_in[:, :128].T[: router_out.shape[0]]
    gain_out[...] = gain_in[...].T[0:1]
    gain_moe_out[...] = extra_in[:, 128:].T[0:1]
    bias_out[...] = bias_in[...]
    for k in range(parts):
        for kind in (0, 1):
            load(kind, k).wait()
            wide[kind, k] = narrow[kind, k].astype(F32)
            store(kind, k).start()
    for copy_in, copy_out in zip(ins, outs):
        copy_in.wait()
        copy_out.start()
    for k in range(parts):
        for kind in (0, 1):
            store(kind, k).wait()
    for copy in outs:
        copy.wait()


def finish(experts, mixed, tokens_grad, grad_in, grad_out, qkv, att, extra, gain, bias):
    any_ = pl.BlockSpec(memory_space=pl.ANY)
    vmem = pl.BlockSpec(memory_space=pltpu.VMEM)
    dma = pltpu.SemaphoreType.DMA
    parts = 8
    rows = grad_in.shape[0] // parts
    own = qkv.shape[0]
    shape = jax.ShapeDtypeStruct
    return pl.pallas_call(
        finish_kernel,
        out_shape=(
            shape(mixed.shape, BF16), shape(tokens_grad.shape, F32), shape((1, *grad_in.shape), F32),
            shape((1, *grad_out.shape), F32), shape(qkv.shape, F32), shape(att.shape, F32), shape((experts, own), F32),
            shape((1, own), F32), shape((1, own), F32), shape(bias.shape, F32),
        ),
        in_specs=[any_] * 4 + [vmem] * 5,
        out_specs=tuple([any_] * 4 + [vmem] * 6),
        scratch_shapes=[
            pltpu.VMEM(mixed.shape, BF16),
            pltpu.VMEM(tokens_grad.shape, F32),
            pltpu.VMEM((2, parts, rows, grad_in.shape[1]), BF16),
            pltpu.VMEM((2, parts, rows, grad_in.shape[1]), F32),
            dma((4,)), dma((2, parts)), dma((2, parts)),
        ],
        compiler_params=pltpu.CompilerParams(vmem_limit_bytes=60 * 1024 * 1024),
        name="finish",
    )(mixed, tokens_grad, grad_in, grad_out, qkv, att, extra, gain, bias)


def shards(
    n, tokens, cotangent, routes, buckets, gain_attn, w_qkv, w_att, rel_bias, gain_moe, w_router, w_in, w_out,
):
    axes = ("dp", "expert")
    count, width = tokens.shape
    experts = w_router.shape[1]
    heads = rel_bias.shape[1]
    own = w_qkv.shape[0]
    cap = max(2, 2 * count // experts)
    pad = max(16, cap)
    direct = n == 16 and own % 8 == 0
    extra = sum(jnp.pad(part.astype(F32), ((low, 256 - low - part.shape[0]), (0, 128 - own)))
                for low, part in ((0, w_router.T), (128, gain_attn[None]), (129, gain_moe[None])))
    full = w_att if direct else lax.all_gather(
        jnp.concatenate([w_qkv, extra[:, :own].T.astype(BF16), w_att], axis=1), axes, axis=0, tiled=True)
    rows, cots, probs, packed, normed, attended, middle, moe_in, chance, w, gains, hot = forward(
        n, pad, experts, heads, direct, tokens, cotangent, w_qkv, w_att, extra, full, routes.T, rel_bias.T, buckets)
    back, ties, prods, grad_in, grad_out = moe(n, cap, pad, experts, rows, cots, w, w_in[0], w_out[0])
    mixed, grad_tokens, grad_qkv, grad_att, grad_extra, grad_gain, grad_bias = backward(
        n, pad, experts, heads, direct, routes.T, gains, hot, w_qkv, extra, probs, prods,
        back, ties, chance, middle, w, cotangent, attended, moe_in, normed, packed, tokens)
    if not direct:
        lead = grad_qkv.shape[0] - heads // 2
        early = jnp.concatenate([grad_qkv[k] for k in range(lead)], axis=1)
        late = [grad_qkv[lead:, :, c * 128 : (c + 1) * 128].transpose(1, 0, 2).reshape(width, width) for c in range(3)]
        both = lax.psum_scatter(jnp.concatenate([early, *late], axis=1), axes, scatter_dimension=0, tiled=True)
        grad_att, grad_extra = both[:, :width], both[:, width : width + 256]
        grad_qkv = both[:, early.shape[1] :]
        grad_gain = jnp.sum(grad_qkv * w_qkv.astype(F32), axis=1, keepdims=True) / gain_attn.astype(F32)[:, None]
        grad_gain = jnp.broadcast_to(grad_gain, (own, 128))
        grad_bias = lax.psum(grad_bias, axes)
    mixed, grad_tokens, grad_in, grad_out, grad_qkv, grad_att, grad_router, grad_gain, grad_gain_moe, grad_bias = finish(
        experts, mixed, grad_tokens, grad_in, grad_out, grad_qkv, grad_att, grad_extra, grad_gain, grad_bias)
    return (
        mixed, grad_tokens, grad_gain.reshape(own), grad_qkv, grad_att, grad_bias.T, grad_gain_moe.reshape(own), grad_router.T,
        grad_in, grad_out,
    )


def solution(mesh):
    both = P(("dp", "expert"))
    return jax.shard_map(
        functools.partial(shards, mesh.shape["expert"]),
        mesh=mesh,
        in_specs=(both, both, both, P(), both, both, both, P(), both, both, P("expert"), P("expert")),
        out_specs=(both, both, both, both, both, P(), both, both, P("expert", None, "dp"), P("expert", None, "dp")),
        check_vma=False,
    )
```

```python
import functools
import jax
import jax.numpy as jnp
from jax import lax
from jax.experimental import pallas as pl
from jax.experimental.pallas import tpu as pltpu
from jax.sharding import PartitionSpec as P

MESH = pl.DeviceIdType.MESH
F32, BF16 = jnp.float32, jnp.bfloat16
NT = (((1,), (1,)), ((), ()))
EPSILON = 1e-06
PART = 384
WIDE = 768
LAG = (0, 1, 4, 99)


def dot(a, b, dims=(((1,), (0,)), ((), ()))):
    return lax.dot_general(a, b, dims, preferred_element_type=F32)


def exact(a, b, dims=(((1,), (0,)), ((), ()))):
    return lax.dot_general(a, b, dims, preferred_element_type=F32, precision=lax.Precision.HIGHEST)


def flipped(index, bits, count):
    result, bit = 0, 1
    while bit < count:
        result = result + bit * (((index // bit) % 2 + (bits // bit) % 2) % 2)
        bit *= 2
    return result


def gelu_parts(hidden):
    c0, c1 = 0.7978845608028654, 0.044715
    square = hidden * hidden
    bend = jnp.tanh(hidden * (c0 + (c0 * c1) * square))
    half = 0.5 + 0.5 * bend
    slope = half + (0.5 * hidden) * (1.0 - bend * bend) * (c0 + (3.0 * c0 * c1) * square)
    return hidden * half, slope


def slots_by_row(routes, me, pad, experts):
    count = routes.shape[1]
    picked = routes == lax.broadcasted_iota(jnp.int32, (experts, count), 0)
    first = lax.broadcasted_iota(jnp.int32, (count, count), 0)
    second = lax.broadcasted_iota(jnp.int32, (count, count), 1)
    before = dot(picked.astype(BF16), (first < second).astype(BF16))
    rank = jnp.sum(jnp.where(picked, before, 0.0), axis=0, keepdims=True).astype(jnp.int32)
    return jnp.bitwise_xor(routes, me) * pad + rank


def grow_strip(strip, w8):
    strip[0:8] = w8
    have = 8
    while have < strip.shape[0]:
        strip[have : 2 * have] = pltpu.roll(strip[0:have], have, 1)
        have *= 2


SPILLS = 7


def layer_kernel(n, cap, pad, experts, heads, direct, *refs):
    (tokens_ref, cot_ref, qkv_ref, att_ref, extra_ref, full_hbm, routes_ref, table_ref, buckets_hbm, win_hbm, wout_hbm,
     mixed_hbm, tokens_grad_hbm, qkv_grad_ref, att_grad_ref, extra_grad_ref, gain_grad_ref, bias_grad_ref,
     gin_hbm, gout_hbm, probs_hbm, *rest) = refs
    spilled, rest = rest[:SPILLS], rest[SPILLS:]
    (blocks, shard, gains, hot, router, rows, cots, ties, xin, cin, back_in, returned, tie_in, sib_recv,
     sib_in, in1, in2, bias_out, bias_in, bias_pair,
     put_sem, prob_sem, load_sem, pair_sem, swap_send, swap_recv, tree_send, tree_recv, turn_send, turn_recv,
     piece_send, piece_recv, piece_out, sib_s, sib_r, s1, r1, s2, r2, bias_s, bias_r, end_sem) = rest
    dp, me = lax.axis_index("dp"), lax.axis_index("expert")
    count, width = tokens_ref.shape
    total = n * pad
    early = 3 * width + 256
    sibling = (1 - dp, me)
    lane = lax.broadcasted_iota(jnp.int32, (count, 128), 1)

    def peer(p):
        return dp, flipped(me, p, n)

    def remote(src, dst, send, recv, device):
        return pltpu.make_async_remote_copy(
            src_ref=src, dst_ref=dst, send_sem=send, recv_sem=recv, device_id=device, device_id_type=MESH)

    def swap(kind, p):
        src, dst = ((rows, xin), (cots, cin), (rows, back_in), (cots, returned), (ties, tie_in))[kind]
        return remote(src.at[p], dst.at[p], swap_send.at[kind, p], swap_recv.at[kind, p], peer(p))

    def start_swaps(kind, wanted):
        def one(p, _):
            @pl.when(wanted(p))
            def _():
                swap(kind, p).start()
            return 0

        lax.fori_loop(1, n, one, 0)

    def greet_all():
        barrier = pltpu.get_barrier_semaphore()

        def greet(p, _):
            pl.semaphore_signal(barrier, inc=1, device_id=peer(p), device_id_type=MESH)
            return 0

        lax.fori_loop(1, n, greet, 0)
        pl.semaphore_signal(barrier, inc=1, device_id=sibling, device_id_type=MESH)
        pl.semaphore_wait(barrier, n)

    half = win_hbm.shape[1] // 2
    steps = half // WIDE
    pieces = [(kind, k) for k in range(steps) for kind in (0, 1)]

    def piece(kind, k):
        place = pl.ds((kind * steps + k) * WIDE, WIDE)
        return remote(blocks.at[:, place], sib_recv.at[kind, k], piece_send.at[kind, k], piece_recv.at[kind, k], sibling)

    def out_piece(kind, k):
        return pltpu.make_async_copy(
            sib_recv.at[kind, k], (gin_hbm, gout_hbm)[kind].at[:, pl.ds(k * WIDE, WIDE)], piece_out.at[kind, k])

    def forward(w, packed, normed, attended, middle, moe_in, chance, probs, strip, bias, ends, weights):
        puts = []

        def put(index, src):
            copy = pltpu.make_async_copy(src, spilled[index], put_sem.at[index])
            copy.start()
            puts.append(copy)

        offsets = [pltpu.make_async_copy(buckets_hbm.at[:, pl.ds(c, 128)], ends.at[i], load_sem.at[i])
                   for i, c in enumerate((0, count - 128))]
        for copy in offsets:
            copy.start()
        if direct:
            weights[:, : 3 * width] = qkv_ref[...].astype(F32)
            weights[:, 3 * width : early] = extra_ref[...].T[: weights.shape[0]]
            weights[:, early:] = att_ref[...].astype(F32)
        greet_all()
        if direct:
            own = weights.shape[0]
            block = 2 * own
            pair = remote(weights, shard, pair_sem.at[0], pair_sem.at[1], sibling)
            pair.start()
        else:
            load = pltpu.make_async_copy(full_hbm, w, pair_sem.at[0])
            load.start()
        slots = slots_by_row(routes_ref[...], me, pad, experts)

        def to_slots(values):
            hits = (slots == lax.broadcasted_iota(jnp.int32, (total, count), 0)).astype(BF16)
            return dot(hits, values).astype(BF16).reshape(n, pad, width)

        def make_cots():
            cots[...] = to_slots(cot_ref[...])
            cin[0] = cots[0]

        def make_bias():
            for copy in offsets:
                copy.wait()
            last, first = ends[1].astype(F32).T[127:128], ends[0].astype(F32).T[0:1]
            line = jnp.concatenate([last, pltpu.roll(first, count - 1, 1)], axis=1)
            line = pltpu.roll(jnp.broadcast_to(line, (8, 2 * count)), 2 * count - 127, 1)[0:1]
            hot[...] = (line.astype(jnp.int32) == lax.broadcasted_iota(jnp.int32, hot.shape, 0)).astype(F32)
            table = exact(table_ref[...], hot[...])
            for h in range(heads):
                row = jnp.broadcast_to(table[h : h + 1], (8, 2 * count))
                place = lax.broadcasted_iota(jnp.int32, row.shape, 0)
                shifted = row
                for r in range(1, 8):
                    shifted = jnp.where(place == r, pltpu.roll(row, r, 1), shifted)
                bias[h] = shifted

        if direct:
            pair.wait()
            mine, other = weights[...], shard[...]
            blocks[pl.ds(pl.multiple_of(me * block, 16), block), : w.shape[1]] = jnp.concatenate(
                [jnp.where(dp == 0, mine, other), jnp.where(dp == 0, other, mine)], axis=0).astype(BF16)
            second, third = 2 - dp, 1 + dp
            far = list(range(4, n, 4))
            near = [0] + far

            def at(t, r, core):
                start, size = ((0, early // 2), (early, width // 2))[t]
                return blocks.at[pl.ds(pl.multiple_of(flipped(me, r, n) * block, 16), block),
                                 pl.ds(pl.multiple_of(start + core * size, 128), size)]

            def hop(t, r, step):
                return remote(at(t, r, dp), at(t, r, dp), tree_send.at[t, r + step], tree_recv.at[t, r + step], peer(step))

            def arrived(t, r):
                remote(at(t, r, dp), at(t, r, dp), tree_send.at[t, r], tree_recv.at[t, r], peer(r)).wait_recv()

            def to_sibling(t, r, core):
                return remote(at(t, r, core), at(t, r, core), turn_send.at[t, r], turn_recv.at[t, r], sibling)

            def turn(t, step):
                if step == 0:
                    for r in far:
                        hop(t, 0, r).start()
                    hop(t, 0, third).start()
                    hop(t, 0, second).start()
                elif step == 1:
                    for r in far:
                        arrived(t, r)
                        hop(t, r, third).start()
                        hop(t, r, second).start()
                        to_sibling(t, r, dp).start()
                elif step == 2:
                    for r in near:
                        arrived(t, r + second)
                        hop(t, r + second, third).start()
                        to_sibling(t, r + second, dp).start()
                elif step == 3:
                    for r in near:
                        arrived(t, r + third)
                        to_sibling(t, r + third, dp).start()
                        arrived(t, r + 3)
                        to_sibling(t, r + 3, dp).start()
                else:
                    def settle(r, _):
                        to_sibling(t, r, 1 - dp).wait_recv()
                        return 0

                    lax.fori_loop(1, n, settle, 0)
                    place = (slice(0, early), slice(early, w.shape[1]))[t]
                    for core in (0, 1):
                        for q in range(n // 2):
                            low = 2 * q * block + core * own
                            pair_rows = [blocks[p : p + own, place].astype(F32) for p in (low, low + block)]
                            w[core * own * n + q * block : core * own * n + (q + 1) * block, place] = jnp.concatenate(
                                pair_rows, axis=0).astype(BF16)

            turn(0, 0)
            make_bias()
            make_cots()
            turn(0, 1)
            turn(1, 0)
            start_swaps(1, lambda p: p % 4 == 0)
            turn(0, 2)
            turn(1, 1)
            turn(0, 3)
            turn(1, 2)
            start_swaps(1, lambda p: p % 4 != 0)
            turn(0, 4)
        else:
            make_bias()
            make_cots()
            start_swaps(1, lambda p: p > 0)
            load.wait()
        gains[...] = w[:, 3 * width + 128 : early].astype(F32).T[0:8]
        router[...] = w[:, 3 * width : 3 * width + 128]
        x = tokens_ref[...].astype(F32)
        normed[...] = (x * lax.rsqrt(jnp.mean(x * x, axis=1, keepdims=True) + EPSILON) * gains[0:1]).astype(BF16)
        put(0, normed)
        for c in range(3):
            cols_c = slice(c * width, (c + 1) * width)
            packed[:, cols_c] = dot(normed[...], w[:, cols_c]).astype(BF16)
        put(1, packed)
        scale = (width // heads) ** -0.5

        def put_probs(k):
            return pltpu.make_async_copy(probs.at[pl.ds(2 * k, 2)], probs_hbm.at[pl.ds(2 * k, 2)], prob_sem.at[k])

        def attend(k, _):
            def part(c):
                return packed[:, pl.ds(pl.multiple_of(c * width + k * 128, 128), 128)]

            queries = (part(0).astype(F32) * scale).astype(BF16)
            keys = part(1)
            values = part(2).astype(F32).T.astype(BF16)
            outs = []
            for h in (0, 1):
                grow_strip(strip, bias[2 * k + h])
                own_keys = jnp.where((lane < 64) == (h == 0), keys, jnp.zeros_like(keys))
                scores = dot(own_keys, queries, NT)
                scores = jnp.concatenate(
                    [scores[128 * b : 128 * b + 128] + strip[:, 384 - 128 * b : 896 - 128 * b] for b in range(4)], axis=0)
                powers = jnp.exp(scores - jnp.max(scores, axis=0, keepdims=True))
                part_weights = (powers * (1.0 / jnp.sum(powers, axis=0, keepdims=True))).astype(BF16)
                probs[2 * k + h] = part_weights
                outs.append(dot(values[64 * h : 64 * h + 64], part_weights))
            put_probs(k).start()
            attended[:, pl.ds(pl.multiple_of(k * 128, 128), 128)] = jnp.concatenate(outs, axis=0).T.astype(BF16)
            if direct:
                for step in (3, 4):
                    @pl.when(k == step + 1)
                    def _():
                        turn(1, step)
            return 0

        lax.fori_loop(0, heads // 2, attend, 0)
        mid = tokens_ref[...].astype(F32) + dot(attended[...], w[:, early:])
        middle[...] = mid
        moe = (mid * lax.rsqrt(jnp.mean(mid * mid, axis=1, keepdims=True) + EPSILON) * gains[1:2]).astype(BF16)
        moe_in[...] = moe
        rows[...] = to_slots(moe)
        start_swaps(0, lambda p: (p < 4) | ((p % 4 == 0) & (p < 12)))
        xin[0] = rows[0]
        put(2, attended)
        put(3, middle)
        put(4, moe_in)
        put(5, w)
        logits = dot(moe, router[...])
        logits = jnp.where(lane < experts, logits, -1e30)
        powers = jnp.exp(logits - jnp.max(logits, axis=1, keepdims=True))
        chance[...] = powers / jnp.sum(powers, axis=1, keepdims=True)
        put(6, chance)
        if direct:
            for t in (0, 1):
                for r in far:
                    hop(t, 0, r).wait_send()
                for r in near:
                    hop(t, r, second).wait_send()
                    hop(t, r, third).wait_send()
                    hop(t, r + second, third).wait_send()

                def settle_sends(r, _):
                    to_sibling(t, r, dp).wait_send()
                    return 0

                lax.fori_loop(1, n, settle_sends, 0)
        for copy in puts:
            copy.wait()
        for k in range(heads // 2):
            put_probs(k).wait()

    def experts_both(win, wout, xt, rt, act, hgr):
        ff = win.shape[1]
        per = 256 // cap
        group_rows = per * cap
        chunk = 1024
        loads = [pltpu.make_async_copy(win_hbm, win, load_sem.at[0]), pltpu.make_async_copy(wout_hbm, wout, load_sem.at[1])]
        for load in loads:
            load.start()

        def packed_rows(ref, g):
            block = ref[pl.ds(g * per, per)].reshape(per * pad, width)
            if pad == cap:
                return block
            r = lax.broadcasted_iota(jnp.int32, (group_rows, per * pad), 0)
            c = lax.broadcasted_iota(jnp.int32, (group_rows, per * pad), 1)
            return dot(((r // cap) * pad + r % cap == c).astype(BF16), block).astype(BF16)

        def spread_rows(block):
            if pad == cap:
                return block.reshape(per, pad, width)
            r = lax.broadcasted_iota(jnp.int32, (per * pad, group_rows), 0)
            c = lax.broadcasted_iota(jnp.int32, (per * pad, group_rows), 1)
            pick = (r // pad == c // cap) & (r % pad == c % cap)
            return dot(pick.astype(BF16), block).astype(BF16).reshape(per, pad, width)

        def group(g, _):
            def over(first, act_on):
                def one(j, _):
                    @pl.when(g * per + j != 0)
                    def _():
                        act_on(g * per + j)
                    return 0

                lax.fori_loop(first, per, one, 0)

            @pl.when(g == 0)
            def _():
                for p in (1, 2, 3):
                    swap(0, p).wait_recv()
                start_swaps(0, lambda p: (p >= 4) & (p % 4 != 0) & (p < 12))
                for load in loads:
                    load.wait()
                over(4, lambda p: swap(0, p).wait_recv())

            @pl.when(g != 0)
            def _():
                over(0, lambda p: swap(0, p).wait_recv())

            @pl.when(g == 1)
            def _():
                start_swaps(0, lambda p: p >= 12)

            over(0, lambda p: swap(1, p).wait_recv())
            here = pl.ds(pl.multiple_of(g * group_rows, group_rows), group_rows)
            x = packed_rows(xin, g)
            logits = dot(x, router[...])
            lanes = lax.broadcasted_iota(jnp.int32, logits.shape, 1)
            logits = jnp.where(lanes < experts, logits, -1e30)
            powers = jnp.exp(logits - jnp.max(logits, axis=1, keepdims=True))
            gate = jnp.sum(jnp.where(lanes == me, powers, 0.0), axis=1, keepdims=True) / jnp.sum(
                powers, axis=1, keepdims=True)
            r = (gate * packed_rows(cin, g).astype(F32)).astype(BF16)
            xt[:, here] = x.T
            rt[:, here] = r.T

            def hidden_chunk(k, _):
                cols = pl.ds(pl.multiple_of(k * chunk, chunk), chunk)
                value, slope = gelu_parts(dot(x, win[:, cols]))
                act[here, cols] = value.astype(BF16)
                hgr[here, cols] = (dot(r, wout[:, cols]) * slope).astype(BF16)
                return 0

            lax.fori_loop(0, ff // chunk, hidden_chunk, 0)
            back = spread_rows(dot(hgr[here], win[...], NT).astype(BF16))
            over(0, lambda p: swap(0, p).wait_send())
            rows[pl.ds(g * per, per)] = back
            over(0, lambda p: swap(2, p).start())
            produced = dot(act[here], wout[...], NT).astype(BF16)
            tie = jnp.sum(r.astype(F32) * produced.astype(F32), axis=1, keepdims=True)
            for j in range(per):
                row = jnp.broadcast_to(tie[j * cap : (j + 1) * cap], (cap, 128)).T[0:8]
                ties[g * per + j] = jnp.concatenate([row, jnp.zeros((8, 128 - cap), F32)], axis=1)
            over(0, lambda p: swap(4, p).start())
            over(0, lambda p: swap(1, p).wait_send())
            cots[pl.ds(g * per, per)] = spread_rows(produced)

            @pl.when(g < n // per // 2)
            def _():
                over(0, lambda p: swap(3, p).start())

            return 0

        lax.fori_loop(0, n // per, group, 0)
        back_in[0] = rows[0]
        tie_in[0] = ties[0]
        returned[0] = cots[0]

        def partial(kind, owner, k):
            cols = pl.ds(pl.multiple_of(owner * half + k * WIDE, 128), WIDE)
            return dot(xt[...], hgr[:, cols]) if kind == 0 else dot(rt[...], act[:, cols])

        for kind, k in pieces:
            place = (kind * steps + k) * WIDE
            blocks[:, place : place + WIDE] = partial(kind, 1 - dp, k).astype(BF16)
            piece(kind, k).start()
        for kind, k in pieces:
            value = partial(kind, dp, k)
            piece(kind, k).wait_recv()
            sib_recv[kind, k] = (value + sib_recv[kind, k].astype(F32)).astype(BF16)
            out_piece(kind, k).start()

    def backward(w, packed, normed, attended, middle, moe_in, chance, prob, mid_grad, att_cot, packed_grad, normed_t, chunk,
                 strip, bias_rows, sib_out, mine, out1, keep, out2):
        loaded = (normed, packed, attended, middle, moe_in, w, chance)
        loads = [pltpu.make_async_copy(spilled[i], loaded[i], load_sem.at[i]) for i in range(SPILLS)]
        order = (6, 3, 5, 2, 4, 0, 1)
        for i in order:
            loads[i].start()

        def fetch(k):
            return pltpu.make_async_copy(probs_hbm.at[pl.ds(2 * k, 2)], prob.at[k % 2], prob_sem.at[k % 2])

        fetch(0).start()
        own = qkv_ref.shape[0]
        lead = (width + 256 + PART - 1) // PART
        chunks = lead + heads // 2

        if direct:
            half_rows = own * n

            def hop(stage, k, d):
                if stage == 0:
                    return remote(sib_out.at[k], sib_in.at[k], sib_s.at[k], sib_r.at[k], sibling)
                if stage == 1:
                    return remote(out1.at[k, d - 1], in1.at[k, d - 1], s1.at[k, d - 1], r1.at[k, d - 1], peer(d))
                return remote(out2.at[k, d - 1], in2.at[k, d - 1], s2.at[k, d - 1], r2.at[k, d - 1], peer(4 * d))

            def owners(k, d):
                places = [pl.multiple_of(flipped(me, d + 4 * z, n) * own, 8) for z in range(4)]
                return jnp.concatenate([mine[k % 2, pl.ds(place, own)] for place in places], axis=0)

            def stage(s, k):
                if s == 0:
                    there = pl.ds(pl.multiple_of((1 - dp) * half_rows, 8), half_rows)
                    here = pl.ds(pl.multiple_of(dp * half_rows, 8), half_rows)
                    sib_out[k] = chunk[there].astype(BF16)
                    hop(0, k, 0).start()
                    mine[k % 2] = chunk[here]
                elif s == 1:
                    hop(0, k, 0).wait_recv()
                    mine[k % 2] = mine[k % 2] + sib_in[k].astype(F32)
                    for d in (3, 1, 2):
                        out1[k, d - 1] = owners(k, d).astype(BF16)
                        hop(1, k, d).start()
                    keep[k] = owners(k, 0)
                elif s == 2:
                    for d in (1, 2, 3):
                        hop(1, k, d).wait_recv()
                    total_rows = keep[k] + (in1[k, 0].astype(F32) + in1[k, 1].astype(F32)) + in1[k, 2].astype(F32)
                    for z in (3, 2, 1):
                        block = total_rows[own * z : own * (z + 1)]
                        out2[k, z - 1] = jnp.concatenate(
                            [block[:, 128 * c : 128 * (c + 1)] for c in range(3)]
                            + [jnp.zeros((out2.shape[2] - 3 * own, 128), F32)], axis=0).astype(BF16)
                        hop(2, k, z).start()
                    keep[k, :own] = total_rows[:own]
                else:
                    for z in (1, 2, 3):
                        hop(2, k, z).wait_recv()
                    far = (in2[k, 0].astype(F32) + in2[k, 1].astype(F32)) + in2[k, 2].astype(F32)
                    keep[k, :own] = keep[k, :own] + jnp.concatenate(
                        [far[own * c : own * (c + 1)] for c in range(3)], axis=1)

            def advance(k):
                stage(0, k)
                for s in range(1, 4):
                    @pl.when((k - LAG[s] >= 0) & (k - LAG[s] < chunks))
                    def _():
                        stage(s, k - LAG[s])

            done = {k: max(s for s in range(4) if LAG[s] <= chunks - 1 - k) for k in range(chunks)}

            def drain(last, *which):
                for k in which or range(chunks):
                    while done[k] < last:
                        done[k] += 1
                        stage(done[k], k)

        else:
            def advance(k):
                copy = pltpu.make_async_copy(chunk, qkv_grad_ref.at[k], end_sem.at[0])
                copy.start()
                copy.wait()

            def drain(*_):
                pass

        expert_of = jnp.broadcast_to(routes_ref[...].astype(F32), (128, count)).T[:, 0:1].astype(jnp.int32)
        picked = expert_of == lane
        first = lax.broadcasted_iota(jnp.int32, (count, count), 0)
        other = lax.broadcasted_iota(jnp.int32, (count, count), 1)
        before = dot((other < first).astype(BF16), picked.astype(BF16))
        rank = jnp.sum(jnp.where(picked, before, 0.0), axis=1, keepdims=True).astype(jnp.int32)
        place = jnp.bitwise_xor(expert_of, me)
        hits = (place * pad + rank == lax.broadcasted_iota(jnp.int32, (count, total), 1)).astype(BF16)

        def each_peer(act_on):
            def one(p, _):
                act_on(p)
                return 0

            lax.fori_loop(1, n, one, 0)

        def arrive(p):
            swap(2, p).wait_recv()
            swap(4, p).wait_recv()

        each_peer(arrive)
        ties_row = exact((place == lax.broadcasted_iota(jnp.int32, (count, n), 1)).astype(F32), jnp.max(tie_in[...], axis=1))
        tie = jnp.sum(jnp.where(lane == rank, ties_row, 0.0), axis=1, keepdims=True)
        for i in order[:1]:
            loads[i].wait()
        logit_grad = (tie * (picked.astype(F32) - chance[...])).astype(BF16)
        grad = dot(hits, back_in[...].reshape(total, width))
        for i in order[1:]:
            loads[i].wait()
        grad = grad + dot(logit_grad, router[...], NT)
        mid = middle[...]
        root = lax.rsqrt(jnp.mean(mid * mid, axis=1, keepdims=True) + EPSILON)
        unit_mid = mid * root
        gain_rows = jnp.sum(grad * unit_mid, axis=0, keepdims=True)
        scaled = grad * gains[1:2]
        mid_g = cot_ref[...].astype(F32) + root * (scaled - unit_mid * jnp.mean(scaled * unit_mid, axis=1, keepdims=True))
        mid_grad[...] = mid_g
        attn_grad = mid_g.astype(BF16)
        att_cot[...] = dot(attn_grad, w[:, early:], NT).astype(BF16)
        attended_t = attended[...].T
        for k in range(lead):
            if (k + 1) * PART <= width:
                chunk[...] = dot(attended_t, attn_grad[:, k * PART : (k + 1) * PART])
            else:
                chunk[:, 0:128] = dot(moe_in[...].T, logit_grad)
                chunk[:, 128:256] = jnp.broadcast_to(gain_rows, (128, width)).T
                chunk[:, 256:] = jnp.zeros((width, PART - 256), F32)
            advance(k)
        normed_t[...] = normed[...].T
        each_peer(lambda p: swap(2, p).wait_send())
        start_swaps(3, lambda p: p >= n // 2)

        scale = (width // heads) ** -0.5

        def attend_back(k, _):
            fetch(k).wait()

            @pl.when(k + 1 < heads // 2)
            def _():
                fetch(k + 1).start()

            def part(c):
                return packed[:, pl.ds(pl.multiple_of(c * width + k * 128, 128), 128)]

            queries, keys, values = part(0), part(1), part(2)
            keys_t = (keys.astype(F32) * scale).T.astype(BF16)
            cot = att_cot[:, pl.ds(pl.multiple_of(k * 128, 128), 128)]
            query_t, key_g, value_g = [], None, None
            for h in (0, 1):
                mask = (lane < 64) == (h == 0)
                own_cot = jnp.where(mask, cot, jnp.zeros_like(cot))
                own_queries = jnp.where(mask, queries, jnp.zeros_like(queries))
                weights = prob[k % 2, h]
                chances = weights.astype(F32)
                product = chances * dot(values, own_cot, NT)
                score_grad = (product - chances * jnp.sum(product, axis=0, keepdims=True)).astype(BF16)
                wide = score_grad.astype(F32)
                for b in range(4):
                    block = wide[128 * b : 128 * b + 128]
                    cols = slice(384 - 128 * b, 896 - 128 * b)
                    if b == 0:
                        strip[:, cols] = block
                        strip[:, 0:384] = jnp.zeros((128, 384), F32)
                        strip[:, 896:1024] = jnp.zeros((128, 128), F32)
                    else:
                        strip[:, cols] += block
                have = 64
                folded = strip[...]
                while have >= 8:
                    folded = folded[:have] + pltpu.roll(folded[have:], 1024 - have, 1)
                    have //= 2
                for s in range(1, 8):
                    folded = jnp.where(lax.broadcasted_iota(jnp.int32, folded.shape, 0) == s,
                                       pltpu.roll(folded, 1024 - s, 1), folded)
                bias_rows[2 * k + h] = folded
                v = dot(weights, own_cot)
                q = dot(score_grad, own_queries)
                value_g = v if h == 0 else value_g + v
                key_g = q if h == 0 else key_g + q
                query_t.append(dot(keys_t[64 * h : 64 * h + 64], score_grad))
            query_g = jnp.concatenate(query_t, axis=0).T.astype(BF16)
            grads = jnp.concatenate([query_g, (key_g * scale).astype(BF16), value_g.astype(BF16)], axis=1)
            for c in range(3):
                packed_grad[:, pl.ds(pl.multiple_of(c * width + k * 128, 128), 128)] = grads[:, c * 128 : (c + 1) * 128]
            chunk[...] = dot(normed_t[...], grads)
            advance(k + lead)
            return 0

        lax.fori_loop(0, heads // 2, attend_back, 0)
        drain(1, chunks - 1)
        drain(2, *range(chunks - 1))
        sums = jnp.concatenate([jnp.sum(bias_rows[h], axis=0, keepdims=True) for h in range(heads)], axis=0)
        bias_out[...] = exact(sums, hot[...], NT)
        if direct:
            pair_hop = remote(bias_out, bias_pair, pair_sem.at[2], pair_sem.at[3], sibling)
            pair_hop.start()

            def bias_hop(p):
                return remote(bias_in.at[me], bias_in.at[me], bias_s.at[p], bias_r.at[p], peer(p))

            def bias_arrived(p):
                there = flipped(me, p, n)
                return remote(bias_in.at[there], bias_in.at[there], bias_s.at[p], bias_r.at[p], (dp, there))

        normed_grad = dot(packed_grad[...], w[:, : 3 * width], NT)
        drain(2)
        if direct:
            pair_hop.wait()
            bias_in[me] = bias_out[...] + bias_pair[...]
            each_peer(lambda p: bias_hop(p).start())
        x = tokens_ref[...].astype(F32)
        root = lax.rsqrt(jnp.mean(x * x, axis=1, keepdims=True) + EPSILON)
        unit_x = x * root
        scaled = normed_grad * gains[0:1]
        mid_grad[...] = mid_grad[...] + root * (scaled - unit_x * jnp.mean(scaled * unit_x, axis=1, keepdims=True))
        ends = [pltpu.make_async_copy(mid_grad, tokens_grad_hbm, end_sem.at[0]),
                pltpu.make_async_copy(att_cot, mixed_hbm, end_sem.at[1])]
        ends[0].start()
        each_peer(lambda p: swap(3, p).wait_recv())
        gate = jnp.sum(jnp.where(picked, chance[...], 0.0), axis=1, keepdims=True)
        att_cot[...] = (middle[...] + gate * dot(hits, returned[...].reshape(total, width))).astype(BF16)
        ends[1].start()
        if direct:
            drain(3)
            each_peer(lambda p: bias_arrived(p).wait_recv())
            total_bias = bias_in[0]
            for p in range(1, n):
                total_bias = total_bias + bias_in[p]
            bias_grad_ref[...] = total_bias
            for k in range(chunks):
                result = keep[k, :own]
                if k >= lead:
                    for c in range(3):
                        start = c * width + (k - lead) * 128
                        qkv_grad_ref[:, start : start + 128] = result[:, c * 128 : (c + 1) * 128]
                elif (k + 1) * PART <= width:
                    att_grad_ref[:, k * PART : (k + 1) * PART] = result
                else:
                    extra_grad_ref[...] = result[:, :256]
            total_gain = jnp.sum(qkv_grad_ref[...] * qkv_ref[...].astype(F32), axis=1, keepdims=True)
            gain_grad_ref[...] = jnp.broadcast_to(total_gain / extra_ref[128:256].T[:own, 0:1], gain_grad_ref.shape)

            def settle_sends(k, _):
                hop(0, k, 0).wait_send()
                for d in (1, 2, 3):
                    hop(1, k, d).wait_send()
                    hop(2, k, d).wait_send()
                return 0

            lax.fori_loop(0, chunks, settle_sends, 0)
            each_peer(lambda p: bias_hop(p).wait_send())
        else:
            bias_grad_ref[...] = bias_out[...]
        for kind in (3, 4):
            each_peer(lambda p: swap(kind, p).wait_send())
        for copy in ends:
            copy.wait()
        for kind, k in pieces:
            piece(kind, k).wait_send()
            out_piece(kind, k).wait()

    wide = w_columns(width)
    scratch = pltpu.VMEM
    shared = [
        scratch((width, wide), BF16), scratch((count, 3 * width), BF16), scratch((count, width), BF16),
        scratch((count, width), BF16), scratch((count, width), F32), scratch((count, width), BF16), scratch((count, 128), F32),
    ]
    own_rows = qkv_ref.shape[0]
    pl.run_scoped(
        forward, *shared, scratch((heads, count, count), BF16), scratch((128, 2 * count), F32),
        scratch((heads, 8, 2 * count), F32), scratch((2, count, 128), jnp.int32),
        scratch((own_rows, wide) if direct else (8, 128), F32))
    pl.run_scoped(
        experts_both, *[scratch((width, win_hbm.shape[1]), BF16) for _ in range(2)],
        *[scratch((width, n * cap), BF16) for _ in range(2)], *[scratch((n * cap, win_hbm.shape[1]), BF16) for _ in range(2)])
    all_chunks = (width + 256 + PART - 1) // PART + heads // 2

    def buffer(shape, kind):
        return scratch((all_chunks, *shape) if direct else (8, 128), kind)

    pl.run_scoped(
        backward, *shared, scratch((2, 2, count, count), BF16), scratch((count, width), F32), scratch((count, width), BF16),
        scratch((count, 3 * width), BF16), scratch((width, count), BF16), scratch((width, PART), F32),
        scratch((128, 2 * count), F32), scratch((heads, 8, 2 * count), F32),
        buffer((own_rows * n, PART), BF16), scratch((2, own_rows * n, PART), F32), buffer((3, 4 * own_rows, PART), BF16),
        buffer((4 * own_rows, PART), F32), buffer((3, -(-3 * own_rows // 16) * 16, 128), BF16))


def w_columns(width):
    return 4 * width + 256


def layer(n, cap, pad, experts, heads, direct, tokens, cotangent, qkv, att, extra, full, routes, table, buckets, win, wout):
    count, width = tokens.shape
    wide = w_columns(width)
    own = qkv.shape[0]
    kinds = table.shape[1]
    ff = win.shape[1]
    chunks = (width + 256 + PART - 1) // PART + heads // 2
    steps = ff // 2 // WIDE
    short = -(-3 * own // 16) * 16
    any_ = pl.BlockSpec(memory_space=pl.ANY)
    vmem = pl.BlockSpec(memory_space=pltpu.VMEM)
    dma = pltpu.SemaphoreType.DMA
    scratch = pltpu.VMEM
    shape = jax.ShapeDtypeStruct

    def landing(*rest):
        return scratch((chunks, *rest) if direct else (16, 128), BF16)

    outs = [
        (shape((count, width), BF16), any_), (shape((count, width), F32), any_),
        (shape((own, 3 * width), F32), vmem) if direct else (shape((chunks, width, PART), F32), any_),
        (shape((own, width), F32), vmem), (shape((own, 256), F32), vmem), (shape((own, 128), F32), vmem),
        (shape((heads, kinds), F32), vmem), (shape((width, ff // 2), BF16), any_), (shape((width, ff // 2), BF16), any_),
        (shape((heads, count, count), BF16), any_), (shape((count, width), BF16), any_),
        (shape((count, 3 * width), BF16), any_), (shape((count, width), BF16), any_), (shape((count, width), F32), any_),
        (shape((count, width), BF16), any_), (shape((width, wide), BF16), any_), (shape((count, 128), F32), any_),
    ]
    slots = scratch((n, pad, width), BF16)
    return pl.pallas_call(
        functools.partial(layer_kernel, n, cap, pad, experts, heads, direct),
        out_shape=tuple(o[0] for o in outs),
        in_specs=[vmem] * 5 + [any_, vmem, vmem, any_, any_, any_],
        out_specs=tuple(o[1] for o in outs),
        scratch_shapes=[
            scratch((width, max(wide, 2 * steps * WIDE)), BF16),
            scratch((own, wide) if direct else (8, 128), F32),
            scratch((8, width), F32), scratch((kinds, 2 * count), F32), scratch((width, 128), BF16),
            slots, slots, scratch((n, 8, 128), F32), slots, slots, slots, slots, scratch((n, 8, 128), F32),
            scratch((2, steps, width, WIDE), BF16),
            landing(own * n, PART), landing(3, 4 * own, PART), landing(3, short, 128),
            scratch((heads, kinds), F32), scratch((n, heads, kinds), F32), scratch((heads, kinds), F32),
            dma((SPILLS,)), dma((heads // 2,)), dma((SPILLS,)), dma((4,)), dma((5, n)), dma((5, n)),
            dma((2, n)), dma((2, n)), dma((2, n)), dma((2, n)),
            dma((2, steps)), dma((2, steps)), dma((2, steps)),
            dma((chunks,)), dma((chunks,)), *[dma((chunks, 3)) for _ in range(4)], dma((n,)), dma((n,)), dma((2,)),
        ],
        compiler_params=pltpu.CompilerParams(
            collective_id=1, has_side_effects=True, vmem_limit_bytes=63 * 1024 * 1024),
        name="layer",
    )(tokens, cotangent, qkv, att, extra, full, routes, table, buckets, win, wout)


def finish_kernel(
    mixed_in, tokens_in, in_hbm, out_hbm, qkv_in, att_in, extra_in, gain_in, bias_in,
    mixed_out, tokens_out, in_out, out_out, qkv_out, att_out, router_out, gain_out, gain_moe_out, bias_out,
    mixed, tokens, narrow, wide, sem, load_sem, store_sem,
):
    ins = [pltpu.make_async_copy(mixed_in, mixed, sem.at[0]), pltpu.make_async_copy(tokens_in, tokens, sem.at[1])]
    outs = [pltpu.make_async_copy(mixed, mixed_out, sem.at[2]), pltpu.make_async_copy(tokens, tokens_out, sem.at[3])]
    parts, rows = narrow.shape[1], narrow.shape[2]

    def load(kind, k):
        return pltpu.make_async_copy(
            (in_hbm, out_hbm)[kind].at[pl.ds(k * rows, rows)], narrow.at[kind, k], load_sem.at[kind, k])

    def store(kind, k):
        return pltpu.make_async_copy(
            wide.at[kind, k], (in_out, out_out)[kind].at[0, pl.ds(k * rows, rows)], store_sem.at[kind, k])

    for k in range(parts):
        for kind in (0, 1):
            load(kind, k).start()
    for copy in ins:
        copy.start()
    qkv_out[...] = qkv_in[...]
    att_out[...] = att_in[...]
    router_out[...] = extra_in[:, :128].T[: router_out.shape[0]]
    gain_out[...] = gain_in[...].T[0:1]
    gain_moe_out[...] = extra_in[:, 128:].T[0:1]
    bias_out[...] = bias_in[...]
    for k in range(parts):
        for kind in (0, 1):
            load(kind, k).wait()
            wide[kind, k] = narrow[kind, k].astype(F32)
            store(kind, k).start()
    for copy_in, copy_out in zip(ins, outs):
        copy_in.wait()
        copy_out.start()
    for k in range(parts):
        for kind in (0, 1):
            store(kind, k).wait()
    for copy in outs:
        copy.wait()


def finish(experts, mixed, tokens_grad, grad_in, grad_out, qkv, att, extra, gain, bias):
    any_ = pl.BlockSpec(memory_space=pl.ANY)
    vmem = pl.BlockSpec(memory_space=pltpu.VMEM)
    dma = pltpu.SemaphoreType.DMA
    parts = 8
    rows = grad_in.shape[0] // parts
    own = qkv.shape[0]
    shape = jax.ShapeDtypeStruct
    return pl.pallas_call(
        finish_kernel,
        out_shape=(
            shape(mixed.shape, BF16), shape(tokens_grad.shape, F32), shape((1, *grad_in.shape), F32),
            shape((1, *grad_out.shape), F32), shape(qkv.shape, F32), shape(att.shape, F32), shape((experts, own), F32),
            shape((1, own), F32), shape((1, own), F32), shape(bias.shape, F32),
        ),
        in_specs=[any_] * 4 + [vmem] * 5,
        out_specs=tuple([any_] * 4 + [vmem] * 6),
        scratch_shapes=[
            pltpu.VMEM(mixed.shape, BF16),
            pltpu.VMEM(tokens_grad.shape, F32),
            pltpu.VMEM((2, parts, rows, grad_in.shape[1]), BF16),
            pltpu.VMEM((2, parts, rows, grad_in.shape[1]), F32),
            dma((4,)), dma((2, parts)), dma((2, parts)),
        ],
        compiler_params=pltpu.CompilerParams(vmem_limit_bytes=60 * 1024 * 1024),
        name="finish",
    )(mixed, tokens_grad, grad_in, grad_out, qkv, att, extra, gain, bias)


def shards(
    n, tokens, cotangent, routes, buckets, gain_attn, w_qkv, w_att, rel_bias, gain_moe, w_router, w_in, w_out,
):
    axes = ("dp", "expert")
    count, width = tokens.shape
    experts = w_router.shape[1]
    heads = rel_bias.shape[1]
    own = w_qkv.shape[0]
    cap = max(2, 2 * count // experts)
    pad = max(16, cap)
    direct = n == 16 and own % 8 == 0
    extra = sum(jnp.pad(part.astype(F32), ((low, 256 - low - part.shape[0]), (0, 128 - own)))
                for low, part in ((0, w_router.T), (128, gain_attn[None]), (129, gain_moe[None])))
    full = w_att if direct else lax.all_gather(
        jnp.concatenate([w_qkv, extra[:, :own].T.astype(BF16), w_att], axis=1), axes, axis=0, tiled=True)
    mixed, grad_tokens, grad_qkv, grad_att, grad_extra, grad_gain, grad_bias, grad_in, grad_out = layer(
        n, cap, pad, experts, heads, direct, tokens, cotangent, w_qkv, w_att, extra, full, routes.T, rel_bias.T, buckets,
        w_in[0], w_out[0])[:9]
    if not direct:
        lead = grad_qkv.shape[0] - heads // 2
        early = jnp.concatenate([grad_qkv[k] for k in range(lead)], axis=1)
        late = [grad_qkv[lead:, :, c * 128 : (c + 1) * 128].transpose(1, 0, 2).reshape(width, width) for c in range(3)]
        both = lax.psum_scatter(jnp.concatenate([early, *late], axis=1), axes, scatter_dimension=0, tiled=True)
        grad_att, grad_extra = both[:, :width], both[:, width : width + 256]
        grad_qkv = both[:, early.shape[1] :]
        grad_gain = jnp.sum(grad_qkv * w_qkv.astype(F32), axis=1, keepdims=True) / gain_attn.astype(F32)[:, None]
        grad_gain = jnp.broadcast_to(grad_gain, (own, 128))
        grad_bias = lax.psum(grad_bias, axes)
    mixed, grad_tokens, grad_in, grad_out, grad_qkv, grad_att, grad_router, grad_gain, grad_gain_moe, grad_bias = finish(
        experts, mixed, grad_tokens, grad_in, grad_out, grad_qkv, grad_att, grad_extra, grad_gain, grad_bias)
    return (
        mixed, grad_tokens, grad_gain.reshape(own), grad_qkv, grad_att, grad_bias.T, grad_gain_moe.reshape(own), grad_router.T,
        grad_in, grad_out,
    )


def solution(mesh):
    both = P(("dp", "expert"))
    return jax.shard_map(
        functools.partial(shards, mesh.shape["expert"]),
        mesh=mesh,
        in_specs=(both, both, both, P(), both, both, both, P(), both, both, P("expert"), P("expert")),
        out_specs=(both, both, both, both, both, P(), both, both, P("expert", None, "dp"), P("expert", None, "dp")),
        check_vma=False,
    )
```

```python
import functools
import jax
import jax.numpy as jnp
from jax import lax
from jax.experimental import pallas as pl
from jax.experimental.pallas import tpu as pltpu
from jax.sharding import PartitionSpec as P

MESH = pl.DeviceIdType.MESH
F32, BF16 = jnp.float32, jnp.bfloat16
NT = (((1,), (1,)), ((), ()))
EPSILON = 1e-06
PART = 384
WIDE = 768
LAG = (0, 1, 3, 5, 99, 99)


def dot(a, b, dims=(((1,), (0,)), ((), ()))):
    return lax.dot_general(a, b, dims, preferred_element_type=F32)


def exact(a, b, dims=(((1,), (0,)), ((), ()))):
    return lax.dot_general(a, b, dims, preferred_element_type=F32, precision=lax.Precision.HIGHEST)


def flipped(index, bits, count):
    result, bit = 0, 1
    while bit < count:
        result = result + bit * (((index // bit) % 2 + (bits // bit) % 2) % 2)
        bit *= 2
    return result


def gelu_parts(hidden):
    c0, c1 = 0.7978845608028654, 0.044715
    square = hidden * hidden
    bend = jnp.tanh(hidden * (c0 + (c0 * c1) * square))
    half = 0.5 + 0.5 * bend
    slope = half + (0.5 * hidden) * (1.0 - bend * bend) * (c0 + (3.0 * c0 * c1) * square)
    return hidden * half, slope


def slots_by_row(routes, me, pad, experts):
    count = routes.shape[1]
    picked = routes == lax.broadcasted_iota(jnp.int32, (experts, count), 0)
    first = lax.broadcasted_iota(jnp.int32, (count, count), 0)
    second = lax.broadcasted_iota(jnp.int32, (count, count), 1)
    before = dot(picked.astype(BF16), (first < second).astype(BF16))
    rank = jnp.sum(jnp.where(picked, before, 0.0), axis=0, keepdims=True).astype(jnp.int32)
    return jnp.bitwise_xor(routes, me) * pad + rank


def grow_strip(strip, w8):
    strip[0:8] = w8
    have = 8
    while have < strip.shape[0]:
        strip[have : 2 * have] = pltpu.roll(strip[0:have], have, 1)
        have *= 2


SPILLS = 7


def layer_kernel(n, cap, pad, experts, heads, direct, *refs):
    (tokens_ref, cot_ref, qkv_ref, att_ref, extra_ref, full_hbm, routes_ref, table_ref, buckets_hbm, win_hbm, wout_hbm,
     mixed_hbm, tokens_grad_hbm, qkv_grad_ref, att_grad_ref, extra_grad_ref, gain_grad_ref, bias_grad_ref,
     gin_hbm, gout_hbm, probs_hbm, *rest) = refs
    spilled, rest = rest[:SPILLS], rest[SPILLS:]
    (blocks, shard, gains, hot, router, rows, cots, ties, xin, cin, back_in, returned, tie_in, sib_recv,
     sib_in, in1, in2, in3, in4, bias_out, bias_in, bias_pair,
     put_sem, prob_sem, load_sem, pair_sem, swap_send, swap_recv, tree_send, tree_recv, turn_send, turn_recv,
     piece_send, piece_recv, piece_out, hop_send, sib_r, r1, r2, r3, r4, bias_sem, end_sem) = rest
    dp, me = lax.axis_index("dp"), lax.axis_index("expert")
    count, width = tokens_ref.shape
    total = n * pad
    early = 3 * width + 256
    per = 256 // cap
    sibling = (1 - dp, me)
    staged = per == 4
    lane = lax.broadcasted_iota(jnp.int32, (count, 128), 1)

    def peer(p):
        return dp, flipped(me, p, n)

    def remote(src, dst, send, recv, device):
        return pltpu.make_async_remote_copy(
            src_ref=src, dst_ref=dst, send_sem=send, recv_sem=recv, device_id=device, device_id_type=MESH)

    def swap(kind, p):
        src, dst = ((rows, xin), (cots, cin), (rows, back_in), (cots, returned), (ties, tie_in))[kind]
        index = p // per if kind < 2 else 0
        return remote(src.at[p], dst.at[p], swap_send.at[kind, index], swap_recv.at[kind, index], peer(p))

    def swaps(kind, g=None):
        src, dst = ((rows, xin), (cots, cin), (rows, back_in), (cots, returned), (ties, tie_in))[kind]
        index, low, blocks_of = (0, 1, n - 1) if g is None else (0, 1, per - 1) if isinstance(g, int) else (g, g * per, per)
        place = pl.ds(low, blocks_of)
        return remote(src.at[place], dst.at[place], swap_send.at[kind, index], swap_recv.at[kind, index], peer(1))

    def start_swaps(kind, wanted):
        def one(p, _):
            @pl.when(wanted(p))
            def _():
                swap(kind, p).start()
            return 0

        lax.fori_loop(1, n, one, 0)

    def greet_all():
        barrier = pltpu.get_barrier_semaphore()

        def greet(p, _):
            pl.semaphore_signal(barrier, inc=1, device_id=peer(p), device_id_type=MESH)
            return 0

        lax.fori_loop(1, n, greet, 0)
        pl.semaphore_signal(barrier, inc=1, device_id=sibling, device_id_type=MESH)
        pl.semaphore_wait(barrier, n)

    half = win_hbm.shape[1] // 2
    steps = half // WIDE
    pieces = [(kind, k) for k in range(steps) for kind in (0, 1)]

    def piece(kind, k):
        place = pl.ds((kind * steps + k) * WIDE, WIDE)
        return remote(blocks.at[:, place], sib_recv.at[kind, k], piece_send.at[kind, k], piece_recv.at[kind, k], sibling)

    def out_piece(kind, k):
        return pltpu.make_async_copy(
            sib_recv.at[kind, k], (gin_hbm, gout_hbm)[kind].at[:, pl.ds(k * WIDE, WIDE)], piece_out.at[kind, k])

    def forward(w, packed, normed, attended, middle, moe_in, chance, probs, strip, bias, ends, weights):
        puts = []

        def put(index, src):
            copy = pltpu.make_async_copy(src, spilled[index], put_sem.at[index])
            copy.start()
            puts.append(copy)

        offsets = [pltpu.make_async_copy(buckets_hbm.at[:, pl.ds(c, 128)], ends.at[i], load_sem.at[i])
                   for i, c in enumerate((0, count - 128))]
        for copy in offsets:
            copy.start()
        if direct:
            weights[:, : 3 * width] = qkv_ref[...].astype(F32)
            weights[:, 3 * width : early] = extra_ref[...].T[: weights.shape[0]]
            weights[:, early:] = att_ref[...].astype(F32)
        greet_all()
        if direct:
            own = weights.shape[0]
            block = 2 * own
            pair = remote(weights, shard, pair_sem.at[0], pair_sem.at[1], sibling)
            pair.start()
        else:
            load = pltpu.make_async_copy(full_hbm, w, pair_sem.at[0])
            load.start()
        slots = slots_by_row(routes_ref[...], me, pad, experts)

        def to_slots(values):
            hits = (slots == lax.broadcasted_iota(jnp.int32, (total, count), 0)).astype(BF16)
            return dot(hits, values).astype(BF16).reshape(n, pad, width)

        def make_cots():
            cots[...] = to_slots(cot_ref[...])
            cin[0] = cots[0]

        def make_bias():
            for copy in offsets:
                copy.wait()
            last, first = ends[1].astype(F32).T[127:128], ends[0].astype(F32).T[0:1]
            line = jnp.concatenate([last, pltpu.roll(first, count - 1, 1)], axis=1)
            line = pltpu.roll(jnp.broadcast_to(line, (8, 2 * count)), 2 * count - 127, 1)[0:1]
            hot[...] = (line.astype(jnp.int32) == lax.broadcasted_iota(jnp.int32, hot.shape, 0)).astype(F32)
            table = exact(table_ref[...], hot[...])
            for h in range(heads):
                row = jnp.broadcast_to(table[h : h + 1], (8, 2 * count))
                place = lax.broadcasted_iota(jnp.int32, row.shape, 0)
                shifted = row
                for r in range(1, 8):
                    shifted = jnp.where(place == r, pltpu.roll(row, r, 1), shifted)
                bias[h] = shifted

        if direct:
            pair.wait()
            mine, other = weights[...], shard[...]
            blocks[pl.ds(pl.multiple_of(me * block, 16), block), : w.shape[1]] = jnp.concatenate(
                [jnp.where(dp == 0, mine, other), jnp.where(dp == 0, other, mine)], axis=0).astype(BF16)
            second, third = 2 - dp, 1 + dp
            far = list(range(4, n, 4))
            near = [0] + far

            def at(t, r, core):
                start, size = ((0, early // 2), (early, width // 2))[t]
                return blocks.at[pl.ds(pl.multiple_of(flipped(me, r, n) * block, 16), block),
                                 pl.ds(pl.multiple_of(start + core * size, 128), size)]

            def hop(t, r, step):
                return remote(at(t, r, dp), at(t, r, dp), tree_send.at[t], tree_recv.at[t, r + step], peer(step))

            def arrived(t, r):
                remote(at(t, r, dp), at(t, r, dp), tree_send.at[t], tree_recv.at[t, r], peer(r)).wait_recv()

            def to_sibling(t, r, core):
                return remote(at(t, r, core), at(t, r, core), turn_send.at[t], turn_recv.at[t], sibling)

            def bulk(t, send, recv):
                place = blocks.at[: (n - 1) * block, : (early // 2, width // 2)[t]]
                return remote(place, place, send.at[t], recv.at[t] if recv is turn_recv else recv.at[t, 0], sibling)

            def turn(t, step):
                if step == 0:
                    hop(t, 0, 8).start()
                    hop(t, 0, 4).start()
                    hop(t, 0, third).start()
                    hop(t, 0, second).start()
                elif step == 1:
                    for r in (8, 4, 12):
                        arrived(t, r)
                        if r == 8:
                            hop(t, 8, 4).start()
                        hop(t, r, third).start()
                        hop(t, r, second).start()
                        to_sibling(t, r, dp).start()
                elif step == 2:
                    for r in near:
                        arrived(t, r + second)
                        hop(t, r + second, third).start()
                        to_sibling(t, r + second, dp).start()
                elif step == 3:
                    for r in near:
                        arrived(t, r + third)
                        to_sibling(t, r + third, dp).start()
                        arrived(t, r + 3)
                        to_sibling(t, r + 3, dp).start()
                else:
                    bulk(t, turn_send, turn_recv).wait_recv()
                    place = (slice(0, early), slice(early, w.shape[1]))[t]
                    for core in (0, 1):
                        for q in range(n // 2):
                            low = 2 * q * block + core * own
                            pair_rows = [blocks[p : p + own, place].astype(F32) for p in (low, low + block)]
                            w[core * own * n + q * block : core * own * n + (q + 1) * block, place] = jnp.concatenate(
                                pair_rows, axis=0).astype(BF16)

            turn(0, 0)
            make_bias()
            make_cots()
            turn(0, 1)
            turn(1, 0)
            start_swaps(1, lambda p: p % 4 == 0)
            turn(0, 2)
            turn(1, 1)
            turn(0, 3)
            turn(1, 2)
            start_swaps(1, lambda p: p % 4 != 0)
            turn(0, 4)
        else:
            make_bias()
            make_cots()
            start_swaps(1, lambda p: p > 0)
            load.wait()
        gains[...] = w[:, 3 * width + 128 : early].astype(F32).T[0:8]
        router[...] = w[:, 3 * width : 3 * width + 128]
        x = tokens_ref[...].astype(F32)
        normed[...] = (x * lax.rsqrt(jnp.mean(x * x, axis=1, keepdims=True) + EPSILON) * gains[0:1]).astype(BF16)
        put(0, normed)
        for c in range(3):
            cols_c = slice(c * width, (c + 1) * width)
            packed[:, cols_c] = dot(normed[...], w[:, cols_c]).astype(BF16)
        put(1, packed)
        scale = (width // heads) ** -0.5

        def put_probs(k):
            return pltpu.make_async_copy(probs.at[pl.ds(2 * k, 2)], probs_hbm.at[pl.ds(2 * k, 2)], prob_sem.at[0])

        def attend(k, _):
            def part(c):
                return packed[:, pl.ds(pl.multiple_of(c * width + k * 128, 128), 128)]

            queries = (part(0).astype(F32) * scale).astype(BF16)
            keys = part(1)
            values = part(2).astype(F32).T.astype(BF16)
            outs = []
            for h in (0, 1):
                grow_strip(strip, bias[2 * k + h])
                own_keys = jnp.where((lane < 64) == (h == 0), keys, jnp.zeros_like(keys))
                scores = dot(own_keys, queries, NT)
                scores = jnp.concatenate(
                    [scores[128 * b : 128 * b + 128] + strip[:, 384 - 128 * b : 896 - 128 * b] for b in range(4)], axis=0)
                powers = jnp.exp(scores - jnp.max(scores, axis=0, keepdims=True))
                part_weights = (powers * (1.0 / jnp.sum(powers, axis=0, keepdims=True))).astype(BF16)
                probs[2 * k + h] = part_weights
                outs.append(dot(values[64 * h : 64 * h + 64], part_weights))
            put_probs(k).start()
            attended[:, pl.ds(pl.multiple_of(k * 128, 128), 128)] = jnp.concatenate(outs, axis=0).T.astype(BF16)
            if direct:
                for step in (3, 4):
                    @pl.when(k == step + 1)
                    def _():
                        turn(1, step)
            return 0

        lax.fori_loop(0, heads // 2, attend, 0)
        mid = tokens_ref[...].astype(F32) + dot(attended[...], w[:, early:])
        middle[...] = mid
        moe = (mid * lax.rsqrt(jnp.mean(mid * mid, axis=1, keepdims=True) + EPSILON) * gains[1:2]).astype(BF16)
        moe_in[...] = moe
        rows[...] = to_slots(moe)
        start_swaps(0, lambda p: (p < 4) | ((p % 4 == 0) & (p < 12)) if staged else p > 0)
        xin[0] = rows[0]
        put(2, attended)
        put(3, middle)
        put(4, moe_in)
        put(5, w)
        logits = dot(moe, router[...])
        logits = jnp.where(lane < experts, logits, -1e30)
        powers = jnp.exp(logits - jnp.max(logits, axis=1, keepdims=True))
        chance[...] = powers / jnp.sum(powers, axis=1, keepdims=True)
        put(6, chance)
        if direct:
            for t in (0, 1):
                bulk(t, tree_send, tree_recv).wait_send()
                bulk(t, turn_send, turn_recv).wait_send()
        for copy in puts:
            copy.wait()
        pltpu.make_async_copy(probs, probs_hbm, prob_sem.at[0]).wait()

    def experts_both(win, wout, xt, rt, act, hgr):
        ff = win.shape[1]
        group_rows = per * cap
        chunk = 1024
        loads = [pltpu.make_async_copy(win_hbm, win, load_sem.at[0]), pltpu.make_async_copy(wout_hbm, wout, load_sem.at[1])]
        for load in loads:
            load.start()

        def packed_rows(ref, g):
            block = ref[pl.ds(g * per, per)].reshape(per * pad, width)
            if pad == cap:
                return block
            r = lax.broadcasted_iota(jnp.int32, (group_rows, per * pad), 0)
            c = lax.broadcasted_iota(jnp.int32, (group_rows, per * pad), 1)
            return dot(((r // cap) * pad + r % cap == c).astype(BF16), block).astype(BF16)

        def spread_rows(block):
            if pad == cap:
                return block.reshape(per, pad, width)
            r = lax.broadcasted_iota(jnp.int32, (per * pad, group_rows), 0)
            c = lax.broadcasted_iota(jnp.int32, (per * pad, group_rows), 1)
            pick = (r // pad == c // cap) & (r % pad == c % cap)
            return dot(pick.astype(BF16), block).astype(BF16).reshape(per, pad, width)

        def group(g, _):
            def over(act_on):
                def one(j, _):
                    @pl.when(g * per + j != 0)
                    def _():
                        act_on(g * per + j)
                    return 0

                lax.fori_loop(0, per, one, 0)

            def all_of(kind, act_on):
                @pl.when(g == 0)
                def _():
                    act_on(swaps(kind, 0))

                @pl.when(g != 0)
                def _():
                    act_on(swaps(kind, g))

            all_of(0, lambda copies: copies.wait_recv())

            @pl.when(g == 0)
            def _():
                if staged:
                    start_swaps(0, lambda p: (p >= 4) & (p % 4 != 0) & (p < 12))
                for load in loads:
                    load.wait()

            if staged:
                @pl.when(g == 1)
                def _():
                    start_swaps(0, lambda p: p >= 12)

            all_of(1, lambda copies: copies.wait_recv())
            here = pl.ds(pl.multiple_of(g * group_rows, group_rows), group_rows)
            x = packed_rows(xin, g)
            logits = dot(x, router[...])
            lanes = lax.broadcasted_iota(jnp.int32, logits.shape, 1)
            logits = jnp.where(lanes < experts, logits, -1e30)
            powers = jnp.exp(logits - jnp.max(logits, axis=1, keepdims=True))
            gate = jnp.sum(jnp.where(lanes == me, powers, 0.0), axis=1, keepdims=True) / jnp.sum(
                powers, axis=1, keepdims=True)
            r = (gate * packed_rows(cin, g).astype(F32)).astype(BF16)
            xt[:, here] = x.T
            rt[:, here] = r.T

            def hidden_chunk(k, _):
                cols = pl.ds(pl.multiple_of(k * chunk, chunk), chunk)
                value, slope = gelu_parts(dot(x, win[:, cols]))
                act[here, cols] = value.astype(BF16)
                hgr[here, cols] = (dot(r, wout[:, cols]) * slope).astype(BF16)
                return 0

            lax.fori_loop(0, ff // chunk, hidden_chunk, 0)
            back = spread_rows(dot(hgr[here], win[...], NT).astype(BF16))
            all_of(0, lambda copies: copies.wait_send())
            rows[pl.ds(g * per, per)] = back
            over(lambda p: swap(2, p).start())
            produced = dot(act[here], wout[...], NT).astype(BF16)
            tie = jnp.sum(r.astype(F32) * produced.astype(F32), axis=1, keepdims=True)
            for j in range(per):
                row = jnp.broadcast_to(tie[j * cap : (j + 1) * cap], (cap, 128)).T[0:8]
                ties[g * per + j] = jnp.concatenate([row, jnp.zeros((8, 128 - cap), F32)], axis=1)
            over(lambda p: swap(4, p).start())
            all_of(1, lambda copies: copies.wait_send())
            cots[pl.ds(g * per, per)] = spread_rows(produced)

            @pl.when(g < n // per // 2)
            def _():
                over(lambda p: swap(3, p).start())

            return 0

        lax.fori_loop(0, n // per, group, 0)
        back_in[0] = rows[0]
        tie_in[0] = ties[0]
        returned[0] = cots[0]

        def partial(kind, owner, k):
            cols = pl.ds(pl.multiple_of(owner * half + k * WIDE, 128), WIDE)
            return dot(xt[...], hgr[:, cols]) if kind == 0 else dot(rt[...], act[:, cols])

        for kind, k in pieces:
            place = (kind * steps + k) * WIDE
            blocks[:, place : place + WIDE] = partial(kind, 1 - dp, k).astype(BF16)
            piece(kind, k).start()
        for kind, k in pieces:
            value = partial(kind, dp, k)
            piece(kind, k).wait_recv()
            sib_recv[kind, k] = (value + sib_recv[kind, k].astype(F32)).astype(BF16)
            out_piece(kind, k).start()

    def backward(w, packed, normed, attended, middle, moe_in, chance, prob, mid_grad, att_cot, packed_grad, normed_t, chunk,
                 strip, bias_rows, mine, keep, out1, out2, out3, out4):
        loaded = (normed, packed, attended, middle, moe_in, w, chance)
        loads = [pltpu.make_async_copy(spilled[i], loaded[i], load_sem.at[i]) for i in range(SPILLS)]
        order = (6, 3, 5, 2, 4, 0, 1)
        for i in order:
            loads[i].start()

        def fetch(k):
            return pltpu.make_async_copy(probs_hbm.at[pl.ds(2 * k, 2)], prob.at[k % 2], prob_sem.at[k % 2])

        fetch(0).start()
        own = qkv_ref.shape[0]
        lead = (width + 256 + PART - 1) // PART
        chunks = lead + heads // 2

        if direct:
            half_rows = own * n

            steps_out = ((out1, in1, r1), (out2, in2, r2), (out3, in3, r3), (out4, in4, r4))
            ways = (1 + dp, 2 - dp, 4, 8)

            def sib_out(k):
                across = blocks.shape[1] // PART
                return blocks.at[pl.ds(pl.multiple_of((k // across) * half_rows, 16), half_rows),
                                 pl.ds(pl.multiple_of((k % across) * PART, 128), PART)]

            def hop(stage, k):
                if stage == 0:
                    return remote(sib_out(k), sib_in.at[k], hop_send.at[0], sib_r.at[k], sibling)
                src, dst, recv = steps_out[stage - 1]
                return remote(src.at[k], dst.at[k], hop_send.at[stage], recv.at[k], peer(ways[stage - 1]))

            def unit(k, u):
                r = ways[0] * (u // 4) + ways[1] * ((u // 2) % 2) + ways[2] * (u % 2)
                places = [pl.multiple_of(flipped(me, r + z, n) * own, 8) for z in (0, ways[3])]
                return jnp.concatenate([mine[k % 2, pl.ds(place, own)] for place in places], axis=0)

            def stage(s, k):
                if s == 0:
                    there = pl.ds(pl.multiple_of((1 - dp) * half_rows, 8), half_rows)
                    here = pl.ds(pl.multiple_of(dp * half_rows, 8), half_rows)
                    sib_out(k)[...] = chunk[there].astype(BF16)
                    hop(0, k).start()
                    mine[k % 2] = chunk[here]
                elif s == 1:
                    hop(0, k).wait_recv()
                    mine[k % 2] = mine[k % 2] + sib_in[k].astype(F32)
                    for u in range(4):
                        out1[k, 2 * own * u : 2 * own * (u + 1)] = unit(k, u + 4).astype(BF16)
                    hop(1, k).start()
                    for u in range(4):
                        keep[k, 2 * own * u : 2 * own * (u + 1)] = unit(k, u)
                elif s in (2, 3):
                    src, dst = steps_out[s - 1][0], steps_out[s - 2][1]
                    left = 8 * own // (1 << (s - 1))
                    hop(s - 1, k).wait_recv()
                    value = keep[k, : 2 * left] + dst[k].astype(F32)
                    src[k] = value[left:].astype(BF16)
                    hop(s, k).start()
                    keep[k, :left] = value[:left]
                elif s == 4:
                    hop(3, k).wait_recv()
                    value = keep[k, : 2 * own] + in3[k].astype(F32)
                    out4[k] = jnp.concatenate(
                        [value[own:, 128 * c : 128 * (c + 1)] for c in range(3)]
                        + [jnp.zeros((out4.shape[1] - 3 * own, 128), F32)], axis=0).astype(BF16)
                    hop(4, k).start()
                    keep[k, :own] = value[:own]
                else:
                    hop(4, k).wait_recv()
                    far = in4[k].astype(F32)
                    keep[k, :own] = keep[k, :own] + jnp.concatenate(
                        [far[own * c : own * (c + 1)] for c in range(3)], axis=1)

            def advance(k):
                stage(0, k)
                for s in range(1, 6):
                    @pl.when((k - LAG[s] >= 0) & (k - LAG[s] < chunks))
                    def _():
                        stage(s, k - LAG[s])

            done = {k: max(s for s in range(6) if LAG[s] <= chunks - 1 - k) for k in range(chunks)}

            def drain(last, *which):
                for k in which or range(chunks):
                    while done[k] < last:
                        done[k] += 1
                        stage(done[k], k)

        else:
            def advance(k):
                copy = pltpu.make_async_copy(chunk, qkv_grad_ref.at[k], end_sem.at[0])
                copy.start()
                copy.wait()

            def drain(*_):
                pass

        expert_of = jnp.broadcast_to(routes_ref[...].astype(F32), (128, count)).T[:, 0:1].astype(jnp.int32)
        picked = expert_of == lane
        first = lax.broadcasted_iota(jnp.int32, (count, count), 0)
        other = lax.broadcasted_iota(jnp.int32, (count, count), 1)
        before = dot((other < first).astype(BF16), picked.astype(BF16))
        rank = jnp.sum(jnp.where(picked, before, 0.0), axis=1, keepdims=True).astype(jnp.int32)
        place = jnp.bitwise_xor(expert_of, me)
        hits = (place * pad + rank == lax.broadcasted_iota(jnp.int32, (count, total), 1)).astype(BF16)

        def each_peer(act_on):
            def one(p, _):
                act_on(p)
                return 0

            lax.fori_loop(1, n, one, 0)

        for kind, k in pieces:
            piece(kind, k).wait_send()
        swaps(2).wait_recv()
        swaps(4).wait_recv()
        ties_row = exact((place == lax.broadcasted_iota(jnp.int32, (count, n), 1)).astype(F32), jnp.max(tie_in[...], axis=1))
        tie = jnp.sum(jnp.where(lane == rank, ties_row, 0.0), axis=1, keepdims=True)
        for i in order[:1]:
            loads[i].wait()
        logit_grad = (tie * (picked.astype(F32) - chance[...])).astype(BF16)
        grad = dot(hits, back_in[...].reshape(total, width))
        for i in order[1:]:
            loads[i].wait()
        grad = grad + dot(logit_grad, router[...], NT)
        mid = middle[...]
        root = lax.rsqrt(jnp.mean(mid * mid, axis=1, keepdims=True) + EPSILON)
        unit_mid = mid * root
        gain_rows = jnp.sum(grad * unit_mid, axis=0, keepdims=True)
        scaled = grad * gains[1:2]
        mid_g = cot_ref[...].astype(F32) + root * (scaled - unit_mid * jnp.mean(scaled * unit_mid, axis=1, keepdims=True))
        mid_grad[...] = mid_g
        attn_grad = mid_g.astype(BF16)
        att_cot[...] = dot(attn_grad, w[:, early:], NT).astype(BF16)
        attended_t = attended[...].T
        for k in range(lead):
            if (k + 1) * PART <= width:
                chunk[...] = dot(attended_t, attn_grad[:, k * PART : (k + 1) * PART])
            else:
                chunk[:, 0:128] = dot(moe_in[...].T, logit_grad)
                chunk[:, 128:256] = jnp.broadcast_to(gain_rows, (128, width)).T
                chunk[:, 256:] = jnp.zeros((width, PART - 256), F32)
            advance(k)
        normed_t[...] = normed[...].T
        swaps(2).wait_send()
        start_swaps(3, lambda p: (p >= n // 2) & (p % 4 == 0))

        scale = (width // heads) ** -0.5

        def attend_back(k, _):
            fetch(k).wait()

            @pl.when(k + 1 < heads // 2)
            def _():
                fetch(k + 1).start()

            def part(c):
                return packed[:, pl.ds(pl.multiple_of(c * width + k * 128, 128), 128)]

            queries, keys, values = part(0), part(1), part(2)
            keys_t = (keys.astype(F32) * scale).T.astype(BF16)
            cot = att_cot[:, pl.ds(pl.multiple_of(k * 128, 128), 128)]
            query_t, key_g, value_g = [], None, None
            for h in (0, 1):
                mask = (lane < 64) == (h == 0)
                own_cot = jnp.where(mask, cot, jnp.zeros_like(cot))
                own_queries = jnp.where(mask, queries, jnp.zeros_like(queries))
                weights = prob[k % 2, h]
                chances = weights.astype(F32)
                product = chances * dot(values, own_cot, NT)
                score_grad = (product - chances * jnp.sum(product, axis=0, keepdims=True)).astype(BF16)
                wide = score_grad.astype(F32)
                for b in range(4):
                    block = wide[128 * b : 128 * b + 128]
                    cols = slice(384 - 128 * b, 896 - 128 * b)
                    if b == 0:
                        strip[:, cols] = block
                        strip[:, 0:384] = jnp.zeros((128, 384), F32)
                        strip[:, 896:1024] = jnp.zeros((128, 128), F32)
                    else:
                        strip[:, cols] += block
                have = 64
                folded = strip[...]
                while have >= 8:
                    folded = folded[:have] + pltpu.roll(folded[have:], 1024 - have, 1)
                    have //= 2
                for s in range(1, 8):
                    folded = jnp.where(lax.broadcasted_iota(jnp.int32, folded.shape, 0) == s,
                                       pltpu.roll(folded, 1024 - s, 1), folded)
                bias_rows[2 * k + h] = folded
                v = dot(weights, own_cot)
                q = dot(score_grad, own_queries)
                value_g = v if h == 0 else value_g + v
                key_g = q if h == 0 else key_g + q
                query_t.append(dot(keys_t[64 * h : 64 * h + 64], score_grad))
            query_g = jnp.concatenate(query_t, axis=0).T.astype(BF16)
            grads = jnp.concatenate([query_g, (key_g * scale).astype(BF16), value_g.astype(BF16)], axis=1)
            for c in range(3):
                packed_grad[:, pl.ds(pl.multiple_of(c * width + k * 128, 128), 128)] = grads[:, c * 128 : (c + 1) * 128]
            chunk[...] = dot(normed_t[...], grads)
            advance(k + lead)

            @pl.when(k ==  0)
            def _():
                start_swaps(3, lambda p: (p >= n // 2) & (p % 4 == 1))

            @pl.when(k ==  0)
            def _():
                start_swaps(3, lambda p: (p >= n // 2) & (p % 4 == 2))

            @pl.when(k ==  1)
            def _():
                start_swaps(3, lambda p: (p >= n // 2) & (p % 4 == 3))

            return 0

        lax.fori_loop(0, heads // 2, attend_back, 0)
        drain(1, chunks - 1)
        drain(2, *range(chunks - 1))
        drain(3, *range(chunks - 3))
        sums = jnp.concatenate([jnp.sum(bias_rows[h], axis=0, keepdims=True) for h in range(heads)], axis=0)
        bias_out[...] = exact(sums, hot[...], NT)
        if direct:
            pair_hop = remote(bias_out, bias_pair, pair_sem.at[2], pair_sem.at[3], sibling)
            pair_hop.start()

            def bias_hop(p):
                return remote(bias_in.at[me], bias_in.at[me], bias_sem.at[0], bias_sem.at[1], peer(p))

            place = bias_in.at[1:]
            bias_all = remote(place, place, bias_sem.at[0], bias_sem.at[1], peer(1))

        normed_grad = dot(packed_grad[...], w[:, : 3 * width], NT)
        drain(2)
        drain(3, *range(chunks - 1))
        drain(4, *range(chunks - 4))
        if direct:
            pair_hop.wait()
            bias_in[me] = bias_out[...] + bias_pair[...]
            each_peer(lambda p: bias_hop(p).start())
        x = tokens_ref[...].astype(F32)
        root = lax.rsqrt(jnp.mean(x * x, axis=1, keepdims=True) + EPSILON)
        unit_x = x * root
        scaled = normed_grad * gains[0:1]
        mid_grad[...] = mid_grad[...] + root * (scaled - unit_x * jnp.mean(scaled * unit_x, axis=1, keepdims=True))
        ends = [pltpu.make_async_copy(mid_grad, tokens_grad_hbm, end_sem.at[0]),
                pltpu.make_async_copy(att_cot, mixed_hbm, end_sem.at[1])]
        ends[0].start()
        drain(3)
        drain(4, *range(chunks - 1))
        swaps(3).wait_recv()
        gate = jnp.sum(jnp.where(picked, chance[...], 0.0), axis=1, keepdims=True)
        att_cot[...] = (middle[...] + gate * dot(hits, returned[...].reshape(total, width))).astype(BF16)
        ends[1].start()
        if direct:
            drain(4)
            drain(5)
            bias_all.wait_recv()
            total_bias = bias_in[0]
            for p in range(1, n):
                total_bias = total_bias + bias_in[p]
            bias_grad_ref[...] = total_bias
            for k in range(chunks):
                result = keep[k, :own]
                if k >= lead:
                    for c in range(3):
                        start = c * width + (k - lead) * 128
                        qkv_grad_ref[:, start : start + 128] = result[:, c * 128 : (c + 1) * 128]
                elif (k + 1) * PART <= width:
                    att_grad_ref[:, k * PART : (k + 1) * PART] = result
                else:
                    extra_grad_ref[...] = result[:, :256]
            total_gain = jnp.sum(qkv_grad_ref[...] * qkv_ref[...].astype(F32), axis=1, keepdims=True)
            gain_grad_ref[...] = jnp.broadcast_to(total_gain / extra_ref[128:256].T[:own, 0:1], gain_grad_ref.shape)

            for s, sent in enumerate((sib_in, out1, out2, out3, out4)):
                remote(sent, sent, hop_send.at[s], sib_r.at[0], sibling).wait_send()
            bias_all.wait_send()
        else:
            bias_grad_ref[...] = bias_out[...]
        for kind in (3, 4):
            swaps(kind).wait_send()
        for copy in ends:
            copy.wait()
        for kind, k in pieces:
            out_piece(kind, k).wait()

    wide = w_columns(width)
    scratch = pltpu.VMEM
    shared = [
        scratch((width, wide), BF16), scratch((count, 3 * width), BF16), scratch((count, width), BF16),
        scratch((count, width), BF16), scratch((count, width), F32), scratch((count, width), BF16), scratch((count, 128), F32),
    ]
    own_rows = qkv_ref.shape[0]
    pl.run_scoped(
        forward, *shared, scratch((heads, count, count), BF16), scratch((128, 2 * count), F32),
        scratch((heads, 8, 2 * count), F32), scratch((2, count, 128), jnp.int32),
        scratch((own_rows, wide) if direct else (8, 128), F32))
    pl.run_scoped(
        experts_both, *[scratch((width, win_hbm.shape[1]), BF16) for _ in range(2)],
        *[scratch((width, n * cap), BF16) for _ in range(2)], *[scratch((n * cap, win_hbm.shape[1]), BF16) for _ in range(2)])
    all_chunks = (width + 256 + PART - 1) // PART + heads // 2

    def buffer(shape, kind):
        return scratch((all_chunks, *shape) if direct else (8, 128), kind)

    pl.run_scoped(
        backward, *shared, scratch((2, 2, count, count), BF16), scratch((count, width), F32), scratch((count, width), BF16),
        scratch((count, 3 * width), BF16), scratch((width, count), BF16), scratch((width, PART), F32),
        scratch((128, 2 * count), F32), scratch((heads, 8, 2 * count), F32),
        scratch((2, own_rows * n, PART), F32), buffer((8 * own_rows, PART), F32),
        *[buffer((own_rows << s, PART), BF16) for s in (3, 2, 1)], buffer((-(-3 * own_rows // 16) * 16, 128), BF16))


def w_columns(width):
    return 4 * width + 256


def layer(n, cap, pad, experts, heads, direct, tokens, cotangent, qkv, att, extra, full, routes, table, buckets, win, wout):
    count, width = tokens.shape
    wide = w_columns(width)
    own = qkv.shape[0]
    kinds = table.shape[1]
    ff = win.shape[1]
    chunks = (width + 256 + PART - 1) // PART + heads // 2
    steps = ff // 2 // WIDE
    short = -(-3 * own // 16) * 16
    any_ = pl.BlockSpec(memory_space=pl.ANY)
    vmem = pl.BlockSpec(memory_space=pltpu.VMEM)
    dma = pltpu.SemaphoreType.DMA
    scratch = pltpu.VMEM
    shape = jax.ShapeDtypeStruct

    def landing(*rest):
        return scratch((chunks, *rest) if direct else (16, 128), BF16)

    outs = [
        (shape((count, width), BF16), any_), (shape((count, width), F32), any_),
        (shape((own, 3 * width), F32), vmem) if direct else (shape((chunks, width, PART), F32), any_),
        (shape((own, width), F32), vmem), (shape((own, 256), F32), vmem), (shape((own, 128), F32), vmem),
        (shape((heads, kinds), F32), vmem), (shape((width, ff // 2), BF16), any_), (shape((width, ff // 2), BF16), any_),
        (shape((heads, count, count), BF16), any_), (shape((count, width), BF16), any_),
        (shape((count, 3 * width), BF16), any_), (shape((count, width), BF16), any_), (shape((count, width), F32), any_),
        (shape((count, width), BF16), any_), (shape((width, wide), BF16), any_), (shape((count, 128), F32), any_),
    ]
    slots = scratch((n, pad, width), BF16)
    return pl.pallas_call(
        functools.partial(layer_kernel, n, cap, pad, experts, heads, direct),
        out_shape=tuple(o[0] for o in outs),
        in_specs=[vmem] * 5 + [any_, vmem, vmem, any_, any_, any_],
        out_specs=tuple(o[1] for o in outs),
        scratch_shapes=[
            scratch((width, max(wide, 2 * steps * WIDE)), BF16),
            scratch((own, wide) if direct else (8, 128), F32),
            scratch((8, width), F32), scratch((kinds, 2 * count), F32), scratch((width, 128), BF16),
            slots, slots, scratch((n, 8, 128), F32), slots, slots, slots, slots, scratch((n, 8, 128), F32),
            scratch((2, steps, width, WIDE), BF16),
            landing(own * n, PART), *[landing(own << s, PART) for s in (3, 2, 1)], landing(short, 128),
            scratch((heads, kinds), F32), scratch((n, heads, kinds), F32), scratch((heads, kinds), F32),
            dma((SPILLS,)), dma((2,)), dma((SPILLS,)), dma((4,)), dma((5, n * cap // 256)), dma((5, n * cap // 256)),
            dma((2,)), dma((2, n)), dma((2,)), dma((2,)),
            dma((2, steps)), dma((2, steps)), dma((2, steps)),
            dma((5,)), *[dma((chunks,)) for _ in range(5)], dma((2,)), dma((2,)),
        ],
        compiler_params=pltpu.CompilerParams(
            collective_id=1, has_side_effects=True, vmem_limit_bytes=63 * 1024 * 1024),
        name="layer",
    )(tokens, cotangent, qkv, att, extra, full, routes, table, buckets, win, wout)


def finish_kernel(
    mixed_in, tokens_in, in_hbm, out_hbm, qkv_in, att_in, extra_in, gain_in, bias_in,
    mixed_out, tokens_out, in_out, out_out, qkv_out, att_out, router_out, gain_out, gain_moe_out, bias_out,
    mixed, tokens, narrow, wide, sem, load_sem, store_sem,
):
    ins = [pltpu.make_async_copy(mixed_in, mixed, sem.at[0]), pltpu.make_async_copy(tokens_in, tokens, sem.at[1])]
    outs = [pltpu.make_async_copy(mixed, mixed_out, sem.at[2]), pltpu.make_async_copy(tokens, tokens_out, sem.at[3])]
    parts, rows = narrow.shape[1], narrow.shape[2]

    def load(kind, k):
        return pltpu.make_async_copy(
            (in_hbm, out_hbm)[kind].at[pl.ds(k * rows, rows)], narrow.at[kind, k], load_sem.at[kind, k])

    def store(kind, k):
        return pltpu.make_async_copy(
            wide.at[kind, k], (in_out, out_out)[kind].at[0, pl.ds(k * rows, rows)], store_sem.at[kind, k])

    for k in range(parts):
        for kind in (0, 1):
            load(kind, k).start()
    for copy in ins:
        copy.start()
    qkv_out[...] = qkv_in[...]
    att_out[...] = att_in[...]
    router_out[...] = extra_in[:, :128].T[: router_out.shape[0]]
    gain_out[...] = gain_in[...].T[0:1]
    gain_moe_out[...] = extra_in[:, 128:].T[0:1]
    bias_out[...] = bias_in[...]
    for k in range(parts):
        for kind in (0, 1):
            load(kind, k).wait()
            wide[kind, k] = narrow[kind, k].astype(F32)
            store(kind, k).start()
    for copy_in, copy_out in zip(ins, outs):
        copy_in.wait()
        copy_out.start()
    for k in range(parts):
        for kind in (0, 1):
            store(kind, k).wait()
    for copy in outs:
        copy.wait()


def finish(experts, mixed, tokens_grad, grad_in, grad_out, qkv, att, extra, gain, bias):
    any_ = pl.BlockSpec(memory_space=pl.ANY)
    vmem = pl.BlockSpec(memory_space=pltpu.VMEM)
    dma = pltpu.SemaphoreType.DMA
    parts = 8
    rows = grad_in.shape[0] // parts
    own = qkv.shape[0]
    shape = jax.ShapeDtypeStruct
    return pl.pallas_call(
        finish_kernel,
        out_shape=(
            shape(mixed.shape, BF16), shape(tokens_grad.shape, F32), shape((1, *grad_in.shape), F32),
            shape((1, *grad_out.shape), F32), shape(qkv.shape, F32), shape(att.shape, F32), shape((experts, own), F32),
            shape((1, own), F32), shape((1, own), F32), shape(bias.shape, F32),
        ),
        in_specs=[any_] * 4 + [vmem] * 5,
        out_specs=tuple([any_] * 4 + [vmem] * 6),
        scratch_shapes=[
            pltpu.VMEM(mixed.shape, BF16),
            pltpu.VMEM(tokens_grad.shape, F32),
            pltpu.VMEM((2, parts, rows, grad_in.shape[1]), BF16),
            pltpu.VMEM((2, parts, rows, grad_in.shape[1]), F32),
            dma((4,)), dma((2, parts)), dma((2, parts)),
        ],
        compiler_params=pltpu.CompilerParams(vmem_limit_bytes=60 * 1024 * 1024),
        name="finish",
    )(mixed, tokens_grad, grad_in, grad_out, qkv, att, extra, gain, bias)


def shards(
    n, tokens, cotangent, routes, buckets, gain_attn, w_qkv, w_att, rel_bias, gain_moe, w_router, w_in, w_out,
):
    axes = ("dp", "expert")
    count, width = tokens.shape
    experts = w_router.shape[1]
    heads = rel_bias.shape[1]
    own = w_qkv.shape[0]
    cap = max(2, 2 * count // experts)
    pad = max(16, cap)
    direct = n == 16 and own % 8 == 0
    extra = sum(jnp.pad(part.astype(F32), ((low, 256 - low - part.shape[0]), (0, 128 - own)))
                for low, part in ((0, w_router.T), (128, gain_attn[None]), (129, gain_moe[None])))
    full = w_att if direct else lax.all_gather(
        jnp.concatenate([w_qkv, extra[:, :own].T.astype(BF16), w_att], axis=1), axes, axis=0, tiled=True)
    mixed, grad_tokens, grad_qkv, grad_att, grad_extra, grad_gain, grad_bias, grad_in, grad_out = layer(
        n, cap, pad, experts, heads, direct, tokens, cotangent, w_qkv, w_att, extra, full, routes.T, rel_bias.T, buckets,
        w_in[0], w_out[0])[:9]
    if not direct:
        lead = grad_qkv.shape[0] - heads // 2
        early = jnp.concatenate([grad_qkv[k] for k in range(lead)], axis=1)
        late = [grad_qkv[lead:, :, c * 128 : (c + 1) * 128].transpose(1, 0, 2).reshape(width, width) for c in range(3)]
        both = lax.psum_scatter(jnp.concatenate([early, *late], axis=1), axes, scatter_dimension=0, tiled=True)
        grad_att, grad_extra = both[:, :width], both[:, width : width + 256]
        grad_qkv = both[:, early.shape[1] :]
        grad_gain = jnp.sum(grad_qkv * w_qkv.astype(F32), axis=1, keepdims=True) / gain_attn.astype(F32)[:, None]
        grad_gain = jnp.broadcast_to(grad_gain, (own, 128))
        grad_bias = lax.psum(grad_bias, axes)
    mixed, grad_tokens, grad_in, grad_out, grad_qkv, grad_att, grad_router, grad_gain, grad_gain_moe, grad_bias = finish(
        experts, mixed, grad_tokens, grad_in, grad_out, grad_qkv, grad_att, grad_extra, grad_gain, grad_bias)
    return (
        mixed, grad_tokens, grad_gain.reshape(own), grad_qkv, grad_att, grad_bias.T, grad_gain_moe.reshape(own), grad_router.T,
        grad_in, grad_out,
    )


def solution(mesh):
    both = P(("dp", "expert"))
    return jax.shard_map(
        functools.partial(shards, mesh.shape["expert"]),
        mesh=mesh,
        in_specs=(both, both, both, P(), both, both, both, P(), both, both, P("expert"), P("expert")),
        out_specs=(both, both, both, both, both, P(), both, both, P("expert", None, "dp"), P("expert", None, "dp")),
        check_vma=False,
    )
```

```python
import functools
import jax
import jax.numpy as jnp
from jax import lax
from jax.experimental import pallas as pl
from jax.experimental.pallas import tpu as pltpu
from jax.sharding import PartitionSpec as P

MESH = pl.DeviceIdType.MESH
F32, BF16 = jnp.float32, jnp.bfloat16
NT = (((1,), (1,)), ((), ()))
EPSILON = 1e-06
PART = 384
WIDE = 768
LAG = (0, 1, 3, 5, 99, 99)


def dot(a, b, dims=(((1,), (0,)), ((), ()))):
    return lax.dot_general(a, b, dims, preferred_element_type=F32)


def exact(a, b, dims=(((1,), (0,)), ((), ()))):
    return lax.dot_general(a, b, dims, preferred_element_type=F32, precision=lax.Precision.HIGHEST)


def flipped(index, bits, count):
    result, bit = 0, 1
    while bit < count:
        result = result + bit * (((index // bit) % 2 + (bits // bit) % 2) % 2)
        bit *= 2
    return result


def gelu_parts(hidden):
    c0, c1 = 0.7978845608028654, 0.044715
    square = hidden * hidden
    bend = jnp.tanh(hidden * (c0 + (c0 * c1) * square))
    half = 0.5 + 0.5 * bend
    slope = half + (0.5 * hidden) * (1.0 - bend * bend) * (c0 + (3.0 * c0 * c1) * square)
    return hidden * half, slope


def slots_by_row(routes, me, pad, experts):
    count = routes.shape[1]
    picked = routes == lax.broadcasted_iota(jnp.int32, (experts, count), 0)
    first = lax.broadcasted_iota(jnp.int32, (count, count), 0)
    second = lax.broadcasted_iota(jnp.int32, (count, count), 1)
    before = dot(picked.astype(BF16), (first < second).astype(BF16))
    rank = jnp.sum(jnp.where(picked, before, 0.0), axis=0, keepdims=True).astype(jnp.int32)
    return jnp.bitwise_xor(routes, me) * pad + rank


def grow_strip(strip, w8):
    strip[0:8] = w8
    have = 8
    while have < strip.shape[0]:
        strip[have : 2 * have] = pltpu.roll(strip[0:have], have, 1)
        have *= 2


SPILLS = 7


def layer_kernel(n, cap, pad, experts, heads, direct, *refs):
    given, (full_hbm, buckets_hbm, win_hbm, wout_hbm), refs = refs[:7], refs[7:11], refs[11:]
    (mixed_hbm, tokens_grad_hbm, qkv_grad_hbm, *small_hbm), refs = refs[:7], refs[7:]
    (gin_hbm, gout_hbm, probs_hbm, *rest) = refs
    spilled, rest = rest[:SPILLS], rest[SPILLS:]
    (blocks, shard, gains, hot, router, rows, cots, ties, xin, cin, back_in, returned, tie_in, sib_recv,
     sib_in, in1, in2, in3, in4, bias_out, bias_in, bias_pair,
     tokens_ref, cot_ref, qkv_ref, att_ref, extra_ref, routes_ref, table_ref,
     qkv_grad_ref, att_grad_ref, extra_grad_ref, gain_grad_ref, bias_grad_ref,
     put_sem, prob_sem, load_sem, pair_sem, swap_send, swap_recv, tree_send, tree_recv, turn_send, turn_recv,
     piece_send, piece_recv, piece_out, hop_send, sib_r, r1, r2, r3, r4, bias_sem, end_sem, given_sem, small_sem) = rest
    held = (tokens_ref, cot_ref, qkv_ref, att_ref, extra_ref, routes_ref, table_ref)
    fetches = [pltpu.make_async_copy(src, dst, given_sem.at[i]) for i, (src, dst) in enumerate(zip(given, held))]
    for copy in fetches:
        copy.start()
    dp, me = lax.axis_index("dp"), lax.axis_index("expert")
    count, width = tokens_ref.shape
    total = n * pad
    early = 3 * width + 256
    per = 256 // cap
    sibling = (1 - dp, me)
    staged = per == 4
    lane = lax.broadcasted_iota(jnp.int32, (count, 128), 1)

    def peer(p):
        return dp, flipped(me, p, n)

    def remote(src, dst, send, recv, device):
        return pltpu.make_async_remote_copy(
            src_ref=src, dst_ref=dst, send_sem=send, recv_sem=recv, device_id=device, device_id_type=MESH)

    def swap(kind, p):
        src, dst = ((rows, xin), (cots, cin), (rows, back_in), (cots, returned), (ties, tie_in))[kind]
        index = p // per if kind < 2 else 0
        return remote(src.at[p], dst.at[p], swap_send.at[kind, index], swap_recv.at[kind, index], peer(p))

    def swaps(kind, g=None):
        src, dst = ((rows, xin), (cots, cin), (rows, back_in), (cots, returned), (ties, tie_in))[kind]
        index, low, blocks_of = (0, 1, n - 1) if g is None else (0, 1, per - 1) if isinstance(g, int) else (g, g * per, per)
        place = pl.ds(low, blocks_of)
        return remote(src.at[place], dst.at[place], swap_send.at[kind, index], swap_recv.at[kind, index], peer(1))

    def start_swaps(kind, wanted):
        def one(p, _):
            @pl.when(wanted(p))
            def _():
                swap(kind, p).start()
            return 0

        lax.fori_loop(1, n, one, 0)

    def greet_all(prepare):
        barrier = pltpu.get_barrier_semaphore()

        def greet(p, _):
            pl.semaphore_signal(barrier, inc=1, device_id=peer(p), device_id_type=MESH)
            return 0

        lax.fori_loop(1, n, greet, 0)
        pl.semaphore_signal(barrier, inc=1, device_id=sibling, device_id_type=MESH)
        prepare()
        pl.semaphore_wait(barrier, n)

    half = win_hbm.shape[1] // 2
    steps = half // WIDE
    pieces = [(kind, k) for k in range(steps) for kind in (0, 1)]

    def piece(kind, k):
        place = pl.ds((kind * steps + k) * WIDE, WIDE)
        return remote(blocks.at[:, place], sib_recv.at[kind, k], piece_send.at[kind, k], piece_recv.at[kind, k], sibling)

    def out_piece(kind, k):
        return pltpu.make_async_copy(
            sib_recv.at[kind, k], (gin_hbm, gout_hbm)[kind].at[:, pl.ds(k * WIDE, WIDE)], piece_out.at[kind, k])

    def forward(w, packed, normed, attended, middle, moe_in, chance, probs, strip, bias, ends, weights):
        puts = []

        def put(index, src):
            copy = pltpu.make_async_copy(src, spilled[index], put_sem.at[index])
            copy.start()
            puts.append(copy)

        offsets = [pltpu.make_async_copy(buckets_hbm.at[:, pl.ds(c, 128)], ends.at[i], load_sem.at[i])
                   for i, c in enumerate((0, count - 128))]
        for copy in offsets:
            copy.start()
        def prepare():
            for copy in fetches:
                copy.wait()
            if direct:
                weights[:, : 3 * width] = qkv_ref[...].astype(F32)
                weights[:, 3 * width : early] = extra_ref[...].T[: weights.shape[0]]
                weights[:, early:] = att_ref[...].astype(F32)

        greet_all(prepare)
        if direct:
            own = weights.shape[0]
            block = 2 * own
            pair = remote(weights, shard, pair_sem.at[0], pair_sem.at[1], sibling)
            pair.start()
        else:
            load = pltpu.make_async_copy(full_hbm, w, pair_sem.at[0])
            load.start()
        slots = slots_by_row(routes_ref[...], me, pad, experts)

        def to_slots(values):
            hits = (slots == lax.broadcasted_iota(jnp.int32, (total, count), 0)).astype(BF16)
            return dot(hits, values).astype(BF16).reshape(n, pad, width)

        def make_cots():
            cots[...] = to_slots(cot_ref[...])
            cin[0] = cots[0]

        def make_bias():
            for copy in offsets:
                copy.wait()
            last, first = ends[1].astype(F32).T[127:128], ends[0].astype(F32).T[0:1]
            line = jnp.concatenate([last, pltpu.roll(first, count - 1, 1)], axis=1)
            line = pltpu.roll(jnp.broadcast_to(line, (8, 2 * count)), 2 * count - 127, 1)[0:1]
            hot[...] = (line.astype(jnp.int32) == lax.broadcasted_iota(jnp.int32, hot.shape, 0)).astype(F32)
            table = exact(table_ref[...], hot[...])
            for h in range(heads):
                row = jnp.broadcast_to(table[h : h + 1], (8, 2 * count))
                place = lax.broadcasted_iota(jnp.int32, row.shape, 0)
                shifted = row
                for r in range(1, 8):
                    shifted = jnp.where(place == r, pltpu.roll(row, r, 1), shifted)
                bias[h] = shifted

        if direct:
            pair.wait()
            mine, other = weights[...], shard[...]
            blocks[pl.ds(pl.multiple_of(me * block, 16), block), : w.shape[1]] = jnp.concatenate(
                [jnp.where(dp == 0, mine, other), jnp.where(dp == 0, other, mine)], axis=0).astype(BF16)
            second, third = 2 - dp, 1 + dp
            far = list(range(4, n, 4))
            near = [0] + far

            def at(t, r, core):
                start, size = ((0, early // 2), (early, width // 2))[t]
                return blocks.at[pl.ds(pl.multiple_of(flipped(me, r, n) * block, 16), block),
                                 pl.ds(pl.multiple_of(start + core * size, 128), size)]

            def hop(t, r, step):
                return remote(at(t, r, dp), at(t, r, dp), tree_send.at[t], tree_recv.at[t, r + step], peer(step))

            def arrived(t, r):
                remote(at(t, r, dp), at(t, r, dp), tree_send.at[t], tree_recv.at[t, r], peer(r)).wait_recv()

            def to_sibling(t, r, core):
                return remote(at(t, r, core), at(t, r, core), turn_send.at[t], turn_recv.at[t], sibling)

            def bulk(t, send, recv):
                place = blocks.at[: (n - 1) * block, : (early // 2, width // 2)[t]]
                return remote(place, place, send.at[t], recv.at[t] if recv is turn_recv else recv.at[t, 0], sibling)

            def turn(t, step):
                if step == 0:
                    hop(t, 0, 8).start()
                    hop(t, 0, 4).start()
                    hop(t, 0, third).start()
                    hop(t, 0, second).start()
                elif step == 1:
                    for r in (8, 4, 12):
                        arrived(t, r)
                        if r == 8:
                            hop(t, 8, 4).start()
                        hop(t, r, third).start()
                        hop(t, r, second).start()
                        to_sibling(t, r, dp).start()
                elif step == 2:
                    for r in near:
                        arrived(t, r + second)
                        hop(t, r + second, third).start()
                        to_sibling(t, r + second, dp).start()
                elif step == 3:
                    for r in near:
                        arrived(t, r + third)
                        to_sibling(t, r + third, dp).start()
                        arrived(t, r + 3)
                        to_sibling(t, r + 3, dp).start()
                else:
                    bulk(t, turn_send, turn_recv).wait_recv()
                    place = (slice(0, early), slice(early, w.shape[1]))[t]
                    for core in (0, 1):
                        for q in range(n // 2):
                            low = 2 * q * block + core * own
                            pair_rows = [blocks[p : p + own, place].astype(F32) for p in (low, low + block)]
                            w[core * own * n + q * block : core * own * n + (q + 1) * block, place] = jnp.concatenate(
                                pair_rows, axis=0).astype(BF16)

            turn(0, 0)
            make_bias()
            make_cots()
            turn(0, 1)
            turn(1, 0)
            start_swaps(1, lambda p: p % 4 == 0)
            turn(0, 2)
            turn(1, 1)
            turn(0, 3)
            turn(1, 2)
            start_swaps(1, lambda p: p % 4 != 0)
            turn(0, 4)
        else:
            make_bias()
            make_cots()
            start_swaps(1, lambda p: p > 0)
            load.wait()
        gains[...] = w[:, 3 * width + 128 : early].astype(F32).T[0:8]
        router[...] = w[:, 3 * width : 3 * width + 128]
        x = tokens_ref[...].astype(F32)
        normed[...] = (x * lax.rsqrt(jnp.mean(x * x, axis=1, keepdims=True) + EPSILON) * gains[0:1]).astype(BF16)
        put(0, normed)
        for c in range(3):
            cols_c = slice(c * width, (c + 1) * width)
            packed[:, cols_c] = dot(normed[...], w[:, cols_c]).astype(BF16)
        put(1, packed)
        scale = (width // heads) ** -0.5

        def put_probs(k):
            return pltpu.make_async_copy(probs.at[pl.ds(2 * k, 2)], probs_hbm.at[pl.ds(2 * k, 2)], prob_sem.at[0])

        def attend(k, _):
            def part(c):
                return packed[:, pl.ds(pl.multiple_of(c * width + k * 128, 128), 128)]

            queries = (part(0).astype(F32) * scale).astype(BF16)
            keys = part(1)
            values = part(2).astype(F32).T.astype(BF16)
            outs = []
            for h in (0, 1):
                grow_strip(strip, bias[2 * k + h])
                own_keys = jnp.where((lane < 64) == (h == 0), keys, jnp.zeros_like(keys))
                scores = dot(own_keys, queries, NT)
                scores = jnp.concatenate(
                    [scores[128 * b : 128 * b + 128] + strip[:, 384 - 128 * b : 896 - 128 * b] for b in range(4)], axis=0)
                powers = jnp.exp(scores - jnp.max(scores, axis=0, keepdims=True))
                part_weights = (powers * (1.0 / jnp.sum(powers, axis=0, keepdims=True))).astype(BF16)
                probs[2 * k + h] = part_weights
                outs.append(dot(values[64 * h : 64 * h + 64], part_weights))
            put_probs(k).start()
            attended[:, pl.ds(pl.multiple_of(k * 128, 128), 128)] = jnp.concatenate(outs, axis=0).T.astype(BF16)
            if direct:
                for step in (3, 4):
                    @pl.when(k == step + 1)
                    def _():
                        turn(1, step)
            return 0

        lax.fori_loop(0, heads // 2, attend, 0)
        mid = tokens_ref[...].astype(F32) + dot(attended[...], w[:, early:])
        middle[...] = mid
        moe = (mid * lax.rsqrt(jnp.mean(mid * mid, axis=1, keepdims=True) + EPSILON) * gains[1:2]).astype(BF16)
        moe_in[...] = moe
        rows[...] = to_slots(moe)
        start_swaps(0, lambda p: (p < 4) | ((p % 4 == 0) & (p < 12)) if staged else p > 0)
        xin[0] = rows[0]
        put(2, attended)
        put(3, middle)
        put(4, moe_in)
        put(5, w)
        logits = dot(moe, router[...])
        logits = jnp.where(lane < experts, logits, -1e30)
        powers = jnp.exp(logits - jnp.max(logits, axis=1, keepdims=True))
        chance[...] = powers / jnp.sum(powers, axis=1, keepdims=True)
        put(6, chance)
        if direct:
            for t in (0, 1):
                bulk(t, tree_send, tree_recv).wait_send()
                bulk(t, turn_send, turn_recv).wait_send()
        for copy in puts:
            copy.wait()
        pltpu.make_async_copy(probs, probs_hbm, prob_sem.at[0]).wait()

    def experts_both(win, wout, xt, rt, act, hgr):
        ff = win.shape[1]
        group_rows = per * cap
        chunk = 1024
        loads = [pltpu.make_async_copy(win_hbm, win, load_sem.at[0]), pltpu.make_async_copy(wout_hbm, wout, load_sem.at[1])]
        for load in loads:
            load.start()

        def packed_rows(ref, g):
            block = ref[pl.ds(g * per, per)].reshape(per * pad, width)
            if pad == cap:
                return block
            r = lax.broadcasted_iota(jnp.int32, (group_rows, per * pad), 0)
            c = lax.broadcasted_iota(jnp.int32, (group_rows, per * pad), 1)
            return dot(((r // cap) * pad + r % cap == c).astype(BF16), block).astype(BF16)

        def spread_rows(block):
            if pad == cap:
                return block.reshape(per, pad, width)
            r = lax.broadcasted_iota(jnp.int32, (per * pad, group_rows), 0)
            c = lax.broadcasted_iota(jnp.int32, (per * pad, group_rows), 1)
            pick = (r // pad == c // cap) & (r % pad == c % cap)
            return dot(pick.astype(BF16), block).astype(BF16).reshape(per, pad, width)

        def group(g, _):
            def over(act_on):
                def one(j, _):
                    @pl.when(g * per + j != 0)
                    def _():
                        act_on(g * per + j)
                    return 0

                lax.fori_loop(0, per, one, 0)

            def all_of(kind, act_on):
                @pl.when(g == 0)
                def _():
                    act_on(swaps(kind, 0))

                @pl.when(g != 0)
                def _():
                    act_on(swaps(kind, g))

            all_of(0, lambda copies: copies.wait_recv())

            @pl.when(g == 0)
            def _():
                if staged:
                    start_swaps(0, lambda p: (p >= 4) & (p % 4 != 0) & (p < 12))
                for load in loads:
                    load.wait()

            if staged:
                @pl.when(g == 1)
                def _():
                    start_swaps(0, lambda p: p >= 12)

            all_of(1, lambda copies: copies.wait_recv())
            here = pl.ds(pl.multiple_of(g * group_rows, group_rows), group_rows)
            x = packed_rows(xin, g)
            logits = dot(x, router[...])
            lanes = lax.broadcasted_iota(jnp.int32, logits.shape, 1)
            logits = jnp.where(lanes < experts, logits, -1e30)
            powers = jnp.exp(logits - jnp.max(logits, axis=1, keepdims=True))
            gate = jnp.sum(jnp.where(lanes == me, powers, 0.0), axis=1, keepdims=True) / jnp.sum(
                powers, axis=1, keepdims=True)
            r = (gate * packed_rows(cin, g).astype(F32)).astype(BF16)
            xt[:, here] = x.T
            rt[:, here] = r.T

            def hidden_chunk(k, _):
                cols = pl.ds(pl.multiple_of(k * chunk, chunk), chunk)
                value, slope = gelu_parts(dot(x, win[:, cols]))
                act[here, cols] = value.astype(BF16)
                hgr[here, cols] = (dot(r, wout[:, cols]) * slope).astype(BF16)
                return 0

            lax.fori_loop(0, ff // chunk, hidden_chunk, 0)
            back = spread_rows(dot(hgr[here], win[...], NT).astype(BF16))
            all_of(0, lambda copies: copies.wait_send())
            rows[pl.ds(g * per, per)] = back
            over(lambda p: swap(2, p).start())
            produced = dot(act[here], wout[...], NT).astype(BF16)
            tie = jnp.sum(r.astype(F32) * produced.astype(F32), axis=1, keepdims=True)
            for j in range(per):
                row = jnp.broadcast_to(tie[j * cap : (j + 1) * cap], (cap, 128)).T[0:8]
                ties[g * per + j] = jnp.concatenate([row, jnp.zeros((8, 128 - cap), F32)], axis=1)
            over(lambda p: swap(4, p).start())
            all_of(1, lambda copies: copies.wait_send())
            cots[pl.ds(g * per, per)] = spread_rows(produced)

            @pl.when(g < n // per // 2)
            def _():
                over(lambda p: swap(3, p).start())

            return 0

        lax.fori_loop(0, n // per, group, 0)
        back_in[0] = rows[0]
        tie_in[0] = ties[0]
        returned[0] = cots[0]

        def partial(kind, owner, k):
            cols = pl.ds(pl.multiple_of(owner * half + k * WIDE, 128), WIDE)
            return dot(xt[...], hgr[:, cols]) if kind == 0 else dot(rt[...], act[:, cols])

        for kind, k in pieces:
            place = (kind * steps + k) * WIDE
            blocks[:, place : place + WIDE] = partial(kind, 1 - dp, k).astype(BF16)
            piece(kind, k).start()
        for kind, k in pieces:
            value = partial(kind, dp, k)
            piece(kind, k).wait_recv()
            sib_recv[kind, k] = (value + sib_recv[kind, k].astype(F32)).astype(BF16)
            out_piece(kind, k).start()

    def backward(w, packed, normed, attended, middle, moe_in, chance, prob, mid_grad, att_cot, packed_grad, normed_t, chunk,
                 strip, bias_rows, mine, keep, out1, out2, out3, out4):
        loaded = (normed, packed, attended, middle, moe_in, w, chance)
        loads = [pltpu.make_async_copy(spilled[i], loaded[i], load_sem.at[i]) for i in range(SPILLS)]
        order = (6, 3, 5, 2, 4, 0, 1)
        for i in order:
            loads[i].start()

        def fetch(k):
            return pltpu.make_async_copy(probs_hbm.at[pl.ds(2 * k, 2)], prob.at[k % 2], prob_sem.at[k % 2])

        fetch(0).start()
        own = qkv_ref.shape[0]
        lead = (width + 256 + PART - 1) // PART
        chunks = lead + heads // 2

        if direct:
            half_rows = own * n

            steps_out = ((out1, in1, r1), (out2, in2, r2), (out3, in3, r3), (out4, in4, r4))
            ways = (1 + dp, 2 - dp, 4, 8)

            def sib_out(k):
                across = blocks.shape[1] // PART
                return blocks.at[pl.ds(pl.multiple_of((k // across) * half_rows, 16), half_rows),
                                 pl.ds(pl.multiple_of((k % across) * PART, 128), PART)]

            def hop(stage, k):
                if stage == 0:
                    return remote(sib_out(k), sib_in.at[k], hop_send.at[0], sib_r.at[k], sibling)
                src, dst, recv = steps_out[stage - 1]
                return remote(src.at[k], dst.at[k], hop_send.at[stage], recv.at[k], peer(ways[stage - 1]))

            def unit(k, u):
                r = ways[0] * (u // 4) + ways[1] * ((u // 2) % 2) + ways[2] * (u % 2)
                places = [pl.multiple_of(flipped(me, r + z, n) * own, 8) for z in (0, ways[3])]
                return jnp.concatenate([mine[k % 2, pl.ds(place, own)] for place in places], axis=0)

            def stage(s, k):
                if s == 0:
                    there = pl.ds(pl.multiple_of((1 - dp) * half_rows, 8), half_rows)
                    here = pl.ds(pl.multiple_of(dp * half_rows, 8), half_rows)
                    sib_out(k)[...] = chunk[there].astype(BF16)
                    hop(0, k).start()
                    mine[k % 2] = chunk[here]
                elif s == 1:
                    hop(0, k).wait_recv()
                    mine[k % 2] = mine[k % 2] + sib_in[k].astype(F32)
                    for u in range(4):
                        out1[k, 2 * own * u : 2 * own * (u + 1)] = unit(k, u + 4).astype(BF16)
                    hop(1, k).start()
                    for u in range(4):
                        keep[k, 2 * own * u : 2 * own * (u + 1)] = unit(k, u)
                elif s in (2, 3):
                    src, dst = steps_out[s - 1][0], steps_out[s - 2][1]
                    left = 8 * own // (1 << (s - 1))
                    hop(s - 1, k).wait_recv()
                    value = keep[k, : 2 * left] + dst[k].astype(F32)
                    src[k] = value[left:].astype(BF16)
                    hop(s, k).start()
                    keep[k, :left] = value[:left]
                elif s == 4:
                    hop(3, k).wait_recv()
                    value = keep[k, : 2 * own] + in3[k].astype(F32)
                    out4[k] = jnp.concatenate(
                        [value[own:, 128 * c : 128 * (c + 1)] for c in range(3)]
                        + [jnp.zeros((out4.shape[1] - 3 * own, 128), F32)], axis=0).astype(BF16)
                    hop(4, k).start()
                    keep[k, :own] = value[:own]
                else:
                    hop(4, k).wait_recv()
                    far = in4[k].astype(F32)
                    keep[k, :own] = keep[k, :own] + jnp.concatenate(
                        [far[own * c : own * (c + 1)] for c in range(3)], axis=1)

            def advance(k):
                stage(0, k)
                for s in range(1, 6):
                    @pl.when((k - LAG[s] >= 0) & (k - LAG[s] < chunks))
                    def _():
                        stage(s, k - LAG[s])

            done = {k: max(s for s in range(6) if LAG[s] <= chunks - 1 - k) for k in range(chunks)}

            def drain(last, *which):
                for k in which or range(chunks):
                    while done[k] < last:
                        done[k] += 1
                        stage(done[k], k)

        else:
            def advance(k):
                copy = pltpu.make_async_copy(chunk, qkv_grad_hbm.at[k], end_sem.at[0])
                copy.start()
                copy.wait()

            def drain(*_):
                pass

        expert_of = jnp.broadcast_to(routes_ref[...].astype(F32), (128, count)).T[:, 0:1].astype(jnp.int32)
        picked = expert_of == lane
        first = lax.broadcasted_iota(jnp.int32, (count, count), 0)
        other = lax.broadcasted_iota(jnp.int32, (count, count), 1)
        before = dot((other < first).astype(BF16), picked.astype(BF16))
        rank = jnp.sum(jnp.where(picked, before, 0.0), axis=1, keepdims=True).astype(jnp.int32)
        place = jnp.bitwise_xor(expert_of, me)
        hits = (place * pad + rank == lax.broadcasted_iota(jnp.int32, (count, total), 1)).astype(BF16)

        def each_peer(act_on):
            def one(p, _):
                act_on(p)
                return 0

            lax.fori_loop(1, n, one, 0)

        for kind, k in pieces:
            piece(kind, k).wait_send()
        swaps(2).wait_recv()
        swaps(4).wait_recv()
        ties_row = exact((place == lax.broadcasted_iota(jnp.int32, (count, n), 1)).astype(F32), jnp.max(tie_in[...], axis=1))
        tie = jnp.sum(jnp.where(lane == rank, ties_row, 0.0), axis=1, keepdims=True)
        for i in order[:1]:
            loads[i].wait()
        logit_grad = (tie * (picked.astype(F32) - chance[...])).astype(BF16)
        grad = dot(hits, back_in[...].reshape(total, width))
        for i in order[1:]:
            loads[i].wait()
        grad = grad + dot(logit_grad, router[...], NT)
        mid = middle[...]
        root = lax.rsqrt(jnp.mean(mid * mid, axis=1, keepdims=True) + EPSILON)
        unit_mid = mid * root
        gain_rows = jnp.sum(grad * unit_mid, axis=0, keepdims=True)
        scaled = grad * gains[1:2]
        mid_g = cot_ref[...].astype(F32) + root * (scaled - unit_mid * jnp.mean(scaled * unit_mid, axis=1, keepdims=True))
        mid_grad[...] = mid_g
        attn_grad = mid_g.astype(BF16)
        att_cot[...] = dot(attn_grad, w[:, early:], NT).astype(BF16)
        attended_t = attended[...].T
        for k in range(lead):
            if (k + 1) * PART <= width:
                chunk[...] = dot(attended_t, attn_grad[:, k * PART : (k + 1) * PART])
            else:
                chunk[:, 0:128] = dot(moe_in[...].T, logit_grad)
                chunk[:, 128:256] = jnp.broadcast_to(gain_rows, (128, width)).T
                chunk[:, 256:] = jnp.zeros((width, PART - 256), F32)
            advance(k)
        normed_t[...] = normed[...].T
        swaps(2).wait_send()
        start_swaps(3, lambda p: (p >= n // 2) & (p % 4 == 0))

        scale = (width // heads) ** -0.5

        def attend_back(k, _):
            fetch(k).wait()

            @pl.when(k + 1 < heads // 2)
            def _():
                fetch(k + 1).start()

            def part(c):
                return packed[:, pl.ds(pl.multiple_of(c * width + k * 128, 128), 128)]

            queries, keys, values = part(0), part(1), part(2)
            keys_t = (keys.astype(F32) * scale).T.astype(BF16)
            cot = att_cot[:, pl.ds(pl.multiple_of(k * 128, 128), 128)]
            query_t, key_g, value_g = [], None, None
            for h in (0, 1):
                mask = (lane < 64) == (h == 0)
                own_cot = jnp.where(mask, cot, jnp.zeros_like(cot))
                own_queries = jnp.where(mask, queries, jnp.zeros_like(queries))
                weights = prob[k % 2, h]
                chances = weights.astype(F32)
                product = chances * dot(values, own_cot, NT)
                score_grad = (product - chances * jnp.sum(product, axis=0, keepdims=True)).astype(BF16)
                wide = score_grad.astype(F32)
                for b in range(4):
                    block = wide[128 * b : 128 * b + 128]
                    cols = slice(384 - 128 * b, 896 - 128 * b)
                    if b == 0:
                        strip[:, cols] = block
                        strip[:, 0:384] = jnp.zeros((128, 384), F32)
                        strip[:, 896:1024] = jnp.zeros((128, 128), F32)
                    else:
                        strip[:, cols] += block
                have = 64
                folded = strip[...]
                while have >= 8:
                    folded = folded[:have] + pltpu.roll(folded[have:], 1024 - have, 1)
                    have //= 2
                for s in range(1, 8):
                    folded = jnp.where(lax.broadcasted_iota(jnp.int32, folded.shape, 0) == s,
                                       pltpu.roll(folded, 1024 - s, 1), folded)
                bias_rows[2 * k + h] = folded
                v = dot(weights, own_cot)
                q = dot(score_grad, own_queries)
                value_g = v if h == 0 else value_g + v
                key_g = q if h == 0 else key_g + q
                query_t.append(dot(keys_t[64 * h : 64 * h + 64], score_grad))
            query_g = jnp.concatenate(query_t, axis=0).T.astype(BF16)
            grads = jnp.concatenate([query_g, (key_g * scale).astype(BF16), value_g.astype(BF16)], axis=1)
            for c in range(3):
                packed_grad[:, pl.ds(pl.multiple_of(c * width + k * 128, 128), 128)] = grads[:, c * 128 : (c + 1) * 128]
            chunk[...] = dot(normed_t[...], grads)
            advance(k + lead)

            @pl.when(k ==  0)
            def _():
                start_swaps(3, lambda p: (p >= n // 2) & (p % 4 == 1))

            @pl.when(k ==  0)
            def _():
                start_swaps(3, lambda p: (p >= n // 2) & (p % 4 == 2))

            @pl.when(k ==  1)
            def _():
                start_swaps(3, lambda p: (p >= n // 2) & (p % 4 == 3))

            return 0

        lax.fori_loop(0, heads // 2, attend_back, 0)
        drain(1, chunks - 1)
        drain(2, *range(chunks - 1))
        drain(3, *range(chunks - 3))
        sums = jnp.concatenate([jnp.sum(bias_rows[h], axis=0, keepdims=True) for h in range(heads)], axis=0)
        bias_out[...] = exact(sums, hot[...], NT)
        if direct:
            pair_hop = remote(bias_out, bias_pair, pair_sem.at[2], pair_sem.at[3], sibling)
            pair_hop.start()

            def bias_hop(p):
                return remote(bias_in.at[me], bias_in.at[me], bias_sem.at[0], bias_sem.at[1], peer(p))

            place = bias_in.at[1:]
            bias_all = remote(place, place, bias_sem.at[0], bias_sem.at[1], peer(1))

        normed_grad = dot(packed_grad[...], w[:, : 3 * width], NT)
        drain(2)
        drain(3, *range(chunks - 1))
        drain(4, *range(chunks - 4))
        if direct:
            pair_hop.wait()
            bias_in[me] = bias_out[...] + bias_pair[...]
            each_peer(lambda p: bias_hop(p).start())
        x = tokens_ref[...].astype(F32)
        root = lax.rsqrt(jnp.mean(x * x, axis=1, keepdims=True) + EPSILON)
        unit_x = x * root
        scaled = normed_grad * gains[0:1]
        mid_grad[...] = mid_grad[...] + root * (scaled - unit_x * jnp.mean(scaled * unit_x, axis=1, keepdims=True))
        ends = [pltpu.make_async_copy(mid_grad, tokens_grad_hbm, end_sem.at[0]),
                pltpu.make_async_copy(att_cot, mixed_hbm, end_sem.at[1])]
        ends[0].start()
        drain(3)
        drain(4, *range(chunks - 1))
        swaps(3).wait_recv()
        gate = jnp.sum(jnp.where(picked, chance[...], 0.0), axis=1, keepdims=True)
        att_cot[...] = (middle[...] + gate * dot(hits, returned[...].reshape(total, width))).astype(BF16)
        ends[1].start()
        if direct:
            drain(4)
            drain(5)
            bias_all.wait_recv()
            total_bias = bias_in[0]
            for p in range(1, n):
                total_bias = total_bias + bias_in[p]
            bias_grad_ref[...] = total_bias
            for k in range(chunks):
                result = keep[k, :own]
                if k >= lead:
                    for c in range(3):
                        start = c * width + (k - lead) * 128
                        qkv_grad_ref[:, start : start + 128] = result[:, c * 128 : (c + 1) * 128]
                elif (k + 1) * PART <= width:
                    att_grad_ref[:, k * PART : (k + 1) * PART] = result
                else:
                    extra_grad_ref[...] = result[:, :256]
            total_gain = jnp.sum(qkv_grad_ref[...] * qkv_ref[...].astype(F32), axis=1, keepdims=True)
            gain_grad_ref[...] = jnp.broadcast_to(total_gain / extra_ref[128:256].T[:own, 0:1], gain_grad_ref.shape)

            for s, sent in enumerate((sib_in, out1, out2, out3, out4)):
                remote(sent, sent, hop_send.at[s], sib_r.at[0], sibling).wait_send()
            bias_all.wait_send()
        else:
            bias_grad_ref[...] = bias_out[...]
        small = [*zip((att_grad_ref, extra_grad_ref, gain_grad_ref, bias_grad_ref), small_hbm)]
        if direct:
            small.append((qkv_grad_ref, qkv_grad_hbm))
        for i, (src, dst) in enumerate(small):
            ends.append(pltpu.make_async_copy(src, dst, small_sem.at[i]))
            ends[-1].start()
        for kind in (3, 4):
            swaps(kind).wait_send()
        for copy in ends:
            copy.wait()
        for kind, k in pieces:
            out_piece(kind, k).wait()

    wide = w_columns(width)
    scratch = pltpu.VMEM
    shared = [
        scratch((width, wide), BF16), scratch((count, 3 * width), BF16), scratch((count, width), BF16),
        scratch((count, width), BF16), scratch((count, width), F32), scratch((count, width), BF16), scratch((count, 128), F32),
    ]
    own_rows = qkv_ref.shape[0]
    pl.run_scoped(
        forward, *shared, scratch((heads, count, count), BF16), scratch((128, 2 * count), F32),
        scratch((heads, 8, 2 * count), F32), scratch((2, count, 128), jnp.int32),
        scratch((own_rows, wide) if direct else (8, 128), F32))
    pl.run_scoped(
        experts_both, *[scratch((width, win_hbm.shape[1]), BF16) for _ in range(2)],
        *[scratch((width, n * cap), BF16) for _ in range(2)], *[scratch((n * cap, win_hbm.shape[1]), BF16) for _ in range(2)])
    all_chunks = (width + 256 + PART - 1) // PART + heads // 2

    def buffer(shape, kind):
        return scratch((all_chunks, *shape) if direct else (8, 128), kind)

    pl.run_scoped(
        backward, *shared, scratch((2, 2, count, count), BF16), scratch((count, width), F32), scratch((count, width), BF16),
        scratch((count, 3 * width), BF16), scratch((width, count), BF16), scratch((width, PART), F32),
        scratch((128, 2 * count), F32), scratch((heads, 8, 2 * count), F32),
        scratch((2, own_rows * n, PART), F32), buffer((8 * own_rows, PART), F32),
        *[buffer((own_rows << s, PART), BF16) for s in (3, 2, 1)], buffer((-(-3 * own_rows // 16) * 16, 128), BF16))


def w_columns(width):
    return 4 * width + 256


def layer(n, cap, pad, experts, heads, direct, tokens, cotangent, qkv, att, extra, full, routes, table, buckets, win, wout):
    count, width = tokens.shape
    wide = w_columns(width)
    own = qkv.shape[0]
    kinds = table.shape[1]
    ff = win.shape[1]
    chunks = (width + 256 + PART - 1) // PART + heads // 2
    steps = ff // 2 // WIDE
    short = -(-3 * own // 16) * 16
    any_ = pl.BlockSpec(memory_space=pl.ANY)
    dma = pltpu.SemaphoreType.DMA
    scratch = pltpu.VMEM
    shape = jax.ShapeDtypeStruct

    def landing(*rest):
        return scratch((chunks, *rest) if direct else (16, 128), BF16)

    small = ((own, width), (own, 256), (own, 128), (heads, kinds))
    outs = [
        (shape((count, width), BF16), any_), (shape((count, width), F32), any_),
        (shape((own, 3 * width) if direct else (chunks, width, PART), F32), any_),
        *[(shape(dims, F32), any_) for dims in small], (shape((width, ff // 2), BF16), any_), (shape((width, ff // 2), BF16), any_),
        (shape((heads, count, count), BF16), any_), (shape((count, width), BF16), any_),
        (shape((count, 3 * width), BF16), any_), (shape((count, width), BF16), any_), (shape((count, width), F32), any_),
        (shape((count, width), BF16), any_), (shape((width, wide), BF16), any_), (shape((count, 128), F32), any_),
    ]
    slots = scratch((n, pad, width), BF16)
    given = (tokens, cotangent, qkv, att, extra, routes, table)
    return pl.pallas_call(
        functools.partial(layer_kernel, n, cap, pad, experts, heads, direct),
        out_shape=tuple(o[0] for o in outs),
        in_specs=[any_] * 11,
        out_specs=tuple(o[1] for o in outs),
        scratch_shapes=[
            scratch((width, max(wide, 2 * steps * WIDE)), BF16),
            scratch((own, wide) if direct else (8, 128), F32),
            scratch((8, width), F32), scratch((kinds, 2 * count), F32), scratch((width, 128), BF16),
            slots, slots, scratch((n, 8, 128), F32), slots, slots, slots, slots, scratch((n, 8, 128), F32),
            scratch((2, steps, width, WIDE), BF16),
            landing(own * n, PART), *[landing(own << s, PART) for s in (3, 2, 1)], landing(short, 128),
            scratch((heads, kinds), F32), scratch((n, heads, kinds), F32), scratch((heads, kinds), F32),
            *[scratch(a.shape, a.dtype) for a in given], scratch((own, 3 * width), F32), *[scratch(dims, F32) for dims in small],
            dma((SPILLS,)), dma((2,)), dma((SPILLS,)), dma((4,)), dma((5, n * cap // 256)), dma((5, n * cap // 256)),
            dma((2,)), dma((2, n)), dma((2,)), dma((2,)),
            dma((2, steps)), dma((2, steps)), dma((2, steps)),
            dma((5,)), *[dma((chunks,)) for _ in range(5)], dma((2,)), dma((2,)), dma((7,)), dma((5,)),
        ],
        compiler_params=pltpu.CompilerParams(
            collective_id=1, has_side_effects=True, vmem_limit_bytes=63 * 1024 * 1024),
        name="layer",
    )(*given, full, buckets, win, wout)


def finish_kernel(
    mixed_in, tokens_in, in_hbm, out_hbm, *refs,
):
    small_ins, (mixed_out, tokens_out, in_out, out_out), small_outs, refs = refs[:5], refs[5:9], refs[9:15], refs[15:]
    (mixed, tokens, narrow, wide, sem, load_sem, store_sem, small_sem) , held = refs[:8], refs[8:]
    fetches = [pltpu.make_async_copy(src, dst, small_sem.at[i]) for i, (src, dst) in enumerate(zip(small_ins, held[:5]))]
    leaves = [pltpu.make_async_copy(src, dst, small_sem.at[5 + i]) for i, (src, dst) in enumerate(zip(held[5:], small_outs))]
    qkv_in, att_in, extra_in, gain_in, bias_in, qkv_out, att_out, router_out, gain_out, gain_moe_out, bias_out = held
    for copy in fetches:
        copy.start()
    ins = [pltpu.make_async_copy(mixed_in, mixed, sem.at[0]), pltpu.make_async_copy(tokens_in, tokens, sem.at[1])]
    outs = [pltpu.make_async_copy(mixed, mixed_out, sem.at[2]), pltpu.make_async_copy(tokens, tokens_out, sem.at[3])]
    parts, rows = narrow.shape[1], narrow.shape[2]

    def load(kind, k):
        return pltpu.make_async_copy(
            (in_hbm, out_hbm)[kind].at[pl.ds(k * rows, rows)], narrow.at[kind, k], load_sem.at[kind, k])

    def store(kind, k):
        return pltpu.make_async_copy(
            wide.at[kind, k], (in_out, out_out)[kind].at[0, pl.ds(k * rows, rows)], store_sem.at[kind, k])

    for k in range(parts):
        for kind in (0, 1):
            load(kind, k).start()
    for copy in ins:
        copy.start()
    for k in range(parts):
        for kind in (0, 1):
            load(kind, k).wait()
            wide[kind, k] = narrow[kind, k].astype(F32)
            store(kind, k).start()
    for copy in fetches:
        copy.wait()
    qkv_out[...] = qkv_in[...]
    att_out[...] = att_in[...]
    router_out[...] = extra_in[:, :128].T[: router_out.shape[0]]
    gain_out[...] = gain_in[...].T[0:1]
    gain_moe_out[...] = extra_in[:, 128:].T[0:1]
    bias_out[...] = bias_in[...]
    for copy in leaves:
        copy.start()
    for copy_in, copy_out in zip(ins, outs):
        copy_in.wait()
        copy_out.start()
    for k in range(parts):
        for kind in (0, 1):
            store(kind, k).wait()
    for copy in outs + leaves:
        copy.wait()


def finish(experts, mixed, tokens_grad, grad_in, grad_out, qkv, att, extra, gain, bias):
    any_ = pl.BlockSpec(memory_space=pl.ANY)
    dma = pltpu.SemaphoreType.DMA
    parts = 8
    rows = grad_in.shape[0] // parts
    own = qkv.shape[0]
    shape = jax.ShapeDtypeStruct
    small = (qkv.shape, att.shape, (experts, own), (1, own), (1, own), bias.shape)
    return pl.pallas_call(
        finish_kernel,
        out_shape=(
            shape(mixed.shape, BF16), shape(tokens_grad.shape, F32), shape((1, *grad_in.shape), F32),
            shape((1, *grad_out.shape), F32), *[shape(dims, F32) for dims in small],
        ),
        in_specs=[any_] * 9,
        out_specs=tuple([any_] * 10),
        scratch_shapes=[
            pltpu.VMEM(mixed.shape, BF16),
            pltpu.VMEM(tokens_grad.shape, F32),
            pltpu.VMEM((2, parts, rows, grad_in.shape[1]), BF16),
            pltpu.VMEM((2, parts, rows, grad_in.shape[1]), F32),
            dma((4,)), dma((2, parts)), dma((2, parts)), dma((11,)),
            *[pltpu.VMEM(dims, F32) for dims in (*[a.shape for a in (qkv, att, extra, gain, bias)], *small)],
        ],
        compiler_params=pltpu.CompilerParams(vmem_limit_bytes=60 * 1024 * 1024),
        name="finish",
    )(mixed, tokens_grad, grad_in, grad_out, qkv, att, extra, gain, bias)


def shards(
    n, tokens, cotangent, routes, buckets, gain_attn, w_qkv, w_att, rel_bias, gain_moe, w_router, w_in, w_out,
):
    axes = ("dp", "expert")
    count, width = tokens.shape
    experts = w_router.shape[1]
    heads = rel_bias.shape[1]
    own = w_qkv.shape[0]
    cap = max(2, 2 * count // experts)
    pad = max(16, cap)
    direct = n == 16 and own % 8 == 0
    extra = sum(jnp.pad(part.astype(F32), ((low, 256 - low - part.shape[0]), (0, 128 - own)))
                for low, part in ((0, w_router.T), (128, gain_attn[None]), (129, gain_moe[None])))
    full = w_att if direct else lax.all_gather(
        jnp.concatenate([w_qkv, extra[:, :own].T.astype(BF16), w_att], axis=1), axes, axis=0, tiled=True)
    mixed, grad_tokens, grad_qkv, grad_att, grad_extra, grad_gain, grad_bias, grad_in, grad_out = layer(
        n, cap, pad, experts, heads, direct, tokens, cotangent, w_qkv, w_att, extra, full, routes.T, rel_bias.T, buckets,
        w_in[0], w_out[0])[:9]
    if not direct:
        lead = grad_qkv.shape[0] - heads // 2
        early = jnp.concatenate([grad_qkv[k] for k in range(lead)], axis=1)
        late = [grad_qkv[lead:, :, c * 128 : (c + 1) * 128].transpose(1, 0, 2).reshape(width, width) for c in range(3)]
        both = lax.psum_scatter(jnp.concatenate([early, *late], axis=1), axes, scatter_dimension=0, tiled=True)
        grad_att, grad_extra = both[:, :width], both[:, width : width + 256]
        grad_qkv = both[:, early.shape[1] :]
        grad_gain = jnp.sum(grad_qkv * w_qkv.astype(F32), axis=1, keepdims=True) / gain_attn.astype(F32)[:, None]
        grad_gain = jnp.broadcast_to(grad_gain, (own, 128))
        grad_bias = lax.psum(grad_bias, axes)
    mixed, grad_tokens, grad_in, grad_out, grad_qkv, grad_att, grad_router, grad_gain, grad_gain_moe, grad_bias = finish(
        experts, mixed, grad_tokens, grad_in, grad_out, grad_qkv, grad_att, grad_extra, grad_gain, grad_bias)
    return (
        mixed, grad_tokens, grad_gain.reshape(own), grad_qkv, grad_att, grad_bias.T, grad_gain_moe.reshape(own), grad_router.T,
        grad_in, grad_out,
    )


def solution(mesh):
    both = P(("dp", "expert"))
    return jax.shard_map(
        functools.partial(shards, mesh.shape["expert"]),
        mesh=mesh,
        in_specs=(both, both, both, P(), both, both, both, P(), both, both, P("expert"), P("expert")),
        out_specs=(both, both, both, both, both, P(), both, both, P("expert", None, "dp"), P("expert", None, "dp")),
        check_vma=False,
    )
```

```python
import functools
import jax
import jax.numpy as jnp
from jax import lax
from jax.experimental import pallas as pl
from jax.experimental.pallas import tpu as pltpu
from jax.sharding import PartitionSpec as P

MESH = pl.DeviceIdType.MESH
F32, BF16 = jnp.float32, jnp.bfloat16
NT = (((1,), (1,)), ((), ()))
EPSILON = 1e-06
PART = 384
WIDE = 768
LAG = (0, 1, 3, 5, 99, 99)


def dot(a, b, dims=(((1,), (0,)), ((), ()))):
    return lax.dot_general(a, b, dims, preferred_element_type=F32)


def exact(a, b, dims=(((1,), (0,)), ((), ()))):
    return lax.dot_general(a, b, dims, preferred_element_type=F32, precision=lax.Precision.HIGHEST)


def flipped(index, bits, count):
    result, bit = 0, 1
    while bit < count:
        result = result + bit * (((index // bit) % 2 + (bits // bit) % 2) % 2)
        bit *= 2
    return result


def gelu_parts(hidden):
    c0, c1 = 0.7978845608028654, 0.044715
    square = hidden * hidden
    bend = jnp.tanh(hidden * (c0 + (c0 * c1) * square))
    half = 0.5 + 0.5 * bend
    slope = half + (0.5 * hidden) * (1.0 - bend * bend) * (c0 + (3.0 * c0 * c1) * square)
    return hidden * half, slope


def slots_by_row(routes, me, pad, experts):
    count = routes.shape[1]
    picked = routes == lax.broadcasted_iota(jnp.int32, (experts, count), 0)
    first = lax.broadcasted_iota(jnp.int32, (count, count), 0)
    second = lax.broadcasted_iota(jnp.int32, (count, count), 1)
    before = dot(picked.astype(BF16), (first < second).astype(BF16))
    rank = jnp.sum(jnp.where(picked, before, 0.0), axis=0, keepdims=True).astype(jnp.int32)
    return jnp.bitwise_xor(routes, me) * pad + rank


def grow_strip(strip, w8):
    strip[0:8] = w8
    have = 8
    while have < strip.shape[0]:
        strip[have : 2 * have] = pltpu.roll(strip[0:have], have, 1)
        have *= 2


SPILLS = 7


def layer_kernel(n, cap, pad, experts, heads, direct, *refs):
    given, (full_hbm, buckets_hbm, win_hbm, wout_hbm), refs = refs[:9], refs[9:13], refs[13:]
    (mixed_hbm, tokens_grad_hbm, qkv_grad_hbm, *small_hbm), refs = refs[:7], refs[7:]
    (gin_hbm, gout_hbm, probs_hbm, *rest) = refs
    spilled, rest = rest[:SPILLS], rest[SPILLS:]
    (blocks, shard, gains, hot, router, rows, cots, ties, xin, cin, back_in, returned, tie_in, sib_recv,
     sib_in, in1, in2, in3, in4, bias_out, bias_in, bias_pair,
     tokens_ref, cot_ref, qkv_ref, att_ref, router_own, gain_one, gain_two, routes_ref, table_ref, extra_ref,
     qkv_grad_ref, att_grad_ref, extra_grad_ref, gain_grad_ref, bias_grad_ref,
     put_sem, prob_sem, load_sem, pair_sem, swap_send, swap_recv, tree_send, tree_recv, turn_send, turn_recv,
     piece_send, piece_recv, piece_out, hop_send, sib_r, r1, r2, r3, r4, bias_sem, end_sem, given_sem, small_sem) = rest
    held = (tokens_ref, cot_ref, qkv_ref, att_ref, router_own, gain_one, gain_two, routes_ref, table_ref)
    fetches = [pltpu.make_async_copy(src, dst, given_sem.at[i]) for i, (src, dst) in enumerate(zip(given, held))]
    for copy in fetches:
        copy.start()
    dp, me = lax.axis_index("dp"), lax.axis_index("expert")
    count, width = tokens_ref.shape
    total = n * pad
    early = 3 * width + 256
    per = 256 // cap
    sibling = (1 - dp, me)
    staged = per == 4
    lane = lax.broadcasted_iota(jnp.int32, (count, 128), 1)

    def peer(p):
        return dp, flipped(me, p, n)

    def remote(src, dst, send, recv, device):
        return pltpu.make_async_remote_copy(
            src_ref=src, dst_ref=dst, send_sem=send, recv_sem=recv, device_id=device, device_id_type=MESH)

    def swap(kind, p):
        src, dst = ((rows, xin), (cots, cin), (rows, back_in), (cots, returned), (ties, tie_in))[kind]
        index = p // per if kind < 2 else 0
        return remote(src.at[p], dst.at[p], swap_send.at[kind, index], swap_recv.at[kind, index], peer(p))

    def swaps(kind, g=None):
        src, dst = ((rows, xin), (cots, cin), (rows, back_in), (cots, returned), (ties, tie_in))[kind]
        index, low, blocks_of = (0, 1, n - 1) if g is None else (0, 1, per - 1) if isinstance(g, int) else (g, g * per, per)
        place = pl.ds(low, blocks_of)
        return remote(src.at[place], dst.at[place], swap_send.at[kind, index], swap_recv.at[kind, index], peer(1))

    def start_swaps(kind, wanted):
        def one(p, _):
            @pl.when(wanted(p))
            def _():
                swap(kind, p).start()
            return 0

        lax.fori_loop(1, n, one, 0)

    def greet_all(prepare):
        barrier = pltpu.get_barrier_semaphore()

        def greet(p, _):
            pl.semaphore_signal(barrier, inc=1, device_id=peer(p), device_id_type=MESH)
            return 0

        lax.fori_loop(1, n, greet, 0)
        pl.semaphore_signal(barrier, inc=1, device_id=sibling, device_id_type=MESH)
        prepare()
        pl.semaphore_wait(barrier, n)

    half = win_hbm.shape[1] // 2
    steps = half // WIDE
    pieces = [(kind, k) for k in range(steps) for kind in (0, 1)]

    def piece(kind, k):
        place = pl.ds((kind * steps + k) * WIDE, WIDE)
        return remote(blocks.at[:, place], sib_recv.at[kind, k], piece_send.at[kind, k], piece_recv.at[kind, k], sibling)

    def out_piece(kind, k):
        return pltpu.make_async_copy(
            sib_recv.at[kind, k], (gin_hbm, gout_hbm)[kind].at[:, pl.ds(k * WIDE, WIDE)], piece_out.at[kind, k])

    def forward(w, packed, normed, attended, middle, moe_in, chance, probs, strip, bias, ends, weights):
        puts = []

        def put(index, src):
            copy = pltpu.make_async_copy(src, spilled[index], put_sem.at[index])
            copy.start()
            puts.append(copy)

        offsets = [pltpu.make_async_copy(buckets_hbm.at[:, pl.ds(c, 128)], ends.at[i], load_sem.at[i])
                   for i, c in enumerate((0, count - 128))]
        for copy in offsets:
            copy.start()
        def prepare():
            for copy in fetches:
                copy.wait()
            if direct:
                weights[:, : 3 * width] = qkv_ref[...].astype(F32)
                here = weights.shape[0]
                extra_ref[...] = jnp.zeros_like(extra_ref)
                extra_ref[0:experts, 0:here] = router_own[...].astype(F32)
                for i, one in enumerate((gain_one, gain_two)):
                    extra_ref[128 + i : 129 + i, 0:here] = one[...].astype(F32).reshape(1, here)
                weights[:, 3 * width : early] = extra_ref[...].T[:here]
                weights[:, early:] = att_ref[...].astype(F32)

        greet_all(prepare)
        if direct:
            own = weights.shape[0]
            block = 2 * own
            pair = remote(weights, shard, pair_sem.at[0], pair_sem.at[1], sibling)
            pair.start()
        else:
            load = pltpu.make_async_copy(full_hbm, w, pair_sem.at[0])
            load.start()
        slots = slots_by_row(routes_ref[...], me, pad, experts)

        def to_slots(values):
            hits = (slots == lax.broadcasted_iota(jnp.int32, (total, count), 0)).astype(BF16)
            return dot(hits, values).astype(BF16).reshape(n, pad, width)

        def make_cots():
            cots[...] = to_slots(cot_ref[...])
            cin[0] = cots[0]

        def make_bias():
            for copy in offsets:
                copy.wait()
            last, first = ends[1].astype(F32).T[127:128], ends[0].astype(F32).T[0:1]
            line = jnp.concatenate([last, pltpu.roll(first, count - 1, 1)], axis=1)
            line = pltpu.roll(jnp.broadcast_to(line, (8, 2 * count)), 2 * count - 127, 1)[0:1]
            hot[...] = (line.astype(jnp.int32) == lax.broadcasted_iota(jnp.int32, hot.shape, 0)).astype(F32)
            table = exact(table_ref[...], hot[...])
            for h in range(heads):
                row = jnp.broadcast_to(table[h : h + 1], (8, 2 * count))
                place = lax.broadcasted_iota(jnp.int32, row.shape, 0)
                shifted = row
                for r in range(1, 8):
                    shifted = jnp.where(place == r, pltpu.roll(row, r, 1), shifted)
                bias[h] = shifted

        if direct:
            pair.wait()
            mine, other = weights[...], shard[...]
            blocks[pl.ds(pl.multiple_of(me * block, 16), block), : w.shape[1]] = jnp.concatenate(
                [jnp.where(dp == 0, mine, other), jnp.where(dp == 0, other, mine)], axis=0).astype(BF16)
            second, third = 2 - dp, 1 + dp
            far = list(range(4, n, 4))
            near = [0] + far

            def at(t, r, core):
                start, size = ((0, early // 2), (early, width // 2))[t]
                return blocks.at[pl.ds(pl.multiple_of(flipped(me, r, n) * block, 16), block),
                                 pl.ds(pl.multiple_of(start + core * size, 128), size)]

            def hop(t, r, step):
                return remote(at(t, r, dp), at(t, r, dp), tree_send.at[t], tree_recv.at[t, r + step], peer(step))

            def arrived(t, r):
                remote(at(t, r, dp), at(t, r, dp), tree_send.at[t], tree_recv.at[t, r], peer(r)).wait_recv()

            def to_sibling(t, r, core):
                return remote(at(t, r, core), at(t, r, core), turn_send.at[t], turn_recv.at[t], sibling)

            def bulk(t, send, recv):
                place = blocks.at[: (n - 1) * block, : (early // 2, width // 2)[t]]
                return remote(place, place, send.at[t], recv.at[t] if recv is turn_recv else recv.at[t, 0], sibling)

            def turn(t, step):
                if step == 0:
                    hop(t, 0, 8).start()
                    hop(t, 0, 4).start()
                    hop(t, 0, third).start()
                    hop(t, 0, second).start()
                elif step == 1:
                    for r in (8, 4, 12):
                        arrived(t, r)
                        if r == 8:
                            hop(t, 8, 4).start()
                        hop(t, r, third).start()
                        hop(t, r, second).start()
                        to_sibling(t, r, dp).start()
                elif step == 2:
                    for r in near:
                        arrived(t, r + second)
                        hop(t, r + second, third).start()
                        to_sibling(t, r + second, dp).start()
                elif step == 3:
                    for r in near:
                        arrived(t, r + third)
                        to_sibling(t, r + third, dp).start()
                        arrived(t, r + 3)
                        to_sibling(t, r + 3, dp).start()
                else:
                    bulk(t, turn_send, turn_recv).wait_recv()
                    place = (slice(0, early), slice(early, w.shape[1]))[t]
                    for core in (0, 1):
                        for q in range(n // 2):
                            low = 2 * q * block + core * own
                            pair_rows = [blocks[p : p + own, place].astype(F32) for p in (low, low + block)]
                            w[core * own * n + q * block : core * own * n + (q + 1) * block, place] = jnp.concatenate(
                                pair_rows, axis=0).astype(BF16)

            turn(0, 0)
            make_bias()
            make_cots()
            turn(0, 1)
            turn(1, 0)
            start_swaps(1, lambda p: p % 4 == 0)
            turn(0, 2)
            turn(1, 1)
            turn(0, 3)
            turn(1, 2)
            start_swaps(1, lambda p: p % 4 != 0)
            turn(0, 4)
        else:
            make_bias()
            make_cots()
            start_swaps(1, lambda p: p > 0)
            load.wait()
        gains[...] = w[:, 3 * width + 128 : early].astype(F32).T[0:8]
        router[...] = w[:, 3 * width : 3 * width + 128]
        x = tokens_ref[...].astype(F32)
        normed[...] = (x * lax.rsqrt(jnp.mean(x * x, axis=1, keepdims=True) + EPSILON) * gains[0:1]).astype(BF16)
        put(0, normed)
        for c in range(3):
            cols_c = slice(c * width, (c + 1) * width)
            packed[:, cols_c] = dot(normed[...], w[:, cols_c]).astype(BF16)
        put(1, packed)
        scale = (width // heads) ** -0.5

        def put_probs(k):
            return pltpu.make_async_copy(probs.at[pl.ds(2 * k, 2)], probs_hbm.at[pl.ds(2 * k, 2)], prob_sem.at[0])

        def attend(k, _):
            def part(c):
                return packed[:, pl.ds(pl.multiple_of(c * width + k * 128, 128), 128)]

            queries = (part(0).astype(F32) * scale).astype(BF16)
            keys = part(1)
            values = part(2).astype(F32).T.astype(BF16)
            outs = []
            for h in (0, 1):
                grow_strip(strip, bias[2 * k + h])
                own_keys = jnp.where((lane < 64) == (h == 0), keys, jnp.zeros_like(keys))
                scores = dot(own_keys, queries, NT)
                scores = jnp.concatenate(
                    [scores[128 * b : 128 * b + 128] + strip[:, 384 - 128 * b : 896 - 128 * b] for b in range(4)], axis=0)
                powers = jnp.exp(scores - jnp.max(scores, axis=0, keepdims=True))
                part_weights = (powers * (1.0 / jnp.sum(powers, axis=0, keepdims=True))).astype(BF16)
                probs[2 * k + h] = part_weights
                outs.append(dot(values[64 * h : 64 * h + 64], part_weights))
            put_probs(k).start()
            attended[:, pl.ds(pl.multiple_of(k * 128, 128), 128)] = jnp.concatenate(outs, axis=0).T.astype(BF16)
            if direct:
                for step in (3, 4):
                    @pl.when(k == step + 1)
                    def _():
                        turn(1, step)
            return 0

        lax.fori_loop(0, heads // 2, attend, 0)
        mid = tokens_ref[...].astype(F32) + dot(attended[...], w[:, early:])
        middle[...] = mid
        moe = (mid * lax.rsqrt(jnp.mean(mid * mid, axis=1, keepdims=True) + EPSILON) * gains[1:2]).astype(BF16)
        moe_in[...] = moe
        rows[...] = to_slots(moe)
        start_swaps(0, lambda p: (p < 4) | ((p % 4 == 0) & (p < 12)) if staged else p > 0)
        xin[0] = rows[0]
        put(2, attended)
        put(3, middle)
        put(4, moe_in)
        put(5, w)
        logits = dot(moe, router[...])
        logits = jnp.where(lane < experts, logits, -1e30)
        powers = jnp.exp(logits - jnp.max(logits, axis=1, keepdims=True))
        chance[...] = powers / jnp.sum(powers, axis=1, keepdims=True)
        put(6, chance)
        if direct:
            for t in (0, 1):
                bulk(t, tree_send, tree_recv).wait_send()
                bulk(t, turn_send, turn_recv).wait_send()
        for copy in puts:
            copy.wait()
        pltpu.make_async_copy(probs, probs_hbm, prob_sem.at[0]).wait()

    def experts_both(win, wout, xt, rt, act, hgr):
        ff = win.shape[1]
        group_rows = per * cap
        chunk = 1024
        loads = [pltpu.make_async_copy(win_hbm, win, load_sem.at[0]), pltpu.make_async_copy(wout_hbm, wout, load_sem.at[1])]
        for load in loads:
            load.start()

        def packed_rows(ref, g):
            block = ref[pl.ds(g * per, per)].reshape(per * pad, width)
            if pad == cap:
                return block
            r = lax.broadcasted_iota(jnp.int32, (group_rows, per * pad), 0)
            c = lax.broadcasted_iota(jnp.int32, (group_rows, per * pad), 1)
            return dot(((r // cap) * pad + r % cap == c).astype(BF16), block).astype(BF16)

        def spread_rows(block):
            if pad == cap:
                return block.reshape(per, pad, width)
            r = lax.broadcasted_iota(jnp.int32, (per * pad, group_rows), 0)
            c = lax.broadcasted_iota(jnp.int32, (per * pad, group_rows), 1)
            pick = (r // pad == c // cap) & (r % pad == c % cap)
            return dot(pick.astype(BF16), block).astype(BF16).reshape(per, pad, width)

        def group(g, _):
            def over(act_on):
                def one(j, _):
                    @pl.when(g * per + j != 0)
                    def _():
                        act_on(g * per + j)
                    return 0

                lax.fori_loop(0, per, one, 0)

            def all_of(kind, act_on):
                @pl.when(g == 0)
                def _():
                    act_on(swaps(kind, 0))

                @pl.when(g != 0)
                def _():
                    act_on(swaps(kind, g))

            all_of(0, lambda copies: copies.wait_recv())

            @pl.when(g == 0)
            def _():
                if staged:
                    start_swaps(0, lambda p: (p >= 4) & (p % 4 != 0) & (p < 12))
                for load in loads:
                    load.wait()

            if staged:
                @pl.when(g == 1)
                def _():
                    start_swaps(0, lambda p: p >= 12)

            all_of(1, lambda copies: copies.wait_recv())
            here = pl.ds(pl.multiple_of(g * group_rows, group_rows), group_rows)
            x = packed_rows(xin, g)
            logits = dot(x, router[...])
            lanes = lax.broadcasted_iota(jnp.int32, logits.shape, 1)
            logits = jnp.where(lanes < experts, logits, -1e30)
            powers = jnp.exp(logits - jnp.max(logits, axis=1, keepdims=True))
            gate = jnp.sum(jnp.where(lanes == me, powers, 0.0), axis=1, keepdims=True) / jnp.sum(
                powers, axis=1, keepdims=True)
            r = (gate * packed_rows(cin, g).astype(F32)).astype(BF16)
            xt[:, here] = x.T
            rt[:, here] = r.T

            def hidden_chunk(k, _):
                cols = pl.ds(pl.multiple_of(k * chunk, chunk), chunk)
                value, slope = gelu_parts(dot(x, win[:, cols]))
                act[here, cols] = value.astype(BF16)
                hgr[here, cols] = (dot(r, wout[:, cols]) * slope).astype(BF16)
                return 0

            lax.fori_loop(0, ff // chunk, hidden_chunk, 0)
            back = spread_rows(dot(hgr[here], win[...], NT).astype(BF16))
            all_of(0, lambda copies: copies.wait_send())
            rows[pl.ds(g * per, per)] = back
            over(lambda p: swap(2, p).start())
            produced = dot(act[here], wout[...], NT).astype(BF16)
            tie = jnp.sum(r.astype(F32) * produced.astype(F32), axis=1, keepdims=True)
            for j in range(per):
                row = jnp.broadcast_to(tie[j * cap : (j + 1) * cap], (cap, 128)).T[0:8]
                ties[g * per + j] = jnp.concatenate([row, jnp.zeros((8, 128 - cap), F32)], axis=1)
            over(lambda p: swap(4, p).start())
            all_of(1, lambda copies: copies.wait_send())
            cots[pl.ds(g * per, per)] = spread_rows(produced)

            @pl.when(g < n // per // 2)
            def _():
                over(lambda p: swap(3, p).start())

            return 0

        lax.fori_loop(0, n // per, group, 0)
        back_in[0] = rows[0]
        tie_in[0] = ties[0]
        returned[0] = cots[0]

        def partial(kind, owner, k):
            cols = pl.ds(pl.multiple_of(owner * half + k * WIDE, 128), WIDE)
            return dot(xt[...], hgr[:, cols]) if kind == 0 else dot(rt[...], act[:, cols])

        for kind, k in pieces:
            place = (kind * steps + k) * WIDE
            blocks[:, place : place + WIDE] = partial(kind, 1 - dp, k).astype(BF16)
            piece(kind, k).start()
        for kind, k in pieces:
            value = partial(kind, dp, k)
            piece(kind, k).wait_recv()
            sib_recv[kind, k] = (value + sib_recv[kind, k].astype(F32)).astype(BF16)
            out_piece(kind, k).start()

    def backward(w, packed, normed, attended, middle, moe_in, chance, prob, mid_grad, att_cot, packed_grad, normed_t, chunk,
                 strip, bias_rows, mine, keep, out1, out2, out3, out4):
        loaded = (normed, packed, attended, middle, moe_in, w, chance)
        loads = [pltpu.make_async_copy(spilled[i], loaded[i], load_sem.at[i]) for i in range(SPILLS)]
        order = (6, 3, 5, 2, 4, 0, 1)
        for i in order:
            loads[i].start()

        def fetch(k):
            return pltpu.make_async_copy(probs_hbm.at[pl.ds(2 * k, 2)], prob.at[k % 2], prob_sem.at[k % 2])

        fetch(0).start()
        own = qkv_ref.shape[0]
        lead = (width + 256 + PART - 1) // PART
        chunks = lead + heads // 2

        if direct:
            half_rows = own * n

            steps_out = ((out1, in1, r1), (out2, in2, r2), (out3, in3, r3), (out4, in4, r4))
            ways = (1 + dp, 2 - dp, 4, 8)

            def sib_out(k):
                across = blocks.shape[1] // PART
                return blocks.at[pl.ds(pl.multiple_of((k // across) * half_rows, 16), half_rows),
                                 pl.ds(pl.multiple_of((k % across) * PART, 128), PART)]

            def hop(stage, k):
                if stage == 0:
                    return remote(sib_out(k), sib_in.at[k], hop_send.at[0], sib_r.at[k], sibling)
                src, dst, recv = steps_out[stage - 1]
                return remote(src.at[k], dst.at[k], hop_send.at[stage], recv.at[k], peer(ways[stage - 1]))

            def unit(k, u):
                r = ways[0] * (u // 4) + ways[1] * ((u // 2) % 2) + ways[2] * (u % 2)
                places = [pl.multiple_of(flipped(me, r + z, n) * own, 8) for z in (0, ways[3])]
                return jnp.concatenate([mine[k % 2, pl.ds(place, own)] for place in places], axis=0)

            def stage(s, k):
                if s == 0:
                    there = pl.ds(pl.multiple_of((1 - dp) * half_rows, 8), half_rows)
                    here = pl.ds(pl.multiple_of(dp * half_rows, 8), half_rows)
                    sib_out(k)[...] = chunk[there].astype(BF16)
                    hop(0, k).start()
                    mine[k % 2] = chunk[here]
                elif s == 1:
                    hop(0, k).wait_recv()
                    mine[k % 2] = mine[k % 2] + sib_in[k].astype(F32)
                    for u in range(4):
                        out1[k, 2 * own * u : 2 * own * (u + 1)] = unit(k, u + 4).astype(BF16)
                    hop(1, k).start()
                    for u in range(4):
                        keep[k, 2 * own * u : 2 * own * (u + 1)] = unit(k, u)
                elif s in (2, 3):
                    src, dst = steps_out[s - 1][0], steps_out[s - 2][1]
                    left = 8 * own // (1 << (s - 1))
                    hop(s - 1, k).wait_recv()
                    value = keep[k, : 2 * left] + dst[k].astype(F32)
                    src[k] = value[left:].astype(BF16)
                    hop(s, k).start()
                    keep[k, :left] = value[:left]
                elif s == 4:
                    hop(3, k).wait_recv()
                    value = keep[k, : 2 * own] + in3[k].astype(F32)
                    out4[k] = jnp.concatenate(
                        [value[own:, 128 * c : 128 * (c + 1)] for c in range(3)]
                        + [jnp.zeros((out4.shape[1] - 3 * own, 128), F32)], axis=0).astype(BF16)
                    hop(4, k).start()
                    keep[k, :own] = value[:own]
                else:
                    hop(4, k).wait_recv()
                    far = in4[k].astype(F32)
                    keep[k, :own] = keep[k, :own] + jnp.concatenate(
                        [far[own * c : own * (c + 1)] for c in range(3)], axis=1)

            def advance(k):
                stage(0, k)
                for s in range(1, 6):
                    @pl.when((k - LAG[s] >= 0) & (k - LAG[s] < chunks))
                    def _():
                        stage(s, k - LAG[s])

            done = {k: max(s for s in range(6) if LAG[s] <= chunks - 1 - k) for k in range(chunks)}

            def drain(last, *which):
                for k in which or range(chunks):
                    while done[k] < last:
                        done[k] += 1
                        stage(done[k], k)

        else:
            def advance(k):
                copy = pltpu.make_async_copy(chunk, qkv_grad_hbm.at[k], end_sem.at[0])
                copy.start()
                copy.wait()

            def drain(*_):
                pass

        expert_of = jnp.broadcast_to(routes_ref[...].astype(F32), (128, count)).T[:, 0:1].astype(jnp.int32)
        picked = expert_of == lane
        first = lax.broadcasted_iota(jnp.int32, (count, count), 0)
        other = lax.broadcasted_iota(jnp.int32, (count, count), 1)
        before = dot((other < first).astype(BF16), picked.astype(BF16))
        rank = jnp.sum(jnp.where(picked, before, 0.0), axis=1, keepdims=True).astype(jnp.int32)
        place = jnp.bitwise_xor(expert_of, me)
        hits = (place * pad + rank == lax.broadcasted_iota(jnp.int32, (count, total), 1)).astype(BF16)

        def each_peer(act_on):
            def one(p, _):
                act_on(p)
                return 0

            lax.fori_loop(1, n, one, 0)

        for kind, k in pieces:
            piece(kind, k).wait_send()
        swaps(2).wait_recv()
        swaps(4).wait_recv()
        ties_row = exact((place == lax.broadcasted_iota(jnp.int32, (count, n), 1)).astype(F32), jnp.max(tie_in[...], axis=1))
        tie = jnp.sum(jnp.where(lane == rank, ties_row, 0.0), axis=1, keepdims=True)
        for i in order[:1]:
            loads[i].wait()
        logit_grad = (tie * (picked.astype(F32) - chance[...])).astype(BF16)
        grad = dot(hits, back_in[...].reshape(total, width))
        for i in order[1:]:
            loads[i].wait()
        grad = grad + dot(logit_grad, router[...], NT)
        mid = middle[...]
        root = lax.rsqrt(jnp.mean(mid * mid, axis=1, keepdims=True) + EPSILON)
        unit_mid = mid * root
        gain_rows = jnp.sum(grad * unit_mid, axis=0, keepdims=True)
        scaled = grad * gains[1:2]
        mid_g = cot_ref[...].astype(F32) + root * (scaled - unit_mid * jnp.mean(scaled * unit_mid, axis=1, keepdims=True))
        mid_grad[...] = mid_g
        attn_grad = mid_g.astype(BF16)
        att_cot[...] = dot(attn_grad, w[:, early:], NT).astype(BF16)
        attended_t = attended[...].T
        for k in range(lead):
            if (k + 1) * PART <= width:
                chunk[...] = dot(attended_t, attn_grad[:, k * PART : (k + 1) * PART])
            else:
                chunk[:, 0:128] = dot(moe_in[...].T, logit_grad)
                chunk[:, 128:256] = jnp.broadcast_to(gain_rows, (128, width)).T
                chunk[:, 256:] = jnp.zeros((width, PART - 256), F32)
            advance(k)
        normed_t[...] = normed[...].T
        swaps(2).wait_send()
        start_swaps(3, lambda p: (p >= n // 2) & (p % 4 == 0))

        scale = (width // heads) ** -0.5

        def attend_back(k, _):
            fetch(k).wait()

            @pl.when(k + 1 < heads // 2)
            def _():
                fetch(k + 1).start()

            def part(c):
                return packed[:, pl.ds(pl.multiple_of(c * width + k * 128, 128), 128)]

            queries, keys, values = part(0), part(1), part(2)
            keys_t = (keys.astype(F32) * scale).T.astype(BF16)
            cot = att_cot[:, pl.ds(pl.multiple_of(k * 128, 128), 128)]
            query_t, key_g, value_g = [], None, None
            for h in (0, 1):
                mask = (lane < 64) == (h == 0)
                own_cot = jnp.where(mask, cot, jnp.zeros_like(cot))
                own_queries = jnp.where(mask, queries, jnp.zeros_like(queries))
                weights = prob[k % 2, h]
                chances = weights.astype(F32)
                product = chances * dot(values, own_cot, NT)
                score_grad = (product - chances * jnp.sum(product, axis=0, keepdims=True)).astype(BF16)
                wide = score_grad.astype(F32)
                for b in range(4):
                    block = wide[128 * b : 128 * b + 128]
                    cols = slice(384 - 128 * b, 896 - 128 * b)
                    if b == 0:
                        strip[:, cols] = block
                        strip[:, 0:384] = jnp.zeros((128, 384), F32)
                        strip[:, 896:1024] = jnp.zeros((128, 128), F32)
                    else:
                        strip[:, cols] += block
                have = 64
                folded = strip[...]
                while have >= 8:
                    folded = folded[:have] + pltpu.roll(folded[have:], 1024 - have, 1)
                    have //= 2
                for s in range(1, 8):
                    folded = jnp.where(lax.broadcasted_iota(jnp.int32, folded.shape, 0) == s,
                                       pltpu.roll(folded, 1024 - s, 1), folded)
                bias_rows[2 * k + h] = folded
                v = dot(weights, own_cot)
                q = dot(score_grad, own_queries)
                value_g = v if h == 0 else value_g + v
                key_g = q if h == 0 else key_g + q
                query_t.append(dot(keys_t[64 * h : 64 * h + 64], score_grad))
            query_g = jnp.concatenate(query_t, axis=0).T.astype(BF16)
            grads = jnp.concatenate([query_g, (key_g * scale).astype(BF16), value_g.astype(BF16)], axis=1)
            for c in range(3):
                packed_grad[:, pl.ds(pl.multiple_of(c * width + k * 128, 128), 128)] = grads[:, c * 128 : (c + 1) * 128]
            chunk[...] = dot(normed_t[...], grads)
            advance(k + lead)

            @pl.when(k == 0)
            def _():
                start_swaps(3, lambda p: (p >= n // 2) & (p % 4 == 1))

            @pl.when(k == 0)
            def _():
                start_swaps(3, lambda p: (p >= n // 2) & (p % 4 == 2))

            @pl.when(k == 0)
            def _():
                start_swaps(3, lambda p: (p >= n // 2) & (p % 4 == 3))

            return 0

        lax.fori_loop(0, heads // 2, attend_back, 0)
        drain(1, chunks - 1)
        drain(2, *range(chunks - 1))
        drain(3, *range(chunks - 3))
        sums = jnp.concatenate([jnp.sum(bias_rows[h], axis=0, keepdims=True) for h in range(heads)], axis=0)
        bias_out[...] = exact(sums, hot[...], NT)
        if direct:
            pair_hop = remote(bias_out, bias_pair, pair_sem.at[2], pair_sem.at[3], sibling)
            pair_hop.start()

            def bias_hop(p):
                return remote(bias_in.at[me], bias_in.at[me], bias_sem.at[0], bias_sem.at[1], peer(p))

            place = bias_in.at[1:]
            bias_all = remote(place, place, bias_sem.at[0], bias_sem.at[1], peer(1))

        normed_grad = dot(packed_grad[...], w[:, : 3 * width], NT)
        drain(2)
        drain(3, *range(chunks - 1))
        drain(4, *range(chunks - 4))
        if direct:
            pair_hop.wait()
            bias_in[me] = bias_out[...] + bias_pair[...]
            each_peer(lambda p: bias_hop(p).start())
        x = tokens_ref[...].astype(F32)
        root = lax.rsqrt(jnp.mean(x * x, axis=1, keepdims=True) + EPSILON)
        unit_x = x * root
        scaled = normed_grad * gains[0:1]
        mid_grad[...] = mid_grad[...] + root * (scaled - unit_x * jnp.mean(scaled * unit_x, axis=1, keepdims=True))
        ends = [pltpu.make_async_copy(mid_grad, tokens_grad_hbm, end_sem.at[0]),
                pltpu.make_async_copy(att_cot, mixed_hbm, end_sem.at[1])]
        ends[0].start()
        drain(3)
        drain(4, *range(chunks - 1))
        swaps(3).wait_recv()
        gate = jnp.sum(jnp.where(picked, chance[...], 0.0), axis=1, keepdims=True)
        att_cot[...] = (middle[...] + gate * dot(hits, returned[...].reshape(total, width))).astype(BF16)
        ends[1].start()
        if direct:
            drain(4)
            drain(5)
            bias_all.wait_recv()
            total_bias = bias_in[0]
            for p in range(1, n):
                total_bias = total_bias + bias_in[p]
            bias_grad_ref[...] = total_bias
            for k in range(chunks):
                result = keep[k, :own]
                if k >= lead:
                    for c in range(3):
                        start = c * width + (k - lead) * 128
                        qkv_grad_ref[:, start : start + 128] = result[:, c * 128 : (c + 1) * 128]
                elif (k + 1) * PART <= width:
                    att_grad_ref[:, k * PART : (k + 1) * PART] = result
                else:
                    extra_grad_ref[...] = result[:, :256]
            total_gain = jnp.sum(qkv_grad_ref[...] * qkv_ref[...].astype(F32), axis=1, keepdims=True)
            gain_grad_ref[...] = jnp.broadcast_to(total_gain / extra_ref[128:256].T[:own, 0:1], gain_grad_ref.shape)

            for s, sent in enumerate((sib_in, out1, out2, out3, out4)):
                remote(sent, sent, hop_send.at[s], sib_r.at[0], sibling).wait_send()
            bias_all.wait_send()
        else:
            bias_grad_ref[...] = bias_out[...]
        small = [*zip((att_grad_ref, extra_grad_ref, gain_grad_ref, bias_grad_ref), small_hbm)]
        if direct:
            small.append((qkv_grad_ref, qkv_grad_hbm))
        for i, (src, dst) in enumerate(small):
            ends.append(pltpu.make_async_copy(src, dst, small_sem.at[i]))
            ends[-1].start()
        for kind in (3, 4):
            swaps(kind).wait_send()
        for copy in ends:
            copy.wait()
        for kind, k in pieces:
            out_piece(kind, k).wait()

    wide = w_columns(width)
    scratch = pltpu.VMEM
    shared = [
        scratch((width, wide), BF16), scratch((count, 3 * width), BF16), scratch((count, width), BF16),
        scratch((count, width), BF16), scratch((count, width), F32), scratch((count, width), BF16), scratch((count, 128), F32),
    ]
    own_rows = qkv_ref.shape[0]
    pl.run_scoped(
        forward, *shared, scratch((heads, count, count), BF16), scratch((128, 2 * count), F32),
        scratch((heads, 8, 2 * count), F32), scratch((2, count, 128), jnp.int32),
        scratch((own_rows, wide) if direct else (8, 128), F32))
    pl.run_scoped(
        experts_both, *[scratch((width, win_hbm.shape[1]), BF16) for _ in range(2)],
        *[scratch((width, n * cap), BF16) for _ in range(2)], *[scratch((n * cap, win_hbm.shape[1]), BF16) for _ in range(2)])
    all_chunks = (width + 256 + PART - 1) // PART + heads // 2

    def buffer(shape, kind):
        return scratch((all_chunks, *shape) if direct else (8, 128), kind)

    pl.run_scoped(
        backward, *shared, scratch((2, 2, count, count), BF16), scratch((count, width), F32), scratch((count, width), BF16),
        scratch((count, 3 * width), BF16), scratch((width, count), BF16), scratch((width, PART), F32),
        scratch((128, 2 * count), F32), scratch((heads, 8, 2 * count), F32),
        scratch((2, own_rows * n, PART), F32), buffer((8 * own_rows, PART), F32),
        *[buffer((own_rows << s, PART), BF16) for s in (3, 2, 1)], buffer((-(-3 * own_rows // 16) * 16, 128), BF16))


def w_columns(width):
    return 4 * width + 256


def layer(n, cap, pad, experts, heads, direct, tokens, cotangent, qkv, att, router, one, two, full, routes, table, buckets,
          win, wout):
    count, width = tokens.shape
    wide = w_columns(width)
    own = qkv.shape[0]
    kinds = table.shape[1]
    ff = win.shape[1]
    chunks = (width + 256 + PART - 1) // PART + heads // 2
    steps = ff // 2 // WIDE
    short = -(-3 * own // 16) * 16
    any_ = pl.BlockSpec(memory_space=pl.ANY)
    dma = pltpu.SemaphoreType.DMA
    scratch = pltpu.VMEM
    shape = jax.ShapeDtypeStruct

    def landing(*rest):
        return scratch((chunks, *rest) if direct else (16, 128), BF16)

    small = ((own, width), (own, 256), (own, 128), (heads, kinds))
    outs = [
        (shape((count, width), BF16), any_), (shape((count, width), F32), any_),
        (shape((own, 3 * width) if direct else (chunks, width, PART), F32), any_),
        *[(shape(dims, F32), any_) for dims in small], (shape((width, ff // 2), BF16), any_), (shape((width, ff // 2), BF16), any_),
        (shape((heads, count, count), BF16), any_), (shape((count, width), BF16), any_),
        (shape((count, 3 * width), BF16), any_), (shape((count, width), BF16), any_), (shape((count, width), F32), any_),
        (shape((count, width), BF16), any_), (shape((width, wide), BF16), any_), (shape((count, 128), F32), any_),
    ]
    slots = scratch((n, pad, width), BF16)
    given = (tokens, cotangent, qkv, att, router, one, two, routes, table)
    return pl.pallas_call(
        functools.partial(layer_kernel, n, cap, pad, experts, heads, direct),
        out_shape=tuple(o[0] for o in outs),
        in_specs=[any_] * 13,
        out_specs=tuple(o[1] for o in outs),
        scratch_shapes=[
            scratch((width, max(wide, 2 * steps * WIDE)), BF16),
            scratch((own, wide) if direct else (8, 128), F32),
            scratch((8, width), F32), scratch((kinds, 2 * count), F32), scratch((width, 128), BF16),
            slots, slots, scratch((n, 8, 128), F32), slots, slots, slots, slots, scratch((n, 8, 128), F32),
            scratch((2, steps, width, WIDE), BF16),
            landing(own * n, PART), *[landing(own << s, PART) for s in (3, 2, 1)], landing(short, 128),
            scratch((heads, kinds), F32), scratch((n, heads, kinds), F32), scratch((heads, kinds), F32),
            *[scratch(a.shape, a.dtype) for a in given], scratch((256, 128), F32), scratch((own, 3 * width), F32), *[scratch(dims, F32) for dims in small],
            dma((SPILLS,)), dma((2,)), dma((SPILLS,)), dma((4,)), dma((5, n * cap // 256)), dma((5, n * cap // 256)),
            dma((2,)), dma((2, n)), dma((2,)), dma((2,)),
            dma((2, steps)), dma((2, steps)), dma((2, steps)),
            dma((5,)), *[dma((chunks,)) for _ in range(5)], dma((2,)), dma((2,)), dma((9,)), dma((5,)),
        ],
        compiler_params=pltpu.CompilerParams(
            collective_id=1, has_side_effects=True, vmem_limit_bytes=63 * 1024 * 1024),
        name="layer",
    )(*given, full, buckets, win, wout)


def finish_kernel(
    mixed_in, tokens_in, in_hbm, out_hbm, *refs,
):
    small_ins, (mixed_out, tokens_out, in_out, out_out), small_outs, refs = refs[:5], refs[5:9], refs[9:15], refs[15:]
    (mixed, tokens, narrow, wide, sem, load_sem, store_sem, small_sem) , held = refs[:8], refs[8:]
    fetches = [pltpu.make_async_copy(src, dst, small_sem.at[i]) for i, (src, dst) in enumerate(zip(small_ins, held[:5]))]
    leaves = [pltpu.make_async_copy(src, dst, small_sem.at[5 + i]) for i, (src, dst) in enumerate(zip(held[5:], small_outs))]
    qkv_in, att_in, extra_in, gain_in, bias_in, qkv_out, att_out, router_out, gain_out, gain_moe_out, bias_out = held
    for copy in fetches:
        copy.start()
    ins = [pltpu.make_async_copy(mixed_in, mixed, sem.at[0]), pltpu.make_async_copy(tokens_in, tokens, sem.at[1])]
    outs = [pltpu.make_async_copy(mixed, mixed_out, sem.at[2]), pltpu.make_async_copy(tokens, tokens_out, sem.at[3])]
    parts, rows = narrow.shape[1], narrow.shape[2]

    def load(kind, k):
        return pltpu.make_async_copy(
            (in_hbm, out_hbm)[kind].at[pl.ds(k * rows, rows)], narrow.at[kind, k], load_sem.at[kind, k])

    def store(kind, k):
        return pltpu.make_async_copy(
            wide.at[kind, k], (in_out, out_out)[kind].at[0, pl.ds(k * rows, rows)], store_sem.at[kind, k])

    for k in range(parts):
        for kind in (0, 1):
            load(kind, k).start()
    for copy in ins:
        copy.start()
    for k in range(parts):
        for kind in (0, 1):
            load(kind, k).wait()
            wide[kind, k] = narrow[kind, k].astype(F32)
            store(kind, k).start()
    for copy in fetches:
        copy.wait()
    qkv_out[...] = qkv_in[...]
    att_out[...] = att_in[...]
    router_out[...] = extra_in[:, :128].T[: router_out.shape[0]]
    gain_out[...] = gain_in[...].T[0:1]
    gain_moe_out[...] = extra_in[:, 128:].T[0:1]
    bias_out[...] = bias_in[...]
    for copy in leaves:
        copy.start()
    for copy_in, copy_out in zip(ins, outs):
        copy_in.wait()
        copy_out.start()
    for k in range(parts):
        for kind in (0, 1):
            store(kind, k).wait()
    for copy in outs + leaves:
        copy.wait()


def finish(experts, mixed, tokens_grad, grad_in, grad_out, qkv, att, extra, gain, bias):
    any_ = pl.BlockSpec(memory_space=pl.ANY)
    dma = pltpu.SemaphoreType.DMA
    parts = 8
    rows = grad_in.shape[0] // parts
    own = qkv.shape[0]
    shape = jax.ShapeDtypeStruct
    small = (qkv.shape, att.shape, (experts, own), (1, own), (1, own), bias.shape)
    return pl.pallas_call(
        finish_kernel,
        out_shape=(
            shape(mixed.shape, BF16), shape(tokens_grad.shape, F32), shape((1, *grad_in.shape), F32),
            shape((1, *grad_out.shape), F32), *[shape(dims, F32) for dims in small],
        ),
        in_specs=[any_] * 9,
        out_specs=tuple([any_] * 10),
        scratch_shapes=[
            pltpu.VMEM(mixed.shape, BF16),
            pltpu.VMEM(tokens_grad.shape, F32),
            pltpu.VMEM((2, parts, rows, grad_in.shape[1]), BF16),
            pltpu.VMEM((2, parts, rows, grad_in.shape[1]), F32),
            dma((4,)), dma((2, parts)), dma((2, parts)), dma((11,)),
            *[pltpu.VMEM(dims, F32) for dims in (*[a.shape for a in (qkv, att, extra, gain, bias)], *small)],
        ],
        compiler_params=pltpu.CompilerParams(vmem_limit_bytes=60 * 1024 * 1024),
        name="finish",
    )(mixed, tokens_grad, grad_in, grad_out, qkv, att, extra, gain, bias)


def shards(
    n, tokens, cotangent, routes, buckets, gain_attn, w_qkv, w_att, rel_bias, gain_moe, w_router, w_in, w_out,
):
    axes = ("dp", "expert")
    count, width = tokens.shape
    experts = w_router.shape[1]
    heads = rel_bias.shape[1]
    own = w_qkv.shape[0]
    cap = max(2, 2 * count // experts)
    pad = max(16, cap)
    direct = n == 16 and own % 8 == 0
    if direct:
        full = w_att
    else:
        extra = jnp.concatenate(
            [w_router, jnp.zeros((own, 128 - experts), BF16), gain_attn[:, None], gain_moe[:, None],
             jnp.zeros((own, 126), BF16)], axis=1)
        full = lax.all_gather(jnp.concatenate([w_qkv, extra, w_att], axis=1), axes, axis=0, tiled=True)
    mixed, grad_tokens, grad_qkv, grad_att, grad_extra, grad_gain, grad_bias, grad_in, grad_out = layer(
        n, cap, pad, experts, heads, direct, tokens, cotangent, w_qkv, w_att, w_router.T, gain_attn, gain_moe, full, routes.T,
        rel_bias.T, buckets,        w_in[0], w_out[0])[:9]
    if not direct:
        lead = grad_qkv.shape[0] - heads // 2
        early = jnp.concatenate([grad_qkv[k] for k in range(lead)], axis=1)
        late = [grad_qkv[lead:, :, c * 128 : (c + 1) * 128].transpose(1, 0, 2).reshape(width, width) for c in range(3)]
        both = lax.psum_scatter(jnp.concatenate([early, *late], axis=1), axes, scatter_dimension=0, tiled=True)
        grad_att, grad_extra = both[:, :width], both[:, width : width + 256]
        grad_qkv = both[:, early.shape[1] :]
        grad_gain = jnp.sum(grad_qkv * w_qkv.astype(F32), axis=1, keepdims=True) / gain_attn.astype(F32)[:, None]
        grad_gain = jnp.broadcast_to(grad_gain, (own, 128))
        grad_bias = lax.psum(grad_bias, axes)
    mixed, grad_tokens, grad_in, grad_out, grad_qkv, grad_att, grad_router, grad_gain, grad_gain_moe, grad_bias = finish(
        experts, mixed, grad_tokens, grad_in, grad_out, grad_qkv, grad_att, grad_extra, grad_gain, grad_bias)
    return (
        mixed, grad_tokens, grad_gain.reshape(own), grad_qkv, grad_att, grad_bias.T, grad_gain_moe.reshape(own), grad_router.T,
        grad_in, grad_out,
    )


def solution(mesh):
    both = P(("dp", "expert"))
    return jax.shard_map(
        functools.partial(shards, mesh.shape["expert"]),
        mesh=mesh,
        in_specs=(both, both, both, P(), both, both, both, P(), both, both, P("expert"), P("expert")),
        out_specs=(both, both, both, both, both, P(), both, both, P("expert", None, "dp"), P("expert", None, "dp")),
        check_vma=False,
    )
```

```python
import functools
import jax
import jax.numpy as jnp
from jax import lax
from jax.experimental import pallas as pl
from jax.experimental.pallas import tpu as pltpu
from jax.sharding import PartitionSpec as P

MESH = pl.DeviceIdType.MESH
F32, BF16 = jnp.float32, jnp.bfloat16
NT = (((1,), (1,)), ((), ()))
EPSILON = 1e-06
PART = 384
WIDE = 768
LAG = (0, 1, 3, 5, 99, 99)


def dot(a, b, dims=(((1,), (0,)), ((), ()))):
    return lax.dot_general(a, b, dims, preferred_element_type=F32)


def exact(a, b, dims=(((1,), (0,)), ((), ()))):
    return lax.dot_general(a, b, dims, preferred_element_type=F32, precision=lax.Precision.HIGHEST)


def flipped(index, bits, count):
    result, bit = 0, 1
    while bit < count:
        result = result + bit * (((index // bit) % 2 + (bits // bit) % 2) % 2)
        bit *= 2
    return result


def gelu_parts(hidden):
    c0, c1 = 0.7978845608028654, 0.044715
    square = hidden * hidden
    bend = jnp.tanh(hidden * (c0 + (c0 * c1) * square))
    half = 0.5 + 0.5 * bend
    slope = half + (0.5 * hidden) * (1.0 - bend * bend) * (c0 + (3.0 * c0 * c1) * square)
    return hidden * half, slope


def slots_by_row(routes, me, pad, experts):
    count = routes.shape[1]
    picked = routes == lax.broadcasted_iota(jnp.int32, (experts, count), 0)
    first = lax.broadcasted_iota(jnp.int32, (count, count), 0)
    second = lax.broadcasted_iota(jnp.int32, (count, count), 1)
    before = dot(picked.astype(BF16), (first < second).astype(BF16))
    rank = jnp.sum(jnp.where(picked, before, 0.0), axis=0, keepdims=True).astype(jnp.int32)
    return jnp.bitwise_xor(routes, me) * pad + rank


def grow_strip(strip, w8):
    strip[0:8] = w8
    have = 8
    while have < strip.shape[0]:
        strip[have : 2 * have] = pltpu.roll(strip[0:have], have, 1)
        have *= 2


SPILLS = 7


def layer_kernel(n, cap, pad, experts, heads, direct, *refs):
    given, (full_hbm, buckets_hbm, win_hbm, wout_hbm), refs = refs[:9], refs[9:13], refs[13:]
    (mixed_hbm, tokens_grad_hbm, qkv_grad_hbm, *small_hbm), refs = refs[:7], refs[7:]
    (gin_hbm, gout_hbm, probs_hbm, *rest) = refs
    spilled, rest = rest[:SPILLS], rest[SPILLS:]
    (blocks, shard, gains, hot, router, rows, cots, ties, xin, cin, back_in, returned, tie_in, sib_recv,
     sib_in, in1, in2, in3, in4, bias_out, bias_in, bias_pair,
     tokens_ref, cot_ref, qkv_ref, att_ref, router_own, gain_one, gain_two, routes_ref, table_ref, extra_ref,
     qkv_grad_ref, att_grad_ref, extra_grad_ref, gain_grad_ref, bias_grad_ref,
     put_sem, prob_sem, load_sem, pair_sem, swap_send, swap_recv, tree_send, tree_recv, turn_send, turn_recv,
     piece_send, piece_recv, piece_out, hop_send, sib_r, r1, r2, r3, r4, bias_sem, end_sem, given_sem, small_sem) = rest
    held = (tokens_ref, cot_ref, qkv_ref, att_ref, router_own, gain_one, gain_two, routes_ref, table_ref)
    fetches = [pltpu.make_async_copy(src, dst, given_sem.at[i]) for i, (src, dst) in enumerate(zip(given, held))]
    for copy in fetches:
        copy.start()
    dp, me = lax.axis_index("dp"), lax.axis_index("expert")
    count, width = tokens_ref.shape
    total = n * pad
    early = 3 * width + 256
    per = 256 // cap
    sibling = (1 - dp, me)
    staged = per == 4
    lane = lax.broadcasted_iota(jnp.int32, (count, 128), 1)

    def peer(p):
        return dp, flipped(me, p, n)

    def remote(src, dst, send, recv, device):
        return pltpu.make_async_remote_copy(
            src_ref=src, dst_ref=dst, send_sem=send, recv_sem=recv, device_id=device, device_id_type=MESH)

    def swap(kind, p):
        src, dst = ((rows, xin), (cots, cin), (rows, back_in), (cots, returned), (ties, tie_in))[kind]
        index = p // per if kind < 2 else 0
        return remote(src.at[p], dst.at[p], swap_send.at[kind, index], swap_recv.at[kind, index], peer(p))

    def swaps(kind, g=None):
        src, dst = ((rows, xin), (cots, cin), (rows, back_in), (cots, returned), (ties, tie_in))[kind]
        index, low, blocks_of = (0, 1, n - 1) if g is None else (0, 1, per - 1) if isinstance(g, int) else (g, g * per, per)
        place = pl.ds(low, blocks_of)
        return remote(src.at[place], dst.at[place], swap_send.at[kind, index], swap_recv.at[kind, index], peer(1))

    def start_swaps(kind, wanted):
        def one(p, _):
            @pl.when(wanted(p))
            def _():
                swap(kind, p).start()
            return 0

        lax.fori_loop(1, n, one, 0)

    def greet_all(prepare):
        barrier = pltpu.get_barrier_semaphore()

        def greet(p, _):
            pl.semaphore_signal(barrier, inc=1, device_id=peer(p), device_id_type=MESH)
            return 0

        lax.fori_loop(1, n, greet, 0)
        pl.semaphore_signal(barrier, inc=1, device_id=sibling, device_id_type=MESH)
        prepare()
        pl.semaphore_wait(barrier, n)

    half = win_hbm.shape[1] // 2
    steps = half // WIDE
    pieces = [(kind, k) for k in range(steps) for kind in (0, 1)]

    def piece(kind, k):
        place = pl.ds((kind * steps + k) * WIDE, WIDE)
        return remote(blocks.at[:, place], sib_recv.at[kind, k], piece_send.at[kind, k], piece_recv.at[kind, k], sibling)

    def out_piece(kind, k):
        return pltpu.make_async_copy(
            sib_recv.at[kind, k], (gin_hbm, gout_hbm)[kind].at[:, pl.ds(k * WIDE, WIDE)], piece_out.at[kind, k])

    def forward(w, packed, normed, attended, middle, moe_in, chance, probs, strip, bias, ends, weights):
        puts = []

        def put(index, src):
            copy = pltpu.make_async_copy(src, spilled[index], put_sem.at[index])
            copy.start()
            puts.append(copy)

        offsets = [pltpu.make_async_copy(buckets_hbm.at[:, pl.ds(c, 128)], ends.at[i], load_sem.at[i])
                   for i, c in enumerate((0, count - 128))]
        for copy in offsets:
            copy.start()
        def prepare():
            for copy in fetches:
                copy.wait()
            if direct:
                weights[:, : 3 * width] = qkv_ref[...].astype(F32)
                here = weights.shape[0]
                extra_ref[...] = jnp.zeros_like(extra_ref)
                extra_ref[0:experts, 0:here] = router_own[...].astype(F32)
                for i, one in enumerate((gain_one, gain_two)):
                    extra_ref[128 + i : 129 + i, 0:here] = one[...].astype(F32).reshape(1, here)
                weights[:, 3 * width : early] = extra_ref[...].T[:here]
                weights[:, early:] = att_ref[...].astype(F32)

        greet_all(prepare)
        if direct:
            own = weights.shape[0]
            block = 2 * own
            pair = remote(weights, shard, pair_sem.at[0], pair_sem.at[1], sibling)
            pair.start()
        else:
            load = pltpu.make_async_copy(full_hbm, w, pair_sem.at[0])
            load.start()
        slots = slots_by_row(routes_ref[...], me, pad, experts)

        def to_slots(values):
            hits = (slots == lax.broadcasted_iota(jnp.int32, (total, count), 0)).astype(BF16)
            return dot(hits, values).astype(BF16).reshape(n, pad, width)

        def make_cots():
            cots[...] = to_slots(cot_ref[...])
            cin[0] = cots[0]

        def make_bias():
            for copy in offsets:
                copy.wait()
            last, first = ends[1].astype(F32).T[127:128], ends[0].astype(F32).T[0:1]
            line = jnp.concatenate([last, pltpu.roll(first, count - 1, 1)], axis=1)
            line = pltpu.roll(jnp.broadcast_to(line, (8, 2 * count)), 2 * count - 127, 1)[0:1]
            hot[...] = (line.astype(jnp.int32) == lax.broadcasted_iota(jnp.int32, hot.shape, 0)).astype(F32)
            table = exact(table_ref[...], hot[...])
            for h in range(heads):
                row = jnp.broadcast_to(table[h : h + 1], (8, 2 * count))
                place = lax.broadcasted_iota(jnp.int32, row.shape, 0)
                shifted = row
                for r in range(1, 8):
                    shifted = jnp.where(place == r, pltpu.roll(row, r, 1), shifted)
                bias[h] = shifted

        if direct:
            pair.wait()
            mine, other = weights[...], shard[...]
            blocks[pl.ds(pl.multiple_of(me * block, 16), block), : w.shape[1]] = jnp.concatenate(
                [jnp.where(dp == 0, mine, other), jnp.where(dp == 0, other, mine)], axis=0).astype(BF16)
            second, third = 2 - dp, 1 + dp
            far = list(range(4, n, 4))
            near = [0] + far

            def at(t, r, core):
                start, size = ((0, early // 2), (early, width // 2))[t]
                return blocks.at[pl.ds(pl.multiple_of(flipped(me, r, n) * block, 16), block),
                                 pl.ds(pl.multiple_of(start + core * size, 128), size)]

            def hop(t, r, step):
                return remote(at(t, r, dp), at(t, r, dp), tree_send.at[t], tree_recv.at[t, r + step], peer(step))

            def arrived(t, r):
                remote(at(t, r, dp), at(t, r, dp), tree_send.at[t], tree_recv.at[t, r], peer(r)).wait_recv()

            def to_sibling(t, r, core):
                return remote(at(t, r, core), at(t, r, core), turn_send.at[t], turn_recv.at[t], sibling)

            def bulk(t, send, recv):
                place = blocks.at[: (n - 1) * block, : (early // 2, width // 2)[t]]
                return remote(place, place, send.at[t], recv.at[t] if recv is turn_recv else recv.at[t, 0], sibling)

            def turn(t, step):
                if step == 0:
                    hop(t, 0, 8).start()
                    hop(t, 0, 4).start()
                    hop(t, 0, third).start()
                    hop(t, 0, second).start()
                elif step == 1:
                    for r in (8, 4, 12):
                        arrived(t, r)
                        if r == 8:
                            hop(t, 8, 4).start()
                        hop(t, r, third).start()
                        hop(t, r, second).start()
                        to_sibling(t, r, dp).start()
                elif step == 2:
                    for r in near:
                        arrived(t, r + second)
                        hop(t, r + second, third).start()
                        to_sibling(t, r + second, dp).start()
                elif step == 3:
                    for r in near:
                        arrived(t, r + third)
                        to_sibling(t, r + third, dp).start()
                        arrived(t, r + 3)
                        to_sibling(t, r + 3, dp).start()
                else:
                    bulk(t, turn_send, turn_recv).wait_recv()
                    place = (slice(0, early), slice(early, w.shape[1]))[t]
                    for core in (0, 1):
                        for q in range(n // 2):
                            low = 2 * q * block + core * own
                            pair_rows = [blocks[p : p + own, place].astype(F32) for p in (low, low + block)]
                            w[core * own * n + q * block : core * own * n + (q + 1) * block, place] = jnp.concatenate(
                                pair_rows, axis=0).astype(BF16)

            turn(0, 0)
            make_bias()
            make_cots()
            turn(0, 1)
            turn(1, 0)
            start_swaps(1, lambda p: p % 4 == 0)
            turn(0, 2)
            turn(1, 1)
            turn(0, 3)
            turn(1, 2)
            start_swaps(1, lambda p: p % 4 != 0)
            turn(0, 4)
        else:
            make_bias()
            make_cots()
            start_swaps(1, lambda p: p > 0)
            load.wait()
        gains[...] = w[:, 3 * width + 128 : early].astype(F32).T[0:8]
        router[...] = w[:, 3 * width : 3 * width + 128]
        x = tokens_ref[...].astype(F32)
        normed[...] = (x * lax.rsqrt(jnp.mean(x * x, axis=1, keepdims=True) + EPSILON) * gains[0:1]).astype(BF16)
        put(0, normed)
        for c in range(3):
            cols_c = slice(c * width, (c + 1) * width)
            packed[:, cols_c] = dot(normed[...], w[:, cols_c]).astype(BF16)
        put(1, packed)
        scale = (width // heads) ** -0.5

        def put_probs(k):
            return pltpu.make_async_copy(probs.at[pl.ds(2 * k, 2)], probs_hbm.at[pl.ds(2 * k, 2)], prob_sem.at[0])

        def attend(k, _):
            def part(c):
                return packed[:, pl.ds(pl.multiple_of(c * width + k * 128, 128), 128)]

            queries = (part(0).astype(F32) * scale).astype(BF16)
            keys = part(1)
            values = part(2).astype(F32).T.astype(BF16)
            outs = []
            for h in (0, 1):
                grow_strip(strip, bias[2 * k + h])
                own_keys = jnp.where((lane < 64) == (h == 0), keys, jnp.zeros_like(keys))
                scores = dot(own_keys, queries, NT)
                scores = jnp.concatenate(
                    [scores[128 * b : 128 * b + 128] + strip[:, 384 - 128 * b : 896 - 128 * b] for b in range(4)], axis=0)
                powers = jnp.exp(scores - jnp.max(scores, axis=0, keepdims=True))
                part_weights = (powers * (1.0 / jnp.sum(powers, axis=0, keepdims=True))).astype(BF16)
                probs[2 * k + h] = part_weights
                outs.append(dot(values[64 * h : 64 * h + 64], part_weights))
            put_probs(k).start()
            attended[:, pl.ds(pl.multiple_of(k * 128, 128), 128)] = jnp.concatenate(outs, axis=0).T.astype(BF16)
            if direct:
                for step in (3, 4):
                    @pl.when(k == step + 1)
                    def _():
                        turn(1, step)
            return 0

        lax.fori_loop(0, heads // 2, attend, 0)
        mid = tokens_ref[...].astype(F32) + dot(attended[...], w[:, early:])
        middle[...] = mid
        moe = (mid * lax.rsqrt(jnp.mean(mid * mid, axis=1, keepdims=True) + EPSILON) * gains[1:2]).astype(BF16)
        moe_in[...] = moe
        rows[...] = to_slots(moe)
        start_swaps(0, lambda p: (p < 4) | ((p % 4 == 0) & (p < 12)) if staged else p > 0)
        xin[0] = rows[0]
        put(2, attended)
        put(3, middle)
        put(4, moe_in)
        put(5, w)
        logits = dot(moe, router[...])
        logits = jnp.where(lane < experts, logits, -1e30)
        powers = jnp.exp(logits - jnp.max(logits, axis=1, keepdims=True))
        chance[...] = powers / jnp.sum(powers, axis=1, keepdims=True)
        put(6, chance)
        if direct:
            for t in (0, 1):
                bulk(t, tree_send, tree_recv).wait_send()
                bulk(t, turn_send, turn_recv).wait_send()
        for copy in puts:
            copy.wait()
        pltpu.make_async_copy(probs, probs_hbm, prob_sem.at[0]).wait()

    def experts_both(win, wout, xt, rt, act, hgr):
        ff = win.shape[1]
        group_rows = per * cap
        chunk = 1024
        loads = [pltpu.make_async_copy(win_hbm, win, load_sem.at[0]), pltpu.make_async_copy(wout_hbm, wout, load_sem.at[1])]
        for load in loads:
            load.start()

        def packed_rows(ref, g):
            block = ref[pl.ds(g * per, per)].reshape(per * pad, width)
            if pad == cap:
                return block
            r = lax.broadcasted_iota(jnp.int32, (group_rows, per * pad), 0)
            c = lax.broadcasted_iota(jnp.int32, (group_rows, per * pad), 1)
            return dot(((r // cap) * pad + r % cap == c).astype(BF16), block).astype(BF16)

        def spread_rows(block):
            if pad == cap:
                return block.reshape(per, pad, width)
            r = lax.broadcasted_iota(jnp.int32, (per * pad, group_rows), 0)
            c = lax.broadcasted_iota(jnp.int32, (per * pad, group_rows), 1)
            pick = (r // pad == c // cap) & (r % pad == c % cap)
            return dot(pick.astype(BF16), block).astype(BF16).reshape(per, pad, width)

        def group(g, _):
            def over(act_on):
                def one(j, _):
                    @pl.when(g * per + j != 0)
                    def _():
                        act_on(g * per + j)
                    return 0

                lax.fori_loop(0, per, one, 0)

            def all_of(kind, act_on):
                @pl.when(g == 0)
                def _():
                    act_on(swaps(kind, 0))

                @pl.when(g != 0)
                def _():
                    act_on(swaps(kind, g))

            all_of(0, lambda copies: copies.wait_recv())

            @pl.when(g == 0)
            def _():
                if staged:
                    start_swaps(0, lambda p: (p >= 4) & (p % 4 != 0) & (p < 12))
                for load in loads:
                    load.wait()

            if staged:
                @pl.when(g == 1)
                def _():
                    start_swaps(0, lambda p: p >= 12)

            all_of(1, lambda copies: copies.wait_recv())
            here = pl.ds(pl.multiple_of(g * group_rows, group_rows), group_rows)
            x = packed_rows(xin, g)
            logits = dot(x, router[...])
            lanes = lax.broadcasted_iota(jnp.int32, logits.shape, 1)
            logits = jnp.where(lanes < experts, logits, -1e30)
            powers = jnp.exp(logits - jnp.max(logits, axis=1, keepdims=True))
            gate = jnp.sum(jnp.where(lanes == me, powers, 0.0), axis=1, keepdims=True) / jnp.sum(
                powers, axis=1, keepdims=True)
            r = (gate * packed_rows(cin, g).astype(F32)).astype(BF16)
            xt[:, here] = x.T
            rt[:, here] = r.T

            def hidden_chunk(k, _):
                cols = pl.ds(pl.multiple_of(k * chunk, chunk), chunk)
                value, slope = gelu_parts(dot(x, win[:, cols]))
                act[here, cols] = value.astype(BF16)
                hgr[here, cols] = (dot(r, wout[:, cols]) * slope).astype(BF16)
                return 0

            lax.fori_loop(0, ff // chunk, hidden_chunk, 0)
            back = spread_rows(dot(hgr[here], win[...], NT).astype(BF16))
            all_of(0, lambda copies: copies.wait_send())
            rows[pl.ds(g * per, per)] = back
            over(lambda p: swap(2, p).start())
            produced = dot(act[here], wout[...], NT).astype(BF16)
            tie = jnp.sum(r.astype(F32) * produced.astype(F32), axis=1, keepdims=True)
            for j in range(per):
                row = jnp.broadcast_to(tie[j * cap : (j + 1) * cap], (cap, 128)).T[0:8]
                ties[g * per + j] = jnp.concatenate([row, jnp.zeros((8, 128 - cap), F32)], axis=1)
            over(lambda p: swap(4, p).start())
            all_of(1, lambda copies: copies.wait_send())
            cots[pl.ds(g * per, per)] = spread_rows(produced)

            @pl.when(g < n // per // 2)
            def _():
                over(lambda p: swap(3, p).start())

            return 0

        lax.fori_loop(0, n // per, group, 0)
        back_in[0] = rows[0]
        tie_in[0] = ties[0]
        returned[0] = cots[0]

        def partial(kind, owner, k):
            cols = pl.ds(pl.multiple_of(owner * half + k * WIDE, 128), WIDE)
            return dot(xt[...], hgr[:, cols]) if kind == 0 else dot(rt[...], act[:, cols])

        for kind, k in pieces:
            place = (kind * steps + k) * WIDE
            blocks[:, place : place + WIDE] = partial(kind, 1 - dp, k).astype(BF16)
            piece(kind, k).start()
        for kind, k in pieces:
            value = partial(kind, dp, k)
            piece(kind, k).wait_recv()
            sib_recv[kind, k] = (value + sib_recv[kind, k].astype(F32)).astype(BF16)
            out_piece(kind, k).start()

    def backward(w, packed, normed, attended, middle, moe_in, chance, prob, mid_grad, att_cot, packed_grad, normed_t, chunk,
                 strip, bias_rows, mine, keep, out1, out2, out3, out4):
        loaded = (normed, packed, attended, middle, moe_in, w, chance)
        loads = [pltpu.make_async_copy(spilled[i], loaded[i], load_sem.at[i]) for i in range(SPILLS)]
        order = (6, 3, 5, 2, 4, 0, 1)
        for i in order:
            loads[i].start()

        def fetch(k):
            return pltpu.make_async_copy(probs_hbm.at[pl.ds(2 * k, 2)], prob.at[k % 2], prob_sem.at[k % 2])

        fetch(0).start()
        own = qkv_ref.shape[0]
        lead = (width + 256 + PART - 1) // PART
        chunks = lead + heads // 2

        if direct:
            half_rows = own * n

            steps_out = ((out1, in1, r1), (out2, in2, r2), (out3, in3, r3), (out4, in4, r4))
            ways = (1 + dp, 2 - dp, 4, 8)

            def sib_out(k):
                across = blocks.shape[1] // PART
                return blocks.at[pl.ds(pl.multiple_of((k // across) * half_rows, 16), half_rows),
                                 pl.ds(pl.multiple_of((k % across) * PART, 128), PART)]

            def hop(stage, k):
                if stage == 0:
                    return remote(sib_out(k), sib_in.at[k], hop_send.at[0], sib_r.at[k], sibling)
                src, dst, recv = steps_out[stage - 1]
                return remote(src.at[k], dst.at[k], hop_send.at[stage], recv.at[k], peer(ways[stage - 1]))

            def unit(k, u):
                r = ways[0] * (u // 4) + ways[1] * ((u // 2) % 2) + ways[2] * (u % 2)
                places = [pl.multiple_of(flipped(me, r + z, n) * own, 8) for z in (0, ways[3])]
                return jnp.concatenate([mine[k % 2, pl.ds(place, own)] for place in places], axis=0)

            def stage(s, k):
                if s == 0:
                    there = pl.ds(pl.multiple_of((1 - dp) * half_rows, 8), half_rows)
                    here = pl.ds(pl.multiple_of(dp * half_rows, 8), half_rows)
                    sib_out(k)[...] = chunk[there].astype(BF16)
                    hop(0, k).start()
                    mine[k % 2] = chunk[here]
                elif s == 1:
                    hop(0, k).wait_recv()
                    mine[k % 2] = mine[k % 2] + sib_in[k].astype(F32)
                    for u in range(4):
                        out1[k, 2 * own * u : 2 * own * (u + 1)] = unit(k, u + 4).astype(BF16)
                    hop(1, k).start()
                    for u in range(4):
                        keep[k, 2 * own * u : 2 * own * (u + 1)] = unit(k, u)
                elif s in (2, 3):
                    src, dst = steps_out[s - 1][0], steps_out[s - 2][1]
                    left = 8 * own // (1 << (s - 1))
                    hop(s - 1, k).wait_recv()
                    value = keep[k, : 2 * left] + dst[k].astype(F32)
                    src[k] = value[left:].astype(BF16)
                    hop(s, k).start()
                    keep[k, :left] = value[:left]
                elif s == 4:
                    hop(3, k).wait_recv()
                    value = keep[k, : 2 * own] + in3[k].astype(F32)
                    out4[k] = jnp.concatenate(
                        [value[own:, 128 * c : 128 * (c + 1)] for c in range(3)]
                        + [jnp.zeros((out4.shape[1] - 3 * own, 128), F32)], axis=0).astype(BF16)
                    hop(4, k).start()
                    keep[k, :own] = value[:own]
                else:
                    hop(4, k).wait_recv()
                    far = in4[k].astype(F32)
                    keep[k, :own] = keep[k, :own] + jnp.concatenate(
                        [far[own * c : own * (c + 1)] for c in range(3)], axis=1)

            def advance(k):
                stage(0, k)
                for s in range(1, 6):
                    @pl.when((k - LAG[s] >= 0) & (k - LAG[s] < chunks))
                    def _():
                        stage(s, k - LAG[s])

            done = {k: max(s for s in range(6) if LAG[s] <= chunks - 1 - k) for k in range(chunks)}

            def drain(last, *which):
                for k in which or range(chunks):
                    while done[k] < last:
                        done[k] += 1
                        stage(done[k], k)

        else:
            def advance(k):
                copy = pltpu.make_async_copy(chunk, qkv_grad_hbm.at[k], end_sem.at[0])
                copy.start()
                copy.wait()

            def drain(*_):
                pass

        expert_of = jnp.broadcast_to(routes_ref[...].astype(F32), (128, count)).T[:, 0:1].astype(jnp.int32)
        picked = expert_of == lane
        first = lax.broadcasted_iota(jnp.int32, (count, count), 0)
        other = lax.broadcasted_iota(jnp.int32, (count, count), 1)
        before = dot((other < first).astype(BF16), picked.astype(BF16))
        rank = jnp.sum(jnp.where(picked, before, 0.0), axis=1, keepdims=True).astype(jnp.int32)
        place = jnp.bitwise_xor(expert_of, me)
        hits = (place * pad + rank == lax.broadcasted_iota(jnp.int32, (count, total), 1)).astype(BF16)

        def each_peer(act_on):
            def one(p, _):
                act_on(p)
                return 0

            lax.fori_loop(1, n, one, 0)

        for kind, k in pieces:
            piece(kind, k).wait_send()
        swaps(2).wait_recv()
        swaps(4).wait_recv()
        ties_row = exact((place == lax.broadcasted_iota(jnp.int32, (count, n), 1)).astype(F32), jnp.max(tie_in[...], axis=1))
        tie = jnp.sum(jnp.where(lane == rank, ties_row, 0.0), axis=1, keepdims=True)
        for i in order[:1]:
            loads[i].wait()
        logit_grad = (tie * (picked.astype(F32) - chance[...])).astype(BF16)
        grad = dot(hits, back_in[...].reshape(total, width))
        for i in order[1:]:
            loads[i].wait()
        grad = grad + dot(logit_grad, router[...], NT)
        mid = middle[...]
        root = lax.rsqrt(jnp.mean(mid * mid, axis=1, keepdims=True) + EPSILON)
        unit_mid = mid * root
        gain_rows = jnp.sum(grad * unit_mid, axis=0, keepdims=True)
        scaled = grad * gains[1:2]
        mid_g = cot_ref[...].astype(F32) + root * (scaled - unit_mid * jnp.mean(scaled * unit_mid, axis=1, keepdims=True))
        mid_grad[...] = mid_g
        attn_grad = mid_g.astype(BF16)
        att_cot[...] = dot(attn_grad, w[:, early:], NT).astype(BF16)
        attended_t = attended[...].T
        for k in range(lead):
            if (k + 1) * PART <= width:
                chunk[...] = dot(attended_t, attn_grad[:, k * PART : (k + 1) * PART])
            else:
                chunk[:, 0:128] = dot(moe_in[...].T, logit_grad)
                chunk[:, 128:256] = jnp.broadcast_to(gain_rows, (128, width)).T
                chunk[:, 256:] = jnp.zeros((width, PART - 256), F32)
            advance(k)
        normed_t[...] = normed[...].T
        swaps(2).wait_send()
        start_swaps(3, lambda p: (p >= n // 2) & (p % 4 == 0))

        scale = (width // heads) ** -0.5

        def attend_back(k, _):
            fetch(k).wait()

            @pl.when(k + 1 < heads // 2)
            def _():
                fetch(k + 1).start()

            def part(c):
                return packed[:, pl.ds(pl.multiple_of(c * width + k * 128, 128), 128)]

            queries, keys, values = part(0), part(1), part(2)
            keys_t = (keys.astype(F32) * scale).T.astype(BF16)
            cot = att_cot[:, pl.ds(pl.multiple_of(k * 128, 128), 128)]
            query_t, key_g, value_g = [], None, None
            for h in (0, 1):
                mask = (lane < 64) == (h == 0)
                own_cot = jnp.where(mask, cot, jnp.zeros_like(cot))
                own_queries = jnp.where(mask, queries, jnp.zeros_like(queries))
                weights = prob[k % 2, h]
                chances = weights.astype(F32)
                product = chances * dot(values, own_cot, NT)
                score_grad = (product - chances * jnp.sum(product, axis=0, keepdims=True)).astype(BF16)
                wide = score_grad.astype(F32)
                for b in range(4):
                    block = wide[128 * b : 128 * b + 128]
                    cols = slice(384 - 128 * b, 896 - 128 * b)
                    if b == 0:
                        strip[:, cols] = block
                        strip[:, 0:384] = jnp.zeros((128, 384), F32)
                        strip[:, 896:1024] = jnp.zeros((128, 128), F32)
                    else:
                        strip[:, cols] += block
                have = 64
                folded = strip[...]
                while have >= 8:
                    folded = folded[:have] + pltpu.roll(folded[have:], 1024 - have, 1)
                    have //= 2
                for s in range(1, 8):
                    folded = jnp.where(lax.broadcasted_iota(jnp.int32, folded.shape, 0) == s,
                                       pltpu.roll(folded, 1024 - s, 1), folded)
                bias_rows[2 * k + h] = folded
                v = dot(weights, own_cot)
                q = dot(score_grad, own_queries)
                value_g = v if h == 0 else value_g + v
                key_g = q if h == 0 else key_g + q
                query_t.append(dot(keys_t[64 * h : 64 * h + 64], score_grad))
            query_g = jnp.concatenate(query_t, axis=0).T.astype(BF16)
            grads = jnp.concatenate([query_g, (key_g * scale).astype(BF16), value_g.astype(BF16)], axis=1)
            for c in range(3):
                packed_grad[:, pl.ds(pl.multiple_of(c * width + k * 128, 128), 128)] = grads[:, c * 128 : (c + 1) * 128]
            chunk[...] = dot(normed_t[...], grads)
            advance(k + lead)

            @pl.when(k == 0)
            def _():
                start_swaps(3, lambda p: (p >= n // 2) & (p % 4 == 1))

            @pl.when(k == 0)
            def _():
                start_swaps(3, lambda p: (p >= n // 2) & (p % 4 == 2))

            @pl.when(k == 0)
            def _():
                start_swaps(3, lambda p: (p >= n // 2) & (p % 4 == 3))

            return 0

        lax.fori_loop(0, heads // 2, attend_back, 0)
        drain(1, chunks - 1)
        drain(2, *range(chunks - 1))
        drain(3, *range(chunks - 3))
        sums = jnp.concatenate([jnp.sum(bias_rows[h], axis=0, keepdims=True) for h in range(heads)], axis=0)
        bias_out[...] = exact(sums, hot[...], NT)
        if direct:
            pair_hop = remote(bias_out, bias_pair, pair_sem.at[2], pair_sem.at[3], sibling)
            pair_hop.start()

            def bias_hop(p):
                return remote(bias_in.at[me], bias_in.at[me], bias_sem.at[0], bias_sem.at[1], peer(p))

            place = bias_in.at[1:]
            bias_all = remote(place, place, bias_sem.at[0], bias_sem.at[1], peer(1))

        normed_grad = dot(packed_grad[...], w[:, : 3 * width], NT)
        drain(2)
        drain(3, *range(chunks - 1))
        drain(4, *range(chunks - 4))
        if direct:
            pair_hop.wait()
            bias_in[me] = bias_out[...] + bias_pair[...]
            each_peer(lambda p: bias_hop(p).start())
        x = tokens_ref[...].astype(F32)
        root = lax.rsqrt(jnp.mean(x * x, axis=1, keepdims=True) + EPSILON)
        unit_x = x * root
        scaled = normed_grad * gains[0:1]
        mid_grad[...] = mid_grad[...] + root * (scaled - unit_x * jnp.mean(scaled * unit_x, axis=1, keepdims=True))
        ends = [pltpu.make_async_copy(mid_grad, tokens_grad_hbm, end_sem.at[0]),
                pltpu.make_async_copy(att_cot, mixed_hbm, end_sem.at[1])]
        ends[0].start()
        drain(3)
        drain(4, *range(chunks - 1))
        swaps(3).wait_recv()
        gate = jnp.sum(jnp.where(picked, chance[...], 0.0), axis=1, keepdims=True)
        att_cot[...] = (middle[...] + gate * dot(hits, returned[...].reshape(total, width))).astype(BF16)
        ends[1].start()
        if direct:
            drain(4)
            drain(5)
            bias_all.wait_recv()
            total_bias = bias_in[0]
            for p in range(1, n):
                total_bias = total_bias + bias_in[p]
            bias_grad_ref[...] = total_bias
            for k in range(chunks):
                result = keep[k, :own]
                if k >= lead:
                    for c in range(3):
                        start = c * width + (k - lead) * 128
                        qkv_grad_ref[:, start : start + 128] = result[:, c * 128 : (c + 1) * 128]
                elif (k + 1) * PART <= width:
                    att_grad_ref[:, k * PART : (k + 1) * PART] = result
                else:
                    extra_grad_ref[...] = result[:, :256]
            total_gain = jnp.sum(qkv_grad_ref[...] * qkv_ref[...].astype(F32), axis=1, keepdims=True)
            gain_grad_ref[...] = jnp.broadcast_to(total_gain / extra_ref[128:256].T[:own, 0:1], gain_grad_ref.shape)

            for s, sent in enumerate((sib_in, out1, out2, out3, out4)):
                remote(sent, sent, hop_send.at[s], sib_r.at[0], sibling).wait_send()
            bias_all.wait_send()
        else:
            bias_grad_ref[...] = bias_out[...]
        small = [*zip((att_grad_ref, extra_grad_ref, gain_grad_ref, bias_grad_ref), small_hbm)]
        if direct:
            small.append((qkv_grad_ref, qkv_grad_hbm))
        for i, (src, dst) in enumerate(small):
            ends.append(pltpu.make_async_copy(src, dst, small_sem.at[i]))
            ends[-1].start()
        for kind in (3, 4):
            swaps(kind).wait_send()
        for copy in ends:
            copy.wait()
        for kind, k in pieces:
            out_piece(kind, k).wait()

    wide = w_columns(width)
    scratch = pltpu.VMEM
    shared = [
        scratch((width, wide), BF16), scratch((count, 3 * width), BF16), scratch((count, width), BF16),
        scratch((count, width), BF16), scratch((count, width), F32), scratch((count, width), BF16), scratch((count, 128), F32),
    ]
    own_rows = qkv_ref.shape[0]
    pl.run_scoped(
        forward, *shared, scratch((heads, count, count), BF16), scratch((128, 2 * count), F32),
        scratch((heads, 8, 2 * count), F32), scratch((2, count, 128), jnp.int32),
        scratch((own_rows, wide) if direct else (8, 128), F32))
    pl.run_scoped(
        experts_both, *[scratch((width, win_hbm.shape[1]), BF16) for _ in range(2)],
        *[scratch((width, n * cap), BF16) for _ in range(2)], *[scratch((n * cap, win_hbm.shape[1]), BF16) for _ in range(2)])
    all_chunks = (width + 256 + PART - 1) // PART + heads // 2

    def buffer(shape, kind):
        return scratch((all_chunks, *shape) if direct else (8, 128), kind)

    pl.run_scoped(
        backward, *shared, scratch((2, 2, count, count), BF16), scratch((count, width), F32), scratch((count, width), BF16),
        scratch((count, 3 * width), BF16), scratch((width, count), BF16), scratch((width, PART), F32),
        scratch((128, 2 * count), F32), scratch((heads, 8, 2 * count), F32),
        scratch((2, own_rows * n, PART), F32), buffer((8 * own_rows, PART), F32),
        *[buffer((own_rows << s, PART), BF16) for s in (3, 2, 1)], buffer((-(-3 * own_rows // 16) * 16, 128), BF16))


def w_columns(width):
    return 4 * width + 256


def layer(n, cap, pad, experts, heads, direct, tokens, cotangent, qkv, att, router, one, two, full, routes, table, buckets,
          win, wout):
    count, width = tokens.shape
    wide = w_columns(width)
    own = qkv.shape[0]
    kinds = table.shape[1]
    ff = win.shape[1]
    chunks = (width + 256 + PART - 1) // PART + heads // 2
    steps = ff // 2 // WIDE
    short = -(-3 * own // 16) * 16
    any_ = pl.BlockSpec(memory_space=pl.ANY)
    dma = pltpu.SemaphoreType.DMA
    scratch = pltpu.VMEM
    shape = jax.ShapeDtypeStruct

    def landing(*rest):
        return scratch((chunks, *rest) if direct else (16, 128), BF16)

    small = ((own, width), (own, 256), (own, 128), (heads, kinds))
    outs = [
        (shape((count, width), BF16), any_), (shape((count, width), F32), any_),
        (shape((own, 3 * width) if direct else (chunks, width, PART), F32), any_),
        *[(shape(dims, F32), any_) for dims in small], (shape((width, ff // 2), BF16), any_), (shape((width, ff // 2), BF16), any_),
        (shape((heads, count, count), BF16), any_), (shape((count, width), BF16), any_),
        (shape((count, 3 * width), BF16), any_), (shape((count, width), BF16), any_), (shape((count, width), F32), any_),
        (shape((count, width), BF16), any_), (shape((width, wide), BF16), any_), (shape((count, 128), F32), any_),
    ]
    slots = scratch((n, pad, width), BF16)
    given = (tokens, cotangent, qkv, att, router, one, two, routes, table)
    return pl.pallas_call(
        functools.partial(layer_kernel, n, cap, pad, experts, heads, direct),
        out_shape=tuple(o[0] for o in outs),
        in_specs=[any_] * 13,
        out_specs=tuple(o[1] for o in outs),
        scratch_shapes=[
            scratch((width, max(wide, 2 * steps * WIDE)), BF16),
            scratch((own, wide) if direct else (8, 128), F32),
            scratch((8, width), F32), scratch((kinds, 2 * count), F32), scratch((width, 128), BF16),
            slots, slots, scratch((n, 8, 128), F32), slots, slots, slots, slots, scratch((n, 8, 128), F32),
            scratch((2, steps, width, WIDE), BF16),
            landing(own * n, PART), *[landing(own << s, PART) for s in (3, 2, 1)], landing(short, 128),
            scratch((heads, kinds), F32), scratch((n, heads, kinds), F32), scratch((heads, kinds), F32),
            *[scratch(a.shape, a.dtype) for a in given], scratch((256, 128), F32), scratch((own, 3 * width), F32), *[scratch(dims, F32) for dims in small],
            dma((SPILLS,)), dma((2,)), dma((SPILLS,)), dma((4,)), dma((5, n * cap // 256)), dma((5, n * cap // 256)),
            dma((2,)), dma((2, n)), dma((2,)), dma((2,)),
            dma((2, steps)), dma((2, steps)), dma((2, steps)),
            dma((5,)), *[dma((chunks,)) for _ in range(5)], dma((2,)), dma((2,)), dma((9,)), dma((5,)),
        ],
        compiler_params=pltpu.CompilerParams(
            collective_id=1, has_side_effects=True, vmem_limit_bytes=63 * 1024 * 1024),
        name="layer",
    )(*given, full, buckets, win, wout)


def finish_kernel(
    mixed_in, tokens_in, in_hbm, out_hbm, *refs,
):
    small_ins, (mixed_out, tokens_out, in_out, out_out), small_outs, refs = refs[:5], refs[5:9], refs[9:15], refs[15:]
    (mixed, tokens, narrow, wide, sem, load_sem, store_sem, small_sem) , held = refs[:8], refs[8:]
    fetches = [pltpu.make_async_copy(src, dst, small_sem.at[i]) for i, (src, dst) in enumerate(zip(small_ins, held[:5]))]
    leaves = [pltpu.make_async_copy(src, dst, small_sem.at[5 + i]) for i, (src, dst) in enumerate(zip(held[5:], small_outs))]
    qkv_in, att_in, extra_in, gain_in, bias_in, qkv_out, att_out, router_out, gain_out, gain_moe_out, bias_out = held
    for copy in fetches:
        copy.start()
    ins = [pltpu.make_async_copy(mixed_in, mixed, sem.at[0]), pltpu.make_async_copy(tokens_in, tokens, sem.at[1])]
    outs = [pltpu.make_async_copy(mixed, mixed_out, sem.at[2]), pltpu.make_async_copy(tokens, tokens_out, sem.at[3])]
    parts, rows = narrow.shape[1], narrow.shape[2]

    def load(kind, k):
        return pltpu.make_async_copy(
            (in_hbm, out_hbm)[kind].at[pl.ds(k * rows, rows)], narrow.at[kind, k], load_sem.at[kind, k])

    def store(kind, k):
        return pltpu.make_async_copy(
            wide.at[kind, k], (in_out, out_out)[kind].at[0, pl.ds(k * rows, rows)], store_sem.at[kind, k])

    for copy in ins:
        copy.start()
    for k in range(parts):
        for kind in (0, 1):
            load(kind, k).start()
    for k in range(parts):
        for kind in (0, 1):
            load(kind, k).wait()
            wide[kind, k] = narrow[kind, k].astype(F32)
            store(kind, k).start()
        if k == 1:
            for copy_in, copy_out in zip(ins, outs):
                copy_in.wait()
                copy_out.start()
    for copy in fetches:
        copy.wait()
    qkv_out[...] = qkv_in[...]
    att_out[...] = att_in[...]
    router_out[...] = extra_in[:, :128].T[: router_out.shape[0]]
    gain_out[...] = gain_in[...].T[0:1]
    gain_moe_out[...] = extra_in[:, 128:].T[0:1]
    bias_out[...] = bias_in[...]
    for copy in leaves:
        copy.start()
    for k in range(parts):
        for kind in (0, 1):
            store(kind, k).wait()
    for copy in outs + leaves:
        copy.wait()


def finish(experts, mixed, tokens_grad, grad_in, grad_out, qkv, att, extra, gain, bias):
    any_ = pl.BlockSpec(memory_space=pl.ANY)
    dma = pltpu.SemaphoreType.DMA
    parts = 8
    rows = grad_in.shape[0] // parts
    own = qkv.shape[0]
    shape = jax.ShapeDtypeStruct
    small = (qkv.shape, att.shape, (experts, own), (1, own), (1, own), bias.shape)
    return pl.pallas_call(
        finish_kernel,
        out_shape=(
            shape(mixed.shape, BF16), shape(tokens_grad.shape, F32), shape((1, *grad_in.shape), F32),
            shape((1, *grad_out.shape), F32), *[shape(dims, F32) for dims in small],
        ),
        in_specs=[any_] * 9,
        out_specs=tuple([any_] * 10),
        scratch_shapes=[
            pltpu.VMEM(mixed.shape, BF16),
            pltpu.VMEM(tokens_grad.shape, F32),
            pltpu.VMEM((2, parts, rows, grad_in.shape[1]), BF16),
            pltpu.VMEM((2, parts, rows, grad_in.shape[1]), F32),
            dma((4,)), dma((2, parts)), dma((2, parts)), dma((11,)),
            *[pltpu.VMEM(dims, F32) for dims in (*[a.shape for a in (qkv, att, extra, gain, bias)], *small)],
        ],
        compiler_params=pltpu.CompilerParams(vmem_limit_bytes=60 * 1024 * 1024),
        name="finish",
    )(mixed, tokens_grad, grad_in, grad_out, qkv, att, extra, gain, bias)


def shards(
    n, tokens, cotangent, routes, buckets, gain_attn, w_qkv, w_att, rel_bias, gain_moe, w_router, w_in, w_out,
):
    axes = ("dp", "expert")
    count, width = tokens.shape
    experts = w_router.shape[1]
    heads = rel_bias.shape[1]
    own = w_qkv.shape[0]
    cap = max(2, 2 * count // experts)
    pad = max(16, cap)
    direct = n == 16 and own % 8 == 0
    if direct:
        full = w_att
    else:
        extra = jnp.concatenate(
            [w_router, jnp.zeros((own, 128 - experts), BF16), gain_attn[:, None], gain_moe[:, None],
             jnp.zeros((own, 126), BF16)], axis=1)
        full = lax.all_gather(jnp.concatenate([w_qkv, extra, w_att], axis=1), axes, axis=0, tiled=True)
    mixed, grad_tokens, grad_qkv, grad_att, grad_extra, grad_gain, grad_bias, grad_in, grad_out = layer(
        n, cap, pad, experts, heads, direct, tokens, cotangent, w_qkv, w_att, w_router.T, gain_attn, gain_moe, full, routes.T,
        rel_bias.T, buckets,        w_in[0], w_out[0])[:9]
    if not direct:
        lead = grad_qkv.shape[0] - heads // 2
        early = jnp.concatenate([grad_qkv[k] for k in range(lead)], axis=1)
        late = [grad_qkv[lead:, :, c * 128 : (c + 1) * 128].transpose(1, 0, 2).reshape(width, width) for c in range(3)]
        both = lax.psum_scatter(jnp.concatenate([early, *late], axis=1), axes, scatter_dimension=0, tiled=True)
        grad_att, grad_extra = both[:, :width], both[:, width : width + 256]
        grad_qkv = both[:, early.shape[1] :]
        grad_gain = jnp.sum(grad_qkv * w_qkv.astype(F32), axis=1, keepdims=True) / gain_attn.astype(F32)[:, None]
        grad_gain = jnp.broadcast_to(grad_gain, (own, 128))
        grad_bias = lax.psum(grad_bias, axes)
    mixed, grad_tokens, grad_in, grad_out, grad_qkv, grad_att, grad_router, grad_gain, grad_gain_moe, grad_bias = finish(
        experts, mixed, grad_tokens, grad_in, grad_out, grad_qkv, grad_att, grad_extra, grad_gain, grad_bias)
    return (
        mixed, grad_tokens, grad_gain.reshape(own), grad_qkv, grad_att, grad_bias.T, grad_gain_moe.reshape(own), grad_router.T,
        grad_in, grad_out,
    )


def solution(mesh):
    both = P(("dp", "expert"))
    return jax.shard_map(
        functools.partial(shards, mesh.shape["expert"]),
        mesh=mesh,
        in_specs=(both, both, both, P(), both, both, both, P(), both, both, P("expert"), P("expert")),
        out_specs=(both, both, both, both, both, P(), both, both, P("expert", None, "dp"), P("expert", None, "dp")),
        check_vma=False,
    )
```
